256 devices in a mesh: mode: 8 (over z_hi, x), grid: 32 (over y, z_lo, core).
Axes of the slice: x: 4, y: 4, z: 8 (z_hi: 2, z_lo: 4; z = z_hi * 4 + z_lo), core: 2. Of those that a mesh axis runs over, the one named last changes fastest.
Arguments:
- omega_re: float32 [56, 512, 1024], P('mode', 'grid'), may hold values from -6 to 6
- omega_im: float32 [56, 512, 1024], P('mode', 'grid'), may hold values from -6 to 6
- base_re: float32 [56, 512, 1024], P('mode', 'grid'), may hold values from -6 to 6
- base_im: float32 [56, 512, 1024], P('mode', 'grid'), may hold values from -6 to 6
- triple: bfloat16 [56, 56, 56], replicated, may hold values from -0.109375 to 0.109375
Outputs:
- new_re: float32 [56, 512, 1024], P('mode', 'grid')
- new_im: float32 [56, 512, 1024], P('mode', 'grid')
The draws below stay inside these ranges and needn't reach their ends.
All inputs are finite; a program needn't handle non-finite values.
Results may differ from the reference program's by a relative error of at most 0.005.
Values may be sent and summed in bfloat16 or wider, within the bound.
No kernel may reach another device: no remote copies, remote signals or barrier semaphores. Data moves between devices by JAX's collectives and lax.ppermute only.
A program may use at most 128 MiB of HBM per device.

```python
import math
import jax
import jax.numpy as jnp
from jax import lax

P_SIZE = 56
NG = 1024
K = 512


def block_levels(key, extent, shards, smallest, top_value):
    gain, own = 1.0, jax.random.fold_in(key, 6)
    for axis_at, parts in shards:
        heights = jnp.exp(jax.random.uniform(jax.random.fold_in(own, axis_at), (parts,), jnp.float32, smallest / len(shards), top_value / len(shards)))
        gain = gain * jnp.repeat(heights, extent[axis_at] // parts).reshape([-1 if axis == axis_at else 1 for axis in range(len(extent))])
    return gain


def noise(stream_key, dims, spread, limit, shards=(), kind=jnp.bfloat16):
    drawn = jax.random.normal(stream_key, dims, jnp.float32) * spread
    if len(shards) > 0:
        drawn = block_levels(stream_key, dims, shards, -0.22, 0.18) * drawn
    return jnp.clip(drawn, min=-limit, max=limit).astype(kind)


def setup_inputs(seed: int = 0) -> dict:
    streams_of = jax.random.split(jax.random.key(seed), 6)
    return {
        "omega_re": noise(streams_of[0], (P_SIZE, K, NG), 1.0, 6.0, ((0, 8), (1, 32)), jnp.float32),
        "omega_im": noise(streams_of[1], (P_SIZE, K, NG), 1.0, 6.0, ((0, 8), (1, 32)), jnp.float32),
        "base_re": noise(streams_of[2], (P_SIZE, K, NG), 1.0, 6.0, ((0, 8), (1, 32)), jnp.float32),
        "base_im": noise(streams_of[3], (P_SIZE, K, NG), 1.0, 6.0, ((0, 8), (1, 32)), jnp.float32),
        "triple": noise(streams_of[4], (P_SIZE, P_SIZE, P_SIZE), (P_SIZE * P_SIZE) ** -0.5, 0.109375),
    }


VISCOSITY = 4.0
STEP_WEIGHT = 0.5

def circle_tables(row_ids, col_ids, length):
    phases = row_ids[:, None] * col_ids[None, :] % length
    angles = phases.astype(jnp.float32) * (2.0 * math.pi / length)
    return (jnp.cos(angles), jnp.sin(angles))

def transform_tables(length, kept):
    points_ids = jnp.arange(length, dtype=jnp.int32)
    wave_ids = jnp.arange(kept, dtype=jnp.int32)
    cos_x, sin_x = circle_tables(points_ids, points_ids, length)
    table_x = jnp.concatenate([cos_x, sin_x], axis=1).astype(jnp.bfloat16)
    cos_y, sin_y = circle_tables(wave_ids, points_ids, length)
    weights = jnp.where(wave_ids == 0, 1.0, 2.0).astype(jnp.float32)[:, None]
    back_cos = (weights * cos_y).astype(jnp.bfloat16)
    back_sin = (weights * sin_y).astype(jnp.bfloat16)
    table_y = jnp.concatenate([cos_y.T, -sin_y.T], axis=1).astype(jnp.bfloat16)
    return (table_x, back_cos, back_sin, table_y)

def signed_waves(length):
    indices = jnp.arange(length, dtype=jnp.int32)
    return jnp.where(indices < length // 2, indices, indices - length).astype(jnp.float32)

def potential_fields(vort_re, vort_im, wave_y, wave_x):
    along_y = wave_y[:, None]
    along_x = wave_x[None, :]
    wave_sq = along_y * along_y + along_x * along_x
    inverse = jnp.where(wave_sq > 0.5, 1.0 / jnp.maximum(wave_sq, 1.0), 0.0)
    psi_re = vort_re * inverse
    psi_im = vort_im * inverse
    fields_re = jnp.stack([vort_re, -along_y * psi_im, along_x * psi_im])
    fields_im = jnp.stack([vort_im, along_y * psi_re, -along_x * psi_re])
    return (fields_re.astype(jnp.bfloat16), fields_im.astype(jnp.bfloat16))

def couple_block(flat_triple, modes):
    vort_part, u_part, v_part = modes
    number = u_part.shape[0]
    contracted = jnp.einsum('aj,jln->aln', flat_triple.astype(jnp.float32), vort_part.astype(jnp.float32))
    contracted = contracted.reshape((number, flat_triple.shape[0] // number) + vort_part.shape[1:])
    flux_x = lax.optimization_barrier(jnp.sum(contracted * u_part[:, None].astype(jnp.float32), axis=0))
    flux_y = lax.optimization_barrier(jnp.sum(contracted * v_part[:, None].astype(jnp.float32), axis=0))
    return (flux_x, flux_y)

def section_update(vort_re, vort_im, base_re, base_im, flux_re, flux_im, wave_y, wave_x, length):
    along_y = wave_y[:, None]
    along_x = wave_x[None, :]
    wave_sq = along_y * along_y + along_x * along_x
    dealias = jnp.where((jnp.abs(along_x) * 3.0 < length) & (along_y * 3.0 < length), 1.0, 0.0)
    adv_re = -(along_x * flux_im[0] + along_y * flux_im[1])
    adv_im = along_x * flux_re[0] + along_y * flux_re[1]
    damping = VISCOSITY / (length * length) * wave_sq
    rhs_re = -dealias * adv_re - damping * vort_re
    rhs_im = -dealias * adv_im - damping * vort_im
    return (base_re + STEP_WEIGHT * rhs_re, base_im + STEP_WEIGHT * rhs_im)

def reference(omega_re, omega_im, base_re, base_im, triple):
    factor = 1.0 / math.sqrt(NG)
    table_x, back_cos, back_sin, table_y = transform_tables(NG, K)
    wide_x = table_x.astype(jnp.float32)
    wide_y = table_y.astype(jnp.float32)
    wave_y = jnp.arange(K, dtype=jnp.int32).astype(jnp.float32)
    wave_x = signed_waves(NG)
    fields_re, fields_im = potential_fields(omega_re, omega_im, wave_y, wave_x)
    physical_list = []
    for member in range(3):
        part_re = jnp.einsum('pkn,nx->pkx', fields_re[member].astype(jnp.float32), wide_x)
        part_im = jnp.einsum('pkn,nx->pkx', fields_im[member].astype(jnp.float32), wide_x)
        cols_re = ((part_re[..., :NG] - part_im[..., NG:]) * factor).astype(jnp.bfloat16)
        cols_im = ((part_re[..., NG:] + part_im[..., :NG]) * factor).astype(jnp.bfloat16)
        values = jnp.einsum('pkx,ky->pxy', cols_re.astype(jnp.float32), back_cos.astype(jnp.float32))
        values = values - jnp.einsum('pkx,ky->pxy', cols_im.astype(jnp.float32), back_sin.astype(jnp.float32))
        physical_list.append((values * factor).astype(jnp.bfloat16))
    physical = jnp.stack(physical_list)
    flat_triple = triple.reshape(P_SIZE * P_SIZE, P_SIZE)

    def per_line(modes):
        flux_x, flux_y = couple_block(flat_triple, (modes[0][:, None], modes[1][:, None], modes[2][:, None]))
        return jnp.stack([flux_x[:, 0], flux_y[:, 0]]).astype(jnp.bfloat16)
    results = lax.map(per_line, (jnp.swapaxes(physical[0], 0, 1), jnp.swapaxes(physical[1], 0, 1), jnp.swapaxes(physical[2], 0, 1)))
    flux = jnp.transpose(results, (1, 2, 0, 3))
    spectra_re = []
    spectra_im = []
    for member in range(2):
        halves = jnp.einsum('pxy,yk->pxk', flux[member].astype(jnp.float32), wide_y) * factor
        half_re = halves[..., :K].astype(jnp.bfloat16)
        half_im = halves[..., K:].astype(jnp.bfloat16)
        part_re = jnp.einsum('pxk,xn->pkn', half_re.astype(jnp.float32), wide_x)
        part_im = jnp.einsum('pxk,xn->pkn', half_im.astype(jnp.float32), wide_x)
        spectra_re.append((part_re[..., :NG] + part_im[..., NG:]) * factor)
        spectra_im.append((part_im[..., :NG] - part_re[..., NG:]) * factor)
    return section_update(omega_re, omega_im, base_re, base_im, jnp.stack(spectra_re), jnp.stack(spectra_im), wave_y, wave_x, NG)
```

```python
import functools
import math

import jax
import jax.numpy as jnp
import ml_dtypes
import numpy as np
from jax import lax
from jax.experimental import pallas as pl
from jax.experimental.pallas import tpu as pltpu
from jax.sharding import PartitionSpec as P

VISCOSITY = 4.0
STEP_WEIGHT = 0.5
NG = 1024
KEPT = 512
MODES = 56
GROUPS = 8
SLABS = 32
DEVS = GROUPS * SLABS
OWN = MODES // GROUPS
ROWS = KEPT // SLABS
PARTS = NG // DEVS
QUART = NG // 4
FACTOR = 1.0 / math.sqrt(NG)
LIVE = 24
BF = jnp.bfloat16
F32 = jnp.float32
VMEM_LIMIT = 56 * 1024 * 1024


def circle(phases):
    angles = (phases % NG).astype(np.float32) * np.float32(2.0 * math.pi / NG)
    return np.cos(angles), np.sin(angles)


def x_tables():
    ahead, back = [], []
    short = np.arange(QUART)
    for part in range(PARTS):
        points = PARTS * short + part
        cos, sin = circle(short[:, None] * points[None, :])
        ahead.append(np.block([[cos, sin], [-sin, cos]]))
        cos, sin = circle(points[:, None] * short[None, :])
        back.append(np.block([[cos, -sin], [sin, cos]]))
    return (
        np.stack(ahead).astype(ml_dtypes.bfloat16),
        np.stack(back).astype(ml_dtypes.bfloat16),
    )


def y_tables():
    waves = np.arange(KEPT)
    points = np.arange(NG)
    cos, sin = circle(waves[:, None] * points[None, :])
    weights = np.where(waves == 0, 1.0, 2.0).astype(np.float32)[:, None]
    ahead = np.stack([(weights * cos).reshape(SLABS, ROWS, NG), (-weights * sin).reshape(SLABS, ROWS, NG)], axis=1)
    ahead = ahead.reshape(2 * KEPT, NG).astype(ml_dtypes.bfloat16)
    back = np.stack([cos.T.reshape(NG, SLABS, ROWS), -sin.T.reshape(NG, SLABS, ROWS)], axis=2)
    back = back[:, :LIVE].reshape(NG, LIVE * 2 * ROWS).astype(ml_dtypes.bfloat16)
    return ahead, back


def regroup(parts):
    lane = lax.broadcasted_iota(jnp.int32, parts[0].shape, parts[0].ndim - 1)
    axis = parts[0].ndim - 1
    low = (lane // 32) % 2 == 0
    high = lane < 64

    def swap(first, second, width, mask):
        return (
            jnp.where(mask, first, pltpu.roll(second, width, axis)),
            jnp.where(mask, pltpu.roll(first, 128 - width, axis), second),
        )

    p0, p1 = swap(parts[0], parts[1], 32, low)
    p2, p3 = swap(parts[2], parts[3], 32, low)
    p0, p2 = swap(p0, p2, 64, high)
    p1, p3 = swap(p1, p3, 64, high)
    return p0, p1, p2, p3


def turn(parts, sign):
    (r0, i0), (r1, i1), (r2, i2), (r3, i3) = parts
    er, ei, fr, fi = r0 + r2, i0 + i2, r0 - r2, i0 - i2
    gr, gi, hr, hi = r1 + r3, i1 + i3, r1 - r3, i1 - i3
    if sign < 0:
        hr, hi = -hr, -hi
    return (
        (er + gr, ei + gi),
        (fr - hi, fi + hr),
        (er - gr, ei - gi),
        (fr + hi, fi - hr),
    )


def waves_of(first_row):
    along_y = (first_row + lax.broadcasted_iota(jnp.int32, (ROWS, NG), 0)).astype(F32)
    index = lax.broadcasted_iota(jnp.int32, (ROWS, NG), 1)
    along_x = jnp.where(index < NG // 2, index, index - NG).astype(F32)
    return along_y, along_x


def columns_kernel(row_ref, re_ref, im_ref, table_ref, out_ref, left_ref, prod_ref, turn_ref):
    along_y, along_x = waves_of(row_ref[0])
    wave_sq = along_y * along_y + along_x * along_x
    inverse = jnp.where(wave_sq > 0.5, 1.0 / jnp.maximum(wave_sq, 1.0), 0.0)
    scale_y = along_y * inverse
    scale_x = along_x * inverse
    for mode in range(OWN):
        w_re, w_im = re_ref[mode], im_ref[mode]
        fields = (
            (w_re, w_im),
            (-scale_y * w_im, scale_y * w_re),
            (scale_x * w_im, -scale_x * w_re),
        )
        for member, (f_re, f_im) in enumerate(fields):
            pieces = [
                (f_re[:, QUART * p : QUART * (p + 1)], f_im[:, QUART * p : QUART * (p + 1)])
                for p in range(4)
            ]
            at = (member * OWN + mode) * ROWS
            for part, (b_re, b_im) in enumerate(turn(pieces, 1)):
                left_ref[part, at : at + ROWS, :QUART] = b_re.astype(BF)
                left_ref[part, at : at + ROWS, QUART:] = b_im.astype(BF)
    for part in range(PARTS):
        prod_ref[part] = (
            jnp.dot(left_ref[part], table_ref[part], preferred_element_type=F32) * FACTOR
        )
    count = 3 * OWN
    for at in range(count):
        rows = slice(at * ROWS, (at + 1) * ROWS)
        block = jnp.concatenate(
            [prod_ref[part, rows, c * QUART : (c + 1) * QUART] for part in range(PARTS) for c in range(2)],
            axis=0,
        )
        turn_ref[pl.ds(at, DEVS, stride=24), :] = block.T
    out_ref[...] = turn_ref[...].reshape(DEVS, 24, 128)[:, :count].astype(BF)


def points_kernel(in_ref, ahead_ref, triple_ref, back_ref, out_ref, left_ref, phys_ref, flux_ref, half_ref):
    count = 3 * OWN
    tall = 24 * GROUPS
    chunk = 256

    def gather(pair, carry):
        for quad in range(SLABS // 4):
            sides = []
            for side in range(2):
                group = pair * 2 + side
                parts = []
                for j in range(4):
                    block = in_ref[group, quad, j].astype(F32)
                    parts.append(jnp.concatenate([block, jnp.zeros((24 - count, 128), F32)], axis=0))
                sides.append(regroup(parts))
            for part in range(PARTS):
                both = jnp.concatenate([sides[0][part], sides[1][part]], axis=0)
                left_ref[part, pl.ds(pl.multiple_of(pair * 48, 48), 48), quad * 128 : (quad + 1) * 128] = both.astype(BF)
        return carry

    lax.fori_loop(0, GROUPS // 2, gather, 0)
    flux_ref[...] = jnp.zeros_like(flux_ref)

    def line(part, carry):
        phys_ref[...] = jnp.dot(left_ref[part], ahead_ref[...], preferred_element_type=F32) * FACTOR

        def points(step, inner):
            lanes = pl.ds(pl.multiple_of(step * chunk, chunk), chunk)
            right = phys_ref[:, lanes].astype(BF)
            sum_x = jnp.zeros((MODES, chunk), F32)
            sum_y = jnp.zeros((MODES, chunk), F32)
            for group in range(GROUPS):
                made = jnp.dot(
                    triple_ref[group * OWN * MODES : (group + 1) * OWN * MODES, :],
                    right,
                    preferred_element_type=F32,
                )
                vel = phys_ref[group * 24 : (group + 1) * 24, lanes]
                for mode in range(OWN):
                    block = made[mode * MODES : (mode + 1) * MODES]
                    sum_x = sum_x + block * vel[OWN + mode : OWN + mode + 1]
                    sum_y = sum_y + block * vel[2 * OWN + mode : 2 * OWN + mode + 1]
            for group in range(GROUPS):
                at = group * 16
                flux_ref[at : at + OWN, lanes] = sum_x[group * OWN : (group + 1) * OWN]
                flux_ref[at + OWN : at + 2 * OWN, lanes] = sum_y[group * OWN : (group + 1) * OWN]
            return inner

        lax.fori_loop(0, NG // chunk, points, 0)
        half_ref[part] = jnp.dot(flux_ref[...].astype(BF), back_ref[...], preferred_element_type=F32) * FACTOR
        return carry

    lax.fori_loop(0, PARTS, line, 0)
    for quad in range(LIVE // 4):
        parts = regroup([half_ref[part, :, quad * 128 : (quad + 1) * 128] for part in range(PARTS)])
        for j in range(4):
            block = parts[j].astype(BF)
            for group in range(GROUPS):
                out_ref[group, quad * 4 + j] = block[group * 16 : (group + 1) * 16]
    out_ref[:, LIVE:] = jnp.zeros((GROUPS, SLABS - LIVE, 16, 128), BF)


def update_kernel(
    row_ref, in_ref, table_ref, re_ref, im_ref, base_re_ref, base_im_ref, new_re_ref, new_im_ref, wide_ref, left_ref, prod_ref
):
    wide_ref[...] = in_ref[...].astype(F32).reshape(DEVS * 16, 128)
    for at in range(2 * OWN):
        block = wide_ref[pl.ds(at, DEVS, stride=16), :].T.astype(BF)
        for part in range(PARTS):
            for c in range(2):
                row = (part * 2 + c) * ROWS
                left_ref[part, at * ROWS : (at + 1) * ROWS, c * QUART : (c + 1) * QUART] = block[row : row + ROWS]
    for part in range(PARTS):
        prod_ref[part] = (
            jnp.dot(left_ref[part], table_ref[part], preferred_element_type=F32) * FACTOR
        )
    along_y, along_x = waves_of(row_ref[0])
    wave_sq = along_y * along_y + along_x * along_x
    keep = (jnp.abs(along_x) * 3.0 < NG) & (along_y * 3.0 < NG)
    damping = VISCOSITY / (NG * NG) * wave_sq
    for mode in range(OWN):
        spectra = []
        for member in range(2):
            rows = slice((member * OWN + mode) * ROWS, (member * OWN + mode + 1) * ROWS)
            spectra.append(
                turn([(prod_ref[part, rows, :QUART], prod_ref[part, rows, QUART:]) for part in range(PARTS)], -1)
            )
        for p in range(4):
            lanes = slice(p * QUART, (p + 1) * QUART)
            (x_re, x_im), (y_re, y_im) = spectra[0][p], spectra[1][p]
            wx, wy = along_x[:, lanes], along_y[:, lanes]
            adv_re = jnp.where(keep[:, lanes], -(wx * x_im + wy * y_im), 0.0)
            adv_im = jnp.where(keep[:, lanes], wx * x_re + wy * y_re, 0.0)
            damp = damping[:, lanes]
            new_re_ref[mode, :, lanes] = base_re_ref[mode, :, lanes] + STEP_WEIGHT * (
                -adv_re - damp * re_ref[mode, :, lanes]
            )
            new_im_ref[mode, :, lanes] = base_im_ref[mode, :, lanes] + STEP_WEIGHT * (
                -adv_im - damp * im_ref[mode, :, lanes]
            )


def call(kernel, outs, scratch, specs, flops):
    return pl.pallas_call(
        kernel,
        out_shape=outs,
        in_specs=specs,
        out_specs=jax.tree.map(lambda _: pl.BlockSpec(memory_space=pltpu.VMEM), outs),
        scratch_shapes=scratch,
        cost_estimate=pl.CostEstimate(flops=flops, bytes_accessed=4 * 1024 * 1024, transcendentals=0),
        compiler_params=pltpu.CompilerParams(vmem_limit_bytes=VMEM_LIMIT),
    )


def shards(omega_re, omega_im, base_re, base_im, triple):
    vmem = pl.BlockSpec(memory_space=pltpu.VMEM)
    smem = pl.BlockSpec(memory_space=pltpu.SMEM)
    count = 3 * OWN
    ahead_x, back_x = x_tables()
    ahead_y, back_y = y_tables()
    first_row = (lax.axis_index("grid") * ROWS).astype(jnp.int32)[None]
    spread = np.zeros((MODES, 24 * GROUPS), np.float32)
    for mode in range(MODES):
        spread[mode, (mode // OWN) * 24 + mode % OWN] = 1.0
    wide_triple = jnp.dot(
        triple.reshape(MODES * MODES, MODES), spread.astype(ml_dtypes.bfloat16), preferred_element_type=BF
    )
    columns = call(
        columns_kernel,
        jax.ShapeDtypeStruct((DEVS, count, 128), BF),
        [
            pltpu.VMEM((PARTS, count * ROWS, 2 * QUART), BF),
            pltpu.VMEM((PARTS, count * ROWS, 2 * QUART), F32),
            pltpu.VMEM((DEVS * 24, 128), F32),
        ],
        [smem, vmem, vmem, vmem],
        1_000_000_000,
    )(first_row, omega_re, omega_im, ahead_x)
    slab = lax.all_to_all(columns, ("mode", "grid"), split_axis=0, concat_axis=0, tiled=True)
    halves = call(
        points_kernel,
        jax.ShapeDtypeStruct((GROUPS, SLABS, 16, 128), BF),
        [
            pltpu.VMEM((PARTS, 24 * GROUPS, NG), BF),
            pltpu.VMEM((24 * GROUPS, NG), F32),
            pltpu.VMEM((16 * GROUPS, NG), F32),
            pltpu.VMEM((PARTS, 16 * GROUPS, LIVE * 32), F32),
        ],
        [vmem] * 4,
        10_000_000_000,
    )(slab.reshape(GROUPS, SLABS // 4, 4, count, 128), ahead_y, wide_triple, back_y)
    rows = lax.all_to_all(halves.reshape(DEVS, 16, 128), ("mode", "grid"), split_axis=0, concat_axis=0, tiled=True)
    new = jax.ShapeDtypeStruct(base_re.shape, F32)
    return call(
        update_kernel,
        (new, new),
        [
            pltpu.VMEM((DEVS * 16, 128), F32),
            pltpu.VMEM((PARTS, 2 * OWN * ROWS, 2 * QUART), BF),
            pltpu.VMEM((PARTS, 2 * OWN * ROWS, 2 * QUART), F32),
        ],
        [smem] + [vmem] * 6,
        1_000_000_000,
    )(first_row, rows, back_x, omega_re, omega_im, base_re, base_im)


def solution(mesh):
    spec = P("mode", "grid", None)
    return jax.shard_map(
        shards, mesh=mesh, in_specs=(spec, spec, spec, spec, P()), out_specs=(spec, spec), check_vma=False
    )
```

```python
import functools
import math

import jax
import jax.numpy as jnp
import ml_dtypes
import numpy as np
from jax import lax
from jax.experimental import pallas as pl
from jax.experimental.pallas import tpu as pltpu
from jax.sharding import PartitionSpec as P

VISCOSITY = 4.0
STEP_WEIGHT = 0.5
NG = 1024
KEPT = 512
MODES = 56
GROUPS = 8
SLABS = 32
DEVS = GROUPS * SLABS
OWN = MODES // GROUPS
ROWS = KEPT // SLABS
PARTS = NG // DEVS
QUART = NG // 4
FACTOR = 1.0 / math.sqrt(NG)
LIVE = 24
BF = jnp.bfloat16
F32 = jnp.float32
VMEM_LIMIT = 20 * 1024 * 1024


def circle(phases):
    angles = (phases % NG).astype(np.float32) * np.float32(2.0 * math.pi / NG)
    return np.cos(angles), np.sin(angles)


def x_tables():
    ahead, back = [], []
    short = np.arange(QUART)
    for part in range(PARTS):
        points = PARTS * short + part
        cos, sin = circle(short[:, None] * points[None, :])
        ahead.append(np.block([[cos, sin], [-sin, cos]]))
        cos, sin = circle(points[:, None] * short[None, :])
        back.append(np.block([[cos, -sin], [sin, cos]]))
    return (
        np.stack(ahead).astype(ml_dtypes.bfloat16),
        np.stack(back).astype(ml_dtypes.bfloat16),
    )


def y_tables():
    waves = np.arange(KEPT)
    points = np.arange(NG)
    cos, sin = circle(waves[:, None] * points[None, :])
    weights = np.where(waves == 0, 1.0, 2.0).astype(np.float32)[:, None]
    ahead = np.stack([(weights * cos).reshape(SLABS, ROWS, NG), (-weights * sin).reshape(SLABS, ROWS, NG)], axis=1)
    ahead = ahead.reshape(2 * KEPT, NG).astype(ml_dtypes.bfloat16)
    back = np.stack([cos.T.reshape(NG, SLABS, ROWS), -sin.T.reshape(NG, SLABS, ROWS)], axis=2)
    back = back[:, :LIVE].reshape(NG, LIVE * 2 * ROWS).astype(ml_dtypes.bfloat16)
    return ahead, back


def regroup(parts):
    lane = lax.broadcasted_iota(jnp.int32, parts[0].shape, parts[0].ndim - 1)
    axis = parts[0].ndim - 1
    low = (lane // 32) % 2 == 0
    high = lane < 64

    def swap(first, second, width, mask):
        return (
            jnp.where(mask, first, pltpu.roll(second, width, axis)),
            jnp.where(mask, pltpu.roll(first, 128 - width, axis), second),
        )

    p0, p1 = swap(parts[0], parts[1], 32, low)
    p2, p3 = swap(parts[2], parts[3], 32, low)
    p0, p2 = swap(p0, p2, 64, high)
    p1, p3 = swap(p1, p3, 64, high)
    return p0, p1, p2, p3


def turn(parts, sign):
    (r0, i0), (r1, i1), (r2, i2), (r3, i3) = parts
    er, ei, fr, fi = r0 + r2, i0 + i2, r0 - r2, i0 - i2
    gr, gi, hr, hi = r1 + r3, i1 + i3, r1 - r3, i1 - i3
    if sign < 0:
        hr, hi = -hr, -hi
    return (
        (er + gr, ei + gi),
        (fr - hi, fi + hr),
        (er - gr, ei - gi),
        (fr + hi, fi - hr),
    )


def waves_of(first_row):
    along_y = (first_row + lax.broadcasted_iota(jnp.int32, (ROWS, NG), 0)).astype(F32)
    index = lax.broadcasted_iota(jnp.int32, (ROWS, NG), 1)
    along_x = jnp.where(index < NG // 2, index, index - NG).astype(F32)
    return along_y, along_x


def columns_kernel(row_ref, re_ref, im_ref, table_ref, out_ref, left_ref, prod_ref, turn_ref):
    along_y, along_x = waves_of(row_ref[0])
    wave_sq = along_y * along_y + along_x * along_x
    inverse = jnp.where(wave_sq > 0.5, 1.0 / jnp.maximum(wave_sq, 1.0), 0.0)
    scale_y = along_y * inverse
    scale_x = along_x * inverse
    for mode in range(OWN):
        w_re, w_im = re_ref[mode], im_ref[mode]
        fields = (
            (w_re, w_im),
            (-scale_y * w_im, scale_y * w_re),
            (scale_x * w_im, -scale_x * w_re),
        )
        for member, (f_re, f_im) in enumerate(fields):
            pieces = [
                (f_re[:, QUART * p : QUART * (p + 1)], f_im[:, QUART * p : QUART * (p + 1)])
                for p in range(4)
            ]
            at = (member * OWN + mode) * ROWS
            for part, (b_re, b_im) in enumerate(turn(pieces, 1)):
                left_ref[part, at : at + ROWS, :QUART] = b_re.astype(BF)
                left_ref[part, at : at + ROWS, QUART:] = b_im.astype(BF)
    for part in range(PARTS):
        prod_ref[part] = (
            jnp.dot(left_ref[part], table_ref[part], preferred_element_type=F32) * FACTOR
        )
    count = 3 * OWN
    for at in range(count):
        rows = slice(at * ROWS, (at + 1) * ROWS)
        block = jnp.concatenate(
            [prod_ref[part, rows, c * QUART : (c + 1) * QUART] for part in range(PARTS) for c in range(2)],
            axis=0,
        )
        turn_ref[pl.ds(at, DEVS, stride=24), :] = block.T
    out_ref[...] = turn_ref[...].reshape(DEVS, 24, 128)[:, :count].astype(BF)


def points_kernel(in_ref, ahead_ref, triple_ref, back_ref, out_ref, left_ref, phys_ref, flux_ref, half_ref):
    count = 3 * OWN
    tall = 24 * GROUPS
    chunk = 512

    def gather(pair, carry):
        for quad in range(SLABS // 4):
            sides = []
            for side in range(2):
                group = pair * 2 + side
                parts = []
                for j in range(4):
                    block = in_ref[group, quad, j].astype(F32)
                    parts.append(jnp.concatenate([block, jnp.zeros((24 - count, 128), F32)], axis=0))
                sides.append(regroup(parts))
            for part in range(PARTS):
                both = jnp.concatenate([sides[0][part], sides[1][part]], axis=0)
                left_ref[part, pl.ds(pl.multiple_of(pair * 48, 48), 48), quad * 128 : (quad + 1) * 128] = both.astype(BF)
        return carry

    lax.fori_loop(0, GROUPS // 2, gather, 0)
    flux_ref[...] = jnp.zeros_like(flux_ref)

    def line(part, carry):
        phys_ref[...] = jnp.dot(left_ref[part], ahead_ref[...], preferred_element_type=F32) * FACTOR

        def points(step, inner):
            lanes = pl.ds(pl.multiple_of(step * chunk, chunk), chunk)
            right = phys_ref[:, lanes].astype(BF)
            sum_x = jnp.zeros((MODES, chunk), F32)
            sum_y = jnp.zeros((MODES, chunk), F32)
            for group in range(GROUPS):
                made = jnp.dot(
                    triple_ref[group * OWN * MODES : (group + 1) * OWN * MODES, :],
                    right,
                    preferred_element_type=F32,
                )
                vel = phys_ref[group * 24 : (group + 1) * 24, lanes]
                for mode in range(OWN):
                    block = made[mode * MODES : (mode + 1) * MODES]
                    sum_x = sum_x + block * vel[OWN + mode : OWN + mode + 1]
                    sum_y = sum_y + block * vel[2 * OWN + mode : 2 * OWN + mode + 1]
            for group in range(GROUPS):
                at = group * 16
                flux_ref[at : at + OWN, lanes] = sum_x[group * OWN : (group + 1) * OWN]
                flux_ref[at + OWN : at + 2 * OWN, lanes] = sum_y[group * OWN : (group + 1) * OWN]
            return inner

        lax.fori_loop(0, NG // chunk, points, 0)
        half_ref[part] = jnp.dot(flux_ref[...].astype(BF), back_ref[...], preferred_element_type=F32) * FACTOR
        return carry

    lax.fori_loop(0, PARTS, line, 0)
    for quad in range(LIVE // 4):
        parts = regroup([half_ref[part, :, quad * 128 : (quad + 1) * 128] for part in range(PARTS)])
        for j in range(4):
            block = parts[j].astype(BF)
            for group in range(GROUPS):
                out_ref[group, quad * 4 + j] = block[group * 16 : (group + 1) * 16]
    out_ref[:, LIVE:] = jnp.zeros((GROUPS, SLABS - LIVE, 16, 128), BF)


def update_kernel(
    row_ref, in_ref, table_ref, re_ref, im_ref, base_re_ref, base_im_ref, new_re_ref, new_im_ref, wide_ref, left_ref, prod_ref
):
    wide_ref[...] = in_ref[...].astype(F32).reshape(DEVS * 16, 128)
    for at in range(2 * OWN):
        block = wide_ref[pl.ds(at, DEVS, stride=16), :].T.astype(BF)
        for part in range(PARTS):
            for c in range(2):
                row = (part * 2 + c) * ROWS
                left_ref[part, at * ROWS : (at + 1) * ROWS, c * QUART : (c + 1) * QUART] = block[row : row + ROWS]
    for part in range(PARTS):
        prod_ref[part] = (
            jnp.dot(left_ref[part], table_ref[part], preferred_element_type=F32) * FACTOR
        )
    along_y, along_x = waves_of(row_ref[0])
    wave_sq = along_y * along_y + along_x * along_x
    keep = (jnp.abs(along_x) * 3.0 < NG) & (along_y * 3.0 < NG)
    damping = VISCOSITY / (NG * NG) * wave_sq
    for mode in range(OWN):
        spectra = []
        for member in range(2):
            rows = slice((member * OWN + mode) * ROWS, (member * OWN + mode + 1) * ROWS)
            spectra.append(
                turn([(prod_ref[part, rows, :QUART], prod_ref[part, rows, QUART:]) for part in range(PARTS)], -1)
            )
        for p in range(4):
            lanes = slice(p * QUART, (p + 1) * QUART)
            (x_re, x_im), (y_re, y_im) = spectra[0][p], spectra[1][p]
            wx, wy = along_x[:, lanes], along_y[:, lanes]
            adv_re = jnp.where(keep[:, lanes], -(wx * x_im + wy * y_im), 0.0)
            adv_im = jnp.where(keep[:, lanes], wx * x_re + wy * y_re, 0.0)
            damp = damping[:, lanes]
            new_re_ref[mode, :, lanes] = base_re_ref[mode, :, lanes] + STEP_WEIGHT * (
                -adv_re - damp * re_ref[mode, :, lanes]
            )
            new_im_ref[mode, :, lanes] = base_im_ref[mode, :, lanes] + STEP_WEIGHT * (
                -adv_im - damp * im_ref[mode, :, lanes]
            )


def call(kernel, outs, scratch, specs, flops):
    return pl.pallas_call(
        kernel,
        out_shape=outs,
        in_specs=specs,
        out_specs=jax.tree.map(lambda _: pl.BlockSpec(memory_space=pltpu.VMEM), outs),
        scratch_shapes=scratch,
        cost_estimate=pl.CostEstimate(flops=flops, bytes_accessed=4 * 1024 * 1024, transcendentals=0),
        compiler_params=pltpu.CompilerParams(vmem_limit_bytes=VMEM_LIMIT),
    )


def shards(omega_re, omega_im, base_re, base_im, triple):
    vmem = pl.BlockSpec(memory_space=pltpu.VMEM)
    smem = pl.BlockSpec(memory_space=pltpu.SMEM)
    count = 3 * OWN
    ahead_x, back_x = x_tables()
    ahead_y, back_y = y_tables()
    first_row = (lax.axis_index("grid") * ROWS).astype(jnp.int32)[None]
    spread = np.zeros((MODES, 24 * GROUPS), np.float32)
    for mode in range(MODES):
        spread[mode, (mode // OWN) * 24 + mode % OWN] = 1.0
    wide_triple = jnp.dot(
        triple.reshape(MODES * MODES, MODES), spread.astype(ml_dtypes.bfloat16), preferred_element_type=BF
    )
    columns = call(
        columns_kernel,
        jax.ShapeDtypeStruct((DEVS, count, 128), BF),
        [
            pltpu.VMEM((PARTS, count * ROWS, 2 * QUART), BF),
            pltpu.VMEM((PARTS, count * ROWS, 2 * QUART), F32),
            pltpu.VMEM((DEVS * 24, 128), F32),
        ],
        [smem, vmem, vmem, vmem],
        1_000_000_000,
    )(first_row, omega_re, omega_im, ahead_x)
    slab = lax.all_to_all(columns, ("mode", "grid"), split_axis=0, concat_axis=0, tiled=True)
    halves = call(
        points_kernel,
        jax.ShapeDtypeStruct((GROUPS, SLABS, 16, 128), BF),
        [
            pltpu.VMEM((PARTS, 24 * GROUPS, NG), BF),
            pltpu.VMEM((24 * GROUPS, NG), F32),
            pltpu.VMEM((16 * GROUPS, NG), F32),
            pltpu.VMEM((PARTS, 16 * GROUPS, LIVE * 32), F32),
        ],
        [vmem] * 4,
        10_000_000_000,
    )(slab.reshape(GROUPS, SLABS // 4, 4, count, 128), ahead_y, wide_triple, back_y)
    rows = lax.all_to_all(halves.reshape(DEVS, 16, 128), ("mode", "grid"), split_axis=0, concat_axis=0, tiled=True)
    new = jax.ShapeDtypeStruct(base_re.shape, F32)
    return call(
        update_kernel,
        (new, new),
        [
            pltpu.VMEM((DEVS * 16, 128), F32),
            pltpu.VMEM((PARTS, 2 * OWN * ROWS, 2 * QUART), BF),
            pltpu.VMEM((PARTS, 2 * OWN * ROWS, 2 * QUART), F32),
        ],
        [smem] + [vmem] * 6,
        1_000_000_000,
    )(first_row, rows, back_x, omega_re, omega_im, base_re, base_im)


def solution(mesh):
    spec = P("mode", "grid", None)
    return jax.shard_map(
        shards, mesh=mesh, in_specs=(spec, spec, spec, spec, P()), out_specs=(spec, spec), check_vma=False
    )
```

```python
import functools
import math

import jax
import jax.numpy as jnp
import ml_dtypes
import numpy as np
from jax import lax
from jax.experimental import pallas as pl
from jax.experimental.pallas import tpu as pltpu
from jax.sharding import PartitionSpec as P

VISCOSITY = 4.0
STEP_WEIGHT = 0.5
NG = 1024
KEPT = 512
MODES = 56
GROUPS = 8
SLABS = 32
DEVS = GROUPS * SLABS
OWN = MODES // GROUPS
ROWS = KEPT // SLABS
PARTS = NG // DEVS
QUART = NG // 4
FACTOR = 1.0 / math.sqrt(NG)
LIVE = 24
BF = jnp.bfloat16
F32 = jnp.float32
SMALL = 20 * 1024 * 1024
LARGE = 56 * 1024 * 1024


def circle(phases):
    angles = (phases % NG).astype(np.float32) * np.float32(2.0 * math.pi / NG)
    return np.cos(angles), np.sin(angles)


def x_tables():
    ahead, back = [], []
    short = np.arange(QUART)
    for part in range(PARTS):
        points = PARTS * short + part
        cos, sin = circle(short[:, None] * points[None, :])
        ahead.append(np.block([[cos, sin], [-sin, cos]]))
        cos, sin = circle(points[:, None] * short[None, :])
        back.append(np.block([[cos, -sin], [sin, cos]]))
    return (
        np.stack(ahead).astype(ml_dtypes.bfloat16),
        np.stack(back).astype(ml_dtypes.bfloat16),
    )


def y_tables():
    waves = np.arange(KEPT)
    points = np.arange(NG)
    cos, sin = circle(waves[:, None] * points[None, :])
    weights = np.where(waves == 0, 1.0, 2.0).astype(np.float32)[:, None]
    ahead = np.stack([(weights * cos).reshape(SLABS, ROWS, NG), (-weights * sin).reshape(SLABS, ROWS, NG)], axis=1)
    ahead = ahead.reshape(2 * KEPT, NG).astype(ml_dtypes.bfloat16)
    back = np.stack([cos.T.reshape(NG, SLABS, ROWS), -sin.T.reshape(NG, SLABS, ROWS)], axis=2)
    back = back[:, :LIVE].reshape(NG, LIVE * 2 * ROWS).astype(ml_dtypes.bfloat16)
    return ahead, back


def lane_masks():
    group = lax.broadcasted_iota(jnp.int32, (1, 128), 1) // 32
    return [group == 0, group == 1, group == 2]


def pick(masks, sources):
    return jnp.where(
        masks[0], sources[0], jnp.where(masks[1], sources[1], jnp.where(masks[2], sources[2], sources[3]))
    )


def turn(parts, sign):
    (r0, i0), (r1, i1), (r2, i2), (r3, i3) = parts
    er, ei, fr, fi = r0 + r2, i0 + i2, r0 - r2, i0 - i2
    gr, gi, hr, hi = r1 + r3, i1 + i3, r1 - r3, i1 - i3
    if sign < 0:
        hr, hi = -hr, -hi
    return (
        (er + gr, ei + gi),
        (fr - hi, fi + hr),
        (er - gr, ei - gi),
        (fr + hi, fi - hr),
    )


def waves_of(first_row):
    along_y = (first_row + lax.broadcasted_iota(jnp.int32, (ROWS, NG), 0)).astype(F32)
    index = lax.broadcasted_iota(jnp.int32, (ROWS, NG), 1)
    along_x = jnp.where(index < NG // 2, index, index - NG).astype(F32)
    return along_y, along_x


def columns_kernel(
    row_ref, re_hbm, im_hbm, table_hbm, out_ref, re_ref, im_ref, table_ref, left_ref, prod_ref, turn_ref, sems
):
    loads = []
    for mode in range(OWN):
        loads.append(
            (
                pltpu.make_async_copy(re_hbm.at[mode], re_ref.at[mode], sems.at[2 * mode]),
                pltpu.make_async_copy(im_hbm.at[mode], im_ref.at[mode], sems.at[2 * mode + 1]),
            )
        )
    tables = [
        pltpu.make_async_copy(table_hbm.at[part], table_ref.at[part], sems.at[2 * OWN + part]) for part in range(PARTS)
    ]
    for pair in loads:
        pair[0].start()
        pair[1].start()
    for copy in tables:
        copy.start()
    count = 3 * OWN
    for at in range(count, 24):
        turn_ref[pl.ds(at, DEVS, stride=24), :] = jnp.zeros((DEVS, 128), F32)
    along_y, along_x = waves_of(row_ref[0])
    wave_sq = along_y * along_y + along_x * along_x
    inverse = jnp.where(wave_sq > 0.5, 1.0 / jnp.maximum(wave_sq, 1.0), 0.0)
    scale_y = along_y * inverse
    scale_x = along_x * inverse
    for mode in range(OWN):
        loads[mode][0].wait()
        loads[mode][1].wait()
        w_re, w_im = re_ref[mode], im_ref[mode]
        fields = (
            (w_re, w_im),
            (-scale_y * w_im, scale_y * w_re),
            (scale_x * w_im, -scale_x * w_re),
        )
        for member, (f_re, f_im) in enumerate(fields):
            pieces = [
                (f_re[:, QUART * p : QUART * (p + 1)], f_im[:, QUART * p : QUART * (p + 1)])
                for p in range(4)
            ]
            at = (member * OWN + mode) * ROWS
            for part, (b_re, b_im) in enumerate(turn(pieces, 1)):
                left_ref[part, at : at + ROWS, :QUART] = b_re.astype(BF)
                left_ref[part, at : at + ROWS, QUART:] = b_im.astype(BF)
    for part in range(PARTS):
        tables[part].wait()
        prod_ref[part] = (
            jnp.dot(left_ref[part], table_ref[part], preferred_element_type=F32) * FACTOR
        )
    shift = row_ref[1]
    slots = [lax.rem(slot + PARTS - shift, PARTS) for slot in range(PARTS)]
    for at in range(count):
        rows = slice(at * ROWS, (at + 1) * ROWS)
        block = jnp.concatenate(
            [prod_ref[slots[slot], rows, c * QUART : (c + 1) * QUART] for slot in range(PARTS) for c in range(2)],
            axis=0,
        )
        turn_ref[pl.ds(at, DEVS, stride=24), :] = block.T
    out_ref[...] = turn_ref[...].reshape(DEVS, 24, 128).astype(BF)


def points_kernel(
    in_ref, ahead_hbm, triple_hbm, back_hbm, out_ref, ahead_ref, triple_ref, back_ref, left_ref, phys_ref, flux_ref, half_ref, sems
):
    chunk = 512
    ahead = pltpu.make_async_copy(ahead_hbm, ahead_ref, sems.at[0])
    couple = pltpu.make_async_copy(triple_hbm, triple_ref, sems.at[1])
    back = pltpu.make_async_copy(back_hbm, back_ref, sems.at[2])
    ahead.start()
    couple.start()
    back.start()
    masks = lane_masks()

    def gather(pair, carry):
        for quad in range(SLABS // 4):
            sides = []
            for side in range(2):
                blocks = [in_ref[pair * 2 + side, quad, j].astype(F32) for j in range(4)]
                parts = []
                for part in range(PARTS):
                    mixed = pick(masks, [blocks[(slot - part) % 4] for slot in range(4)])
                    parts.append(pltpu.roll(mixed, 128 - 32 * part, 1) if part else mixed)
                sides.append(parts)
            for part in range(PARTS):
                both = jnp.concatenate([sides[0][part], sides[1][part]], axis=0)
                left_ref[part, pl.ds(pl.multiple_of(pair * 48, 48), 48), quad * 128 : (quad + 1) * 128] = both.astype(BF)
        return carry

    lax.fori_loop(0, GROUPS // 2, gather, 0)
    flux_ref[...] = jnp.zeros_like(flux_ref)
    ahead.wait()
    couple.wait()
    back.wait()

    def line(part, carry):
        phys_ref[...] = jnp.dot(left_ref[part], ahead_ref[...], preferred_element_type=F32) * FACTOR
        for step in range(NG // chunk):
            lanes = slice(step * chunk, (step + 1) * chunk)
            right = jnp.concatenate(
                [phys_ref[group * 24 : group * 24 + OWN, lanes] for group in range(GROUPS)], axis=0
            ).astype(BF)
            sum_x = jnp.zeros((MODES, chunk), F32)
            sum_y = jnp.zeros((MODES, chunk), F32)
            for group in range(GROUPS):
                made = jnp.dot(
                    triple_ref[group * OWN * MODES : (group + 1) * OWN * MODES, :],
                    right,
                    preferred_element_type=F32,
                )
                vel = phys_ref[group * 24 : (group + 1) * 24, lanes]
                for mode in range(OWN):
                    block = made[mode * MODES : (mode + 1) * MODES]
                    sum_x = sum_x + block * vel[OWN + mode : OWN + mode + 1]
                    sum_y = sum_y + block * vel[2 * OWN + mode : 2 * OWN + mode + 1]
            for group in range(GROUPS):
                at = group * 16
                flux_ref[at : at + OWN, lanes] = sum_x[group * OWN : (group + 1) * OWN]
                flux_ref[at + OWN : at + 2 * OWN, lanes] = sum_y[group * OWN : (group + 1) * OWN]
        half_ref[part] = jnp.dot(flux_ref[...].astype(BF), back_ref[...], preferred_element_type=F32) * FACTOR
        return carry

    lax.fori_loop(0, PARTS, line, 0)
    for quad in range(LIVE // 4):
        rolled = []
        for part in range(PARTS):
            block = half_ref[part, :, quad * 128 : (quad + 1) * 128]
            rolled.append(pltpu.roll(block, 32 * part, 1) if part else block)
        for j in range(4):
            block = pick(masks, [rolled[(slot - j) % 4] for slot in range(4)]).astype(BF)
            for group in range(GROUPS):
                out_ref[group, quad * 4 + j] = block[group * 16 : (group + 1) * 16]
    out_ref[:, LIVE:] = jnp.zeros((GROUPS, SLABS - LIVE, 16, 128), BF)


def update_kernel(
    row_ref, in_ref, table_ref, re_ref, im_ref, base_re_ref, base_im_ref, new_re_ref, new_im_ref, wide_ref, left_ref, prod_ref
):
    wide_ref[...] = in_ref[...].astype(F32).reshape(DEVS * 16, 128)
    shift = row_ref[1]
    slots = [lax.rem(slot + PARTS - shift, PARTS) for slot in range(PARTS)]
    for at in range(2 * OWN):
        block = wide_ref[pl.ds(at, DEVS, stride=16), :].T.astype(BF)
        for slot in range(PARTS):
            for c in range(2):
                row = (slot * 2 + c) * ROWS
                left_ref[slots[slot], at * ROWS : (at + 1) * ROWS, c * QUART : (c + 1) * QUART] = block[row : row + ROWS]
    for part in range(PARTS):
        prod_ref[part] = (
            jnp.dot(left_ref[part], table_ref[part], preferred_element_type=F32) * FACTOR
        )
    along_y, along_x = waves_of(row_ref[0])
    wave_sq = along_y * along_y + along_x * along_x
    keep = (jnp.abs(along_x) * 3.0 < NG) & (along_y * 3.0 < NG)
    damping = VISCOSITY / (NG * NG) * wave_sq
    for mode in range(OWN):
        spectra = []
        for member in range(2):
            rows = slice((member * OWN + mode) * ROWS, (member * OWN + mode + 1) * ROWS)
            spectra.append(
                turn([(prod_ref[part, rows, :QUART], prod_ref[part, rows, QUART:]) for part in range(PARTS)], -1)
            )
        for p in range(4):
            lanes = slice(p * QUART, (p + 1) * QUART)
            (x_re, x_im), (y_re, y_im) = spectra[0][p], spectra[1][p]
            wx, wy = along_x[:, lanes], along_y[:, lanes]
            adv_re = jnp.where(keep[:, lanes], -(wx * x_im + wy * y_im), 0.0)
            adv_im = jnp.where(keep[:, lanes], wx * x_re + wy * y_re, 0.0)
            damp = damping[:, lanes]
            new_re_ref[mode, :, lanes] = base_re_ref[mode, :, lanes] + STEP_WEIGHT * (
                -adv_re - damp * re_ref[mode, :, lanes]
            )
            new_im_ref[mode, :, lanes] = base_im_ref[mode, :, lanes] + STEP_WEIGHT * (
                -adv_im - damp * im_ref[mode, :, lanes]
            )


def call(kernel, outs, scratch, specs, flops, limit=SMALL):
    return pl.pallas_call(
        kernel,
        out_shape=outs,
        in_specs=specs,
        out_specs=jax.tree.map(lambda _: pl.BlockSpec(memory_space=pltpu.VMEM), outs),
        scratch_shapes=scratch,
        cost_estimate=pl.CostEstimate(flops=flops, bytes_accessed=4 * 1024 * 1024, transcendentals=0),
        compiler_params=pltpu.CompilerParams(vmem_limit_bytes=limit),
    )


def shards(omega_re, omega_im, base_re, base_im, triple):
    vmem = pl.BlockSpec(memory_space=pltpu.VMEM)
    smem = pl.BlockSpec(memory_space=pltpu.SMEM)
    hbm = pl.BlockSpec(memory_space=pltpu.HBM)
    count = 3 * OWN
    ahead_x, back_x = x_tables()
    ahead_y, back_y = y_tables()
    slab_at = lax.axis_index("grid").astype(jnp.int32)
    place = jnp.stack([slab_at * ROWS, slab_at % PARTS])
    columns = call(
        columns_kernel,
        jax.ShapeDtypeStruct((DEVS, 24, 128), BF),
        [
            pltpu.VMEM((OWN, ROWS, NG), F32),
            pltpu.VMEM((OWN, ROWS, NG), F32),
            pltpu.VMEM((PARTS, 2 * QUART, 2 * QUART), BF),
            pltpu.VMEM((PARTS, count * ROWS, 2 * QUART), BF),
            pltpu.VMEM((PARTS, count * ROWS, 2 * QUART), F32),
            pltpu.VMEM((DEVS * 24, 128), F32),
            pltpu.SemaphoreType.DMA((2 * OWN + PARTS,)),
        ],
        [smem, hbm, hbm, hbm],
        1_000_000_000,
        LARGE,
    )(place, omega_re, omega_im, ahead_x)
    slab = lax.all_to_all(columns, ("mode", "grid"), split_axis=0, concat_axis=0, tiled=True)
    halves = call(
        points_kernel,
        jax.ShapeDtypeStruct((GROUPS, SLABS, 16, 128), BF),
        [
            pltpu.VMEM(ahead_y.shape, BF),
            pltpu.VMEM((MODES * MODES, MODES), BF),
            pltpu.VMEM(back_y.shape, BF),
            pltpu.VMEM((PARTS, 24 * GROUPS, NG), BF),
            pltpu.VMEM((24 * GROUPS, NG), F32),
            pltpu.VMEM((16 * GROUPS, NG), F32),
            pltpu.VMEM((PARTS, 16 * GROUPS, LIVE * 32), F32),
            pltpu.SemaphoreType.DMA((3,)),
        ],
        [vmem, hbm, hbm, hbm],
        10_000_000_000,
    )(slab.reshape(GROUPS, SLABS // 4, 4, 24, 128), ahead_y, triple.reshape(MODES * MODES, MODES), back_y)
    rows = lax.all_to_all(halves.reshape(DEVS, 16, 128), ("mode", "grid"), split_axis=0, concat_axis=0, tiled=True)
    new = jax.ShapeDtypeStruct(base_re.shape, F32)
    return call(
        update_kernel,
        (new, new),
        [
            pltpu.VMEM((DEVS * 16, 128), F32),
            pltpu.VMEM((PARTS, 2 * OWN * ROWS, 2 * QUART), BF),
            pltpu.VMEM((PARTS, 2 * OWN * ROWS, 2 * QUART), F32),
        ],
        [smem] + [vmem] * 6,
        1_000_000_000,
    )(place, rows, back_x, omega_re, omega_im, base_re, base_im)


def solution(mesh):
    spec = P("mode", "grid", None)
    return jax.shard_map(
        shards, mesh=mesh, in_specs=(spec, spec, spec, spec, P()), out_specs=(spec, spec), check_vma=False
    )
```

```python
import functools
import math

import jax
import jax.numpy as jnp
import ml_dtypes
import numpy as np
from jax import lax
from jax.experimental import pallas as pl
from jax.experimental.pallas import tpu as pltpu
from jax.sharding import PartitionSpec as P

VISCOSITY = 4.0
STEP_WEIGHT = 0.5
NG = 1024
KEPT = 512
MODES = 56
GROUPS = 8
SLABS = 32
DEVS = GROUPS * SLABS
OWN = MODES // GROUPS
ROWS = KEPT // SLABS
PARTS = NG // DEVS
QUART = NG // 4
FACTOR = 1.0 / math.sqrt(NG)
LIVE = 24
BF = jnp.bfloat16
F32 = jnp.float32
SMALL = 20 * 1024 * 1024
LARGE = 56 * 1024 * 1024


def circle(phases):
    angles = (phases % NG).astype(np.float32) * np.float32(2.0 * math.pi / NG)
    return np.cos(angles), np.sin(angles)


def x_tables():
    ahead, back = [], []
    short = np.arange(QUART)
    for part in range(PARTS):
        points = PARTS * short + part
        cos, sin = circle(short[:, None] * points[None, :])
        ahead.append(np.block([[cos, sin]]))
        cos, sin = circle(points[:, None] * short[None, :])
        back.append(np.block([[cos, -sin], [sin, cos]]))
    return (
        np.stack(ahead).astype(ml_dtypes.bfloat16),
        np.stack(back).astype(ml_dtypes.bfloat16),
    )


def y_tables():
    waves = np.arange(KEPT)
    points = np.arange(NG)
    cos, sin = circle(waves[:, None] * points[None, :])
    weights = np.where(waves == 0, 1.0, 2.0).astype(np.float32)[:, None]
    ahead = np.stack([(weights * cos).reshape(SLABS, ROWS, NG), (-weights * sin).reshape(SLABS, ROWS, NG)], axis=1)
    ahead = ahead.reshape(2 * KEPT, NG).astype(ml_dtypes.bfloat16)
    back = np.stack([cos.T.reshape(NG, SLABS, ROWS), -sin.T.reshape(NG, SLABS, ROWS)], axis=2)
    back = back[:, :LIVE].reshape(NG, LIVE * 2 * ROWS).astype(ml_dtypes.bfloat16)
    return ahead, back


def lane_masks():
    group = lax.broadcasted_iota(jnp.int32, (1, 128), 1) // 32
    return [group == 0, group == 1, group == 2]


def pick(masks, sources):
    return jnp.where(
        masks[0], sources[0], jnp.where(masks[1], sources[1], jnp.where(masks[2], sources[2], sources[3]))
    )


def turn(parts, sign):
    (r0, i0), (r1, i1), (r2, i2), (r3, i3) = parts
    er, ei, fr, fi = r0 + r2, i0 + i2, r0 - r2, i0 - i2
    gr, gi, hr, hi = r1 + r3, i1 + i3, r1 - r3, i1 - i3
    if sign < 0:
        hr, hi = -hr, -hi
    return (
        (er + gr, ei + gi),
        (fr - hi, fi + hr),
        (er - gr, ei - gi),
        (fr + hi, fi - hr),
    )


def waves_of(first_row):
    along_y = (first_row + lax.broadcasted_iota(jnp.int32, (ROWS, NG), 0)).astype(F32)
    index = lax.broadcasted_iota(jnp.int32, (ROWS, NG), 1)
    along_x = jnp.where(index < NG // 2, index, index - NG).astype(F32)
    return along_y, along_x


def slots_of(shift):
    return [lax.rem(slot + PARTS - lax.rem(shift, PARTS), PARTS) for slot in range(PARTS)]


def columns_kernel(
    re_hbm, im_hbm, table_hbm, out_hbm, re_ref, im_ref, table_ref, left_ref, prod_ref, turn_ref, send_ref, sems
):
    loads = []
    for mode in range(OWN):
        loads.append(
            (
                pltpu.make_async_copy(re_hbm.at[mode], re_ref.at[mode], sems.at[2 * mode]),
                pltpu.make_async_copy(im_hbm.at[mode], im_ref.at[mode], sems.at[2 * mode + 1]),
            )
        )
    tables = [
        pltpu.make_async_copy(table_hbm.at[part], table_ref.at[part, pl.ds(0, QUART)], sems.at[2 * OWN + part])
        for part in range(PARTS)
    ]
    for pair in loads:
        pair[0].start()
        pair[1].start()
    for copy in tables:
        copy.start()
    count = 3 * OWN
    half = DEVS // 2
    for at in range(count, 24):
        turn_ref[pl.ds(at, half, stride=24), :] = jnp.zeros((half, 128), F32)
    slab = lax.axis_index("grid")
    along_y, along_x = waves_of(slab * ROWS)
    wave_sq = along_y * along_y + along_x * along_x
    inverse = jnp.where(wave_sq > 0.5, 1.0 / jnp.maximum(wave_sq, 1.0), 0.0)
    scale_y = along_y * inverse
    scale_x = along_x * inverse
    for mode in range(OWN):
        loads[mode][0].wait()
        loads[mode][1].wait()
        w_re, w_im = re_ref[mode], im_ref[mode]
        fields = (
            (w_re, w_im),
            (-scale_y * w_im, scale_y * w_re),
            (scale_x * w_im, -scale_x * w_re),
        )
        for member, (f_re, f_im) in enumerate(fields):
            pieces = [
                (f_re[:, QUART * p : QUART * (p + 1)], f_im[:, QUART * p : QUART * (p + 1)])
                for p in range(4)
            ]
            at = (member * OWN + mode) * ROWS
            for part, (b_re, b_im) in enumerate(turn(pieces, 1)):
                left_ref[part, at : at + ROWS, :QUART] = b_re.astype(BF)
                left_ref[part, at : at + ROWS, QUART:] = b_im.astype(BF)
    for part in range(PARTS):
        tables[part].wait()
        table_ref[part, QUART:, :QUART] = -table_ref[part, :QUART, QUART:]
        table_ref[part, QUART:, QUART:] = table_ref[part, :QUART, :QUART]
        prod_ref[part] = (
            jnp.dot(left_ref[part], table_ref[part], preferred_element_type=F32) * FACTOR
        )
    slots = slots_of(slab)
    sends = []
    for side in range(2):
        for at in range(count):
            rows = slice(at * ROWS, (at + 1) * ROWS)
            block = jnp.concatenate(
                [
                    prod_ref[slots[slot], rows, c * QUART + side * half : c * QUART + (side + 1) * half]
                    for slot in range(PARTS)
                    for c in range(2)
                ],
                axis=0,
            )
            turn_ref[pl.ds(at, half, stride=24), :] = block.T
        send_ref[side] = turn_ref[...].reshape(half, 24, 128).astype(BF)
        sends.append(
            pltpu.make_async_copy(
                send_ref.at[side], out_hbm.at[pl.ds(side * half, half)], sems.at[2 * OWN + PARTS + side]
            )
        )
        sends[side].start()
    for copy in sends:
        copy.wait()


def points_kernel(
    in_ref, ahead_hbm, triple_hbm, back_hbm, out_ref, ahead_ref, triple_ref, back_ref, left_ref, phys_ref, flux_ref, half_ref, sems
):
    chunk = 512
    tall = 24 * GROUPS
    ahead = pltpu.make_async_copy(ahead_hbm, ahead_ref, sems.at[0])
    couple = pltpu.make_async_copy(triple_hbm, triple_ref, sems.at[1])
    back = pltpu.make_async_copy(back_hbm, back_ref, sems.at[2])
    ahead.start()
    couple.start()
    back.start()
    masks = lane_masks()

    def gather(pair, carry):
        for quad in range(SLABS // 4):
            sides = []
            for side in range(2):
                blocks = [in_ref[pair * 2 + side, quad, j].astype(F32) for j in range(4)]
                parts = []
                for part in range(PARTS):
                    mixed = pick(masks, [blocks[(slot - part) % 4] for slot in range(4)])
                    parts.append(pltpu.roll(mixed, 128 - 32 * part, 1) if part else mixed)
                sides.append(parts)
            for part in range(PARTS):
                both = jnp.concatenate([sides[0][part], sides[1][part]], axis=0)
                rows = pl.ds(pl.multiple_of(part * tall + pair * 48, 48), 48)
                left_ref[rows, quad * 128 : (quad + 1) * 128] = both.astype(BF)
        return carry

    lax.fori_loop(0, GROUPS // 2, gather, 0)
    ahead.wait()
    phys_ref[...] = jnp.dot(left_ref[...], ahead_ref[...], preferred_element_type=F32) * FACTOR
    couple.wait()

    def line(part, carry):
        base = pl.multiple_of(part * tall, tall)
        for step in range(NG // chunk):
            lanes = slice(step * chunk, (step + 1) * chunk)
            right = jnp.concatenate(
                [phys_ref[pl.ds(base + group * 24, 24), lanes][:OWN] for group in range(GROUPS)], axis=0
            ).astype(BF)
            sum_x = jnp.zeros((MODES, chunk), F32)
            sum_y = jnp.zeros((MODES, chunk), F32)
            for group in range(GROUPS):
                made = jnp.dot(
                    triple_ref[group * OWN * MODES : (group + 1) * OWN * MODES, :],
                    right,
                    preferred_element_type=F32,
                )
                vel = phys_ref[pl.ds(base + group * 24, 24), lanes]
                for mode in range(OWN):
                    block = made[mode * MODES : (mode + 1) * MODES]
                    sum_x = sum_x + block * vel[OWN + mode : OWN + mode + 1]
                    sum_y = sum_y + block * vel[2 * OWN + mode : 2 * OWN + mode + 1]
            for group in range(GROUPS):
                own = slice(group * OWN, (group + 1) * OWN)
                both = jnp.concatenate([sum_x[own], sum_y[own], jnp.zeros((2, chunk), F32)], axis=0)
                flux_ref[pl.ds(pl.multiple_of((part * GROUPS + group) * 16, 16), 16), lanes] = both.astype(BF)
        return carry

    lax.fori_loop(0, PARTS, line, 0)
    back.wait()
    half_ref[...] = jnp.dot(flux_ref[...], back_ref[...], preferred_element_type=F32) * FACTOR
    for quad in range(LIVE // 4):
        rolled = []
        for part in range(PARTS):
            block = half_ref[part * 128 : (part + 1) * 128, quad * 128 : (quad + 1) * 128]
            rolled.append(pltpu.roll(block, 32 * part, 1) if part else block)
        for j in range(4):
            block = pick(masks, [rolled[(slot - j) % 4] for slot in range(4)]).astype(BF)
            for group in range(GROUPS):
                out_ref[group, quad * 4 + j] = block[group * 16 : (group + 1) * 16]
    out_ref[:, LIVE:] = jnp.zeros((GROUPS, SLABS - LIVE, 16, 128), BF)


def update_kernel(
    in_ref, table_ref, re_ref, im_ref, base_re_ref, base_im_ref, new_re, new_im, wide_ref, left_ref, prod_ref, new_re_ref, new_im_ref, sems
):
    wide_ref[...] = in_ref[...].astype(F32).reshape(DEVS * 16, 128)
    slab = lax.axis_index("grid")
    slots = slots_of(slab)
    for at in range(2 * OWN):
        block = wide_ref[pl.ds(at, DEVS, stride=16), :].T.astype(BF)
        for slot in range(PARTS):
            for c in range(2):
                row = (slot * 2 + c) * ROWS
                left_ref[slots[slot], at * ROWS : (at + 1) * ROWS, c * QUART : (c + 1) * QUART] = block[row : row + ROWS]
    for part in range(PARTS):
        prod_ref[part] = (
            jnp.dot(left_ref[part], table_ref[part], preferred_element_type=F32) * FACTOR
        )
    along_y, along_x = waves_of(slab * ROWS)
    wave_sq = along_y * along_y + along_x * along_x
    keep = (jnp.abs(along_x) * 3.0 < NG) & (along_y * 3.0 < NG)
    damping = VISCOSITY / (NG * NG) * wave_sq
    stores = []
    for mode in range(OWN):
        spectra = []
        for member in range(2):
            rows = slice((member * OWN + mode) * ROWS, (member * OWN + mode + 1) * ROWS)
            spectra.append(
                turn([(prod_ref[part, rows, :QUART], prod_ref[part, rows, QUART:]) for part in range(PARTS)], -1)
            )
        for p in range(4):
            lanes = slice(p * QUART, (p + 1) * QUART)
            (x_re, x_im), (y_re, y_im) = spectra[0][p], spectra[1][p]
            wx, wy = along_x[:, lanes], along_y[:, lanes]
            adv_re = jnp.where(keep[:, lanes], -(wx * x_im + wy * y_im), 0.0)
            adv_im = jnp.where(keep[:, lanes], wx * x_re + wy * y_re, 0.0)
            damp = damping[:, lanes]
            new_re_ref[mode, :, lanes] = base_re_ref[mode, :, lanes] + STEP_WEIGHT * (
                -adv_re - damp * re_ref[mode, :, lanes]
            )
            new_im_ref[mode, :, lanes] = base_im_ref[mode, :, lanes] + STEP_WEIGHT * (
                -adv_im - damp * im_ref[mode, :, lanes]
            )
        stores.append(pltpu.make_async_copy(new_re_ref.at[mode], new_re.at[mode], sems.at[2 * mode]))
        stores.append(pltpu.make_async_copy(new_im_ref.at[mode], new_im.at[mode], sems.at[2 * mode + 1]))
        stores[-2].start()
        stores[-1].start()
    for copy in stores:
        copy.wait()


def call(kernel, outs, scratch, specs, flops, limit=SMALL, space=pltpu.VMEM):
    return pl.pallas_call(
        kernel,
        out_shape=outs,
        in_specs=specs,
        out_specs=jax.tree.map(lambda _: pl.BlockSpec(memory_space=space), outs),
        scratch_shapes=scratch,
        cost_estimate=pl.CostEstimate(flops=flops, bytes_accessed=4 * 1024 * 1024, transcendentals=0),
        compiler_params=pltpu.CompilerParams(vmem_limit_bytes=limit),
    )


def shards(omega_re, omega_im, base_re, base_im, triple):
    vmem = pl.BlockSpec(memory_space=pltpu.VMEM)
    hbm = pl.BlockSpec(memory_space=pltpu.HBM)
    count = 3 * OWN
    ahead_x, back_x = x_tables()
    ahead_y, back_y = y_tables()
    columns = call(
        columns_kernel,
        jax.ShapeDtypeStruct((DEVS, 24, 128), BF),
        [
            pltpu.VMEM((OWN, ROWS, NG), F32),
            pltpu.VMEM((OWN, ROWS, NG), F32),
            pltpu.VMEM((PARTS, 2 * QUART, 2 * QUART), BF),
            pltpu.VMEM((PARTS, count * ROWS, 2 * QUART), BF),
            pltpu.VMEM((PARTS, count * ROWS, 2 * QUART), F32),
            pltpu.VMEM((DEVS // 2 * 24, 128), F32),
            pltpu.VMEM((2, DEVS // 2, 24, 128), BF),
            pltpu.SemaphoreType.DMA((2 * OWN + PARTS + 2,)),
        ],
        [hbm, hbm, hbm],
        1_000_000_000,
        LARGE,
        pltpu.HBM,
    )(omega_re, omega_im, ahead_x)
    slab = lax.all_to_all(columns, ("mode", "grid"), split_axis=0, concat_axis=0, tiled=True)
    halves = call(
        points_kernel,
        jax.ShapeDtypeStruct((GROUPS, SLABS, 16, 128), BF),
        [
            pltpu.VMEM(ahead_y.shape, BF),
            pltpu.VMEM((MODES * MODES, MODES), BF),
            pltpu.VMEM(back_y.shape, BF),
            pltpu.VMEM((PARTS * 24 * GROUPS, NG), BF),
            pltpu.VMEM((PARTS * 24 * GROUPS, NG), F32),
            pltpu.VMEM((PARTS * 16 * GROUPS, NG), BF),
            pltpu.VMEM((PARTS * 16 * GROUPS, LIVE * 32), F32),
            pltpu.SemaphoreType.DMA((3,)),
        ],
        [vmem, hbm, hbm, hbm],
        10_000_000_000,
    )(slab.reshape(GROUPS, SLABS // 4, 4, 24, 128), ahead_y, triple.reshape(MODES * MODES, MODES), back_y)
    rows = lax.all_to_all(halves.reshape(DEVS, 16, 128), ("mode", "grid"), split_axis=0, concat_axis=0, tiled=True)
    new = jax.ShapeDtypeStruct(base_re.shape, F32)
    return call(
        update_kernel,
        (new, new),
        [
            pltpu.VMEM((DEVS * 16, 128), F32),
            pltpu.VMEM((PARTS, 2 * OWN * ROWS, 2 * QUART), BF),
            pltpu.VMEM((PARTS, 2 * OWN * ROWS, 2 * QUART), F32),
            pltpu.VMEM(base_re.shape, F32),
            pltpu.VMEM(base_re.shape, F32),
            pltpu.SemaphoreType.DMA((2 * OWN,)),
        ],
        [vmem] * 6,
        1_000_000_000,
        SMALL,
        pltpu.HBM,
    )(rows, back_x, omega_re, omega_im, base_re, base_im)


def solution(mesh):
    spec = P("mode", "grid", None)
    return jax.shard_map(
        shards, mesh=mesh, in_specs=(spec, spec, spec, spec, P()), out_specs=(spec, spec), check_vma=False
    )
```

```python
import functools
import math

import jax
import jax.numpy as jnp
import ml_dtypes
import numpy as np
from jax import lax
from jax.experimental import pallas as pl
from jax.experimental.pallas import tpu as pltpu
from jax.sharding import PartitionSpec as P

VISCOSITY = 4.0
STEP_WEIGHT = 0.5
NG = 1024
KEPT = 512
MODES = 56
GROUPS = 8
SLABS = 32
DEVS = GROUPS * SLABS
OWN = MODES // GROUPS
ROWS = KEPT // SLABS
PARTS = NG // DEVS
QUART = NG // 4
FACTOR = 1.0 / math.sqrt(NG)
OUT = 22
HOME = 2 * OWN
LIVE = 24
BF = jnp.bfloat16
F32 = jnp.float32
SMALL = 20 * 1024 * 1024
LARGE = 56 * 1024 * 1024


def circle(phases):
    angles = (phases % NG).astype(np.float32) * np.float32(2.0 * math.pi / NG)
    return np.cos(angles), np.sin(angles)


def x_tables():
    ahead, back = [], []
    short = np.arange(QUART)
    for part in range(PARTS):
        points = PARTS * short + part
        cos, sin = circle(short[:, None] * points[None, :])
        ahead.append(np.block([[cos, sin]]))
        cos, sin = circle(points[:, None] * short[None, :])
        back.append(np.block([[cos, -sin], [sin, cos]]))
    return (
        np.stack(ahead).astype(ml_dtypes.bfloat16),
        np.stack(back).astype(ml_dtypes.bfloat16),
    )


def y_tables():
    waves = np.arange(KEPT)
    points = np.arange(NG)
    cos, sin = circle(waves[:, None] * points[None, :])
    weights = np.where(waves == 0, 1.0, 2.0).astype(np.float32)[:, None]
    ahead = np.stack([(weights * cos).reshape(SLABS, ROWS, NG), (-weights * sin).reshape(SLABS, ROWS, NG)], axis=1)
    ahead = ahead.reshape(2 * KEPT, NG).astype(ml_dtypes.bfloat16)
    back = np.stack([cos.T.reshape(NG, SLABS, ROWS), -sin.T.reshape(NG, SLABS, ROWS)], axis=2)
    back = back[:, :LIVE].reshape(NG, LIVE * 2 * ROWS).astype(ml_dtypes.bfloat16)
    return ahead, back


def lane_masks():
    group = lax.broadcasted_iota(jnp.int32, (1, 128), 1) // 32
    return [group == 0, group == 1, group == 2]


def pick(masks, sources):
    return jnp.where(
        masks[0], sources[0], jnp.where(masks[1], sources[1], jnp.where(masks[2], sources[2], sources[3]))
    )


def turn(parts, sign):
    (r0, i0), (r1, i1), (r2, i2), (r3, i3) = parts
    er, ei, fr, fi = r0 + r2, i0 + i2, r0 - r2, i0 - i2
    gr, gi, hr, hi = r1 + r3, i1 + i3, r1 - r3, i1 - i3
    if sign < 0:
        hr, hi = -hr, -hi
    return (
        (er + gr, ei + gi),
        (fr - hi, fi + hr),
        (er - gr, ei - gi),
        (fr + hi, fi - hr),
    )


def waves_of(first_row):
    along_y = (first_row + lax.broadcasted_iota(jnp.int32, (ROWS, NG), 0)).astype(F32)
    index = lax.broadcasted_iota(jnp.int32, (ROWS, NG), 1)
    along_x = jnp.where(index < NG // 2, index, index - NG).astype(F32)
    return along_y, along_x


def slots_of(shift):
    return [lax.rem(slot + PARTS - lax.rem(shift, PARTS), PARTS) for slot in range(PARTS)]


def columns_kernel(
    re_hbm, im_hbm, table_hbm, out_hbm, re_ref, im_ref, table_ref, left_ref, prod_ref, turn_ref, send_ref, sems
):
    loads = []
    for mode in range(OWN):
        loads.append(
            (
                pltpu.make_async_copy(re_hbm.at[mode], re_ref.at[mode], sems.at[2 * mode]),
                pltpu.make_async_copy(im_hbm.at[mode], im_ref.at[mode], sems.at[2 * mode + 1]),
            )
        )
    tables = [
        pltpu.make_async_copy(table_hbm.at[part], table_ref.at[part, pl.ds(0, QUART)], sems.at[2 * OWN + part])
        for part in range(PARTS)
    ]
    for pair in loads:
        pair[0].start()
        pair[1].start()
    for copy in tables:
        copy.start()
    count = 3 * OWN
    half = DEVS // 2
    for at in range(count, OUT):
        turn_ref[pl.ds(at, half, stride=OUT), :] = jnp.zeros((half, 128), F32)
    slab = lax.axis_index("grid")
    along_y, along_x = waves_of(slab * ROWS)
    wave_sq = along_y * along_y + along_x * along_x
    inverse = jnp.where(wave_sq > 0.5, 1.0 / jnp.maximum(wave_sq, 1.0), 0.0)
    scale_y = along_y * inverse
    scale_x = along_x * inverse
    for mode in range(OWN):
        loads[mode][0].wait()
        loads[mode][1].wait()
        w_re, w_im = re_ref[mode], im_ref[mode]
        fields = (
            (w_re, w_im),
            (-scale_y * w_im, scale_y * w_re),
            (scale_x * w_im, -scale_x * w_re),
        )
        for member, (f_re, f_im) in enumerate(fields):
            pieces = [
                (f_re[:, QUART * p : QUART * (p + 1)], f_im[:, QUART * p : QUART * (p + 1)])
                for p in range(4)
            ]
            at = (member * OWN + mode) * ROWS
            for part, (b_re, b_im) in enumerate(turn(pieces, 1)):
                left_ref[part, at : at + ROWS, :QUART] = b_re.astype(BF)
                left_ref[part, at : at + ROWS, QUART:] = b_im.astype(BF)
    for part in range(PARTS):
        tables[part].wait()
        table_ref[part, QUART:, :QUART] = -table_ref[part, :QUART, QUART:]
        table_ref[part, QUART:, QUART:] = table_ref[part, :QUART, :QUART]
        prod_ref[part] = (
            jnp.dot(left_ref[part], table_ref[part], preferred_element_type=F32) * FACTOR
        )
    slots = slots_of(slab)
    sends = []
    for side in range(2):
        for at in range(count):
            rows = slice(at * ROWS, (at + 1) * ROWS)
            block = jnp.concatenate(
                [
                    prod_ref[slots[slot], rows, c * QUART + side * half : c * QUART + (side + 1) * half]
                    for slot in range(PARTS)
                    for c in range(2)
                ],
                axis=0,
            )
            turn_ref[pl.ds(at, half, stride=OUT), :] = block.T
        send_ref[side] = turn_ref[...].astype(BF)
        sends.append(
            pltpu.make_async_copy(
                send_ref.at[side], out_hbm.at[pl.ds(side * half * OUT, half * OUT)], sems.at[2 * OWN + PARTS + side]
            )
        )
        sends[side].start()
    for copy in sends:
        copy.wait()


def points_kernel(
    in_ref, ahead_hbm, triple_hbm, back_hbm, out_ref, ahead_ref, triple_ref, back_ref, wide_ref, left_ref, phys_ref, flux_ref, half_ref, send_ref, sems
):
    chunk = 512
    tall = 24 * GROUPS
    ahead = pltpu.make_async_copy(ahead_hbm, ahead_ref, sems.at[0])
    couple = pltpu.make_async_copy(triple_hbm, triple_ref, sems.at[1])
    back = pltpu.make_async_copy(back_hbm, back_ref, sems.at[2])
    ahead.start()
    couple.start()
    back.start()
    masks = lane_masks()
    span = SLABS * OUT
    for side in range(2):
        wide_ref[side, span:] = jnp.zeros((8, 128), F32)

    def gather(pair, carry):
        for side in range(2):
            wide_ref[side, :span] = in_ref[pl.ds(pl.multiple_of((pair * 2 + side) * span, span), span)].astype(F32)
        for quad in range(SLABS // 4):
            sides = []
            for side in range(2):
                blocks = [wide_ref[side, (quad * 4 + j) * OUT : (quad * 4 + j) * OUT + 24] for j in range(4)]
                parts = []
                for part in range(PARTS):
                    mixed = pick(masks, [blocks[(slot - part) % 4] for slot in range(4)])
                    parts.append(pltpu.roll(mixed, 128 - 32 * part, 1) if part else mixed)
                sides.append(parts)
            for part in range(PARTS):
                both = jnp.concatenate([sides[0][part], sides[1][part]], axis=0)
                rows = pl.ds(pl.multiple_of(part * tall + pair * 48, 48), 48)
                left_ref[rows, quad * 128 : (quad + 1) * 128] = both.astype(BF)
        return carry

    lax.fori_loop(0, GROUPS // 2, gather, 0)
    ahead.wait()
    phys_ref[...] = jnp.dot(left_ref[...], ahead_ref[...], preferred_element_type=F32) * FACTOR
    couple.wait()

    def line(part, carry):
        base = pl.multiple_of(part * tall, tall)
        for step in range(NG // chunk):
            lanes = slice(step * chunk, (step + 1) * chunk)
            right = jnp.concatenate(
                [phys_ref[pl.ds(base + group * 24, 24), lanes][:OWN] for group in range(GROUPS)], axis=0
            ).astype(BF)
            sum_x = jnp.zeros((MODES, chunk), F32)
            sum_y = jnp.zeros((MODES, chunk), F32)
            for group in range(GROUPS):
                made = jnp.dot(
                    triple_ref[group * OWN * MODES : (group + 1) * OWN * MODES, :],
                    right,
                    preferred_element_type=F32,
                )
                vel = phys_ref[pl.ds(base + group * 24, 24), lanes]
                for mode in range(OWN):
                    block = made[mode * MODES : (mode + 1) * MODES]
                    sum_x = sum_x + block * vel[OWN + mode : OWN + mode + 1]
                    sum_y = sum_y + block * vel[2 * OWN + mode : 2 * OWN + mode + 1]
            for group in range(GROUPS):
                own = slice(group * OWN, (group + 1) * OWN)
                both = jnp.concatenate([sum_x[own], sum_y[own], jnp.zeros((2, chunk), F32)], axis=0)
                flux_ref[pl.ds(pl.multiple_of((part * GROUPS + group) * 16, 16), 16), lanes] = both.astype(BF)
        return carry

    lax.fori_loop(0, PARTS, line, 0)
    back.wait()
    half_ref[...] = jnp.dot(flux_ref[...], back_ref[...], preferred_element_type=F32) * FACTOR
    for quad in range(LIVE // 4):
        rolled = []
        for part in range(PARTS):
            block = half_ref[part * 128 : (part + 1) * 128, quad * 128 : (quad + 1) * 128]
            rolled.append(pltpu.roll(block, 32 * part, 1) if part else block)
        for j in range(4):
            block = pick(masks, [rolled[(slot - j) % 4] for slot in range(4)])
            for group in range(GROUPS):
                at = (group * SLABS + quad * 4 + j) * HOME
                send_ref[at : at + HOME] = block[group * 16 : group * 16 + HOME]
    for group in range(GROUPS):
        at = (group * SLABS + LIVE) * HOME
        send_ref[at : at + (SLABS - LIVE) * HOME] = jnp.zeros(((SLABS - LIVE) * HOME, 128), F32)
    out_ref[...] = send_ref[...].astype(BF)


def update_kernel(
    in_ref, table_ref, re_ref, im_ref, base_re_ref, base_im_ref, new_re, new_im, wide_ref, left_ref, prod_ref, new_re_ref, new_im_ref, sems
):
    wide_ref[...] = in_ref[...].astype(F32)
    slab = lax.axis_index("grid")
    slots = slots_of(slab)
    for at in range(2 * OWN):
        block = wide_ref[pl.ds(at, DEVS, stride=HOME), :].T.astype(BF)
        for slot in range(PARTS):
            for c in range(2):
                row = (slot * 2 + c) * ROWS
                left_ref[slots[slot], at * ROWS : (at + 1) * ROWS, c * QUART : (c + 1) * QUART] = block[row : row + ROWS]
    for part in range(PARTS):
        prod_ref[part] = (
            jnp.dot(left_ref[part], table_ref[part], preferred_element_type=F32) * FACTOR
        )
    along_y, along_x = waves_of(slab * ROWS)
    wave_sq = along_y * along_y + along_x * along_x
    keep = (jnp.abs(along_x) * 3.0 < NG) & (along_y * 3.0 < NG)
    damping = VISCOSITY / (NG * NG) * wave_sq
    stores = []
    for mode in range(OWN):
        spectra = []
        for member in range(2):
            rows = slice((member * OWN + mode) * ROWS, (member * OWN + mode + 1) * ROWS)
            spectra.append(
                turn([(prod_ref[part, rows, :QUART], prod_ref[part, rows, QUART:]) for part in range(PARTS)], -1)
            )
        for p in range(4):
            lanes = slice(p * QUART, (p + 1) * QUART)
            (x_re, x_im), (y_re, y_im) = spectra[0][p], spectra[1][p]
            wx, wy = along_x[:, lanes], along_y[:, lanes]
            adv_re = jnp.where(keep[:, lanes], -(wx * x_im + wy * y_im), 0.0)
            adv_im = jnp.where(keep[:, lanes], wx * x_re + wy * y_re, 0.0)
            damp = damping[:, lanes]
            new_re_ref[mode, :, lanes] = base_re_ref[mode, :, lanes] + STEP_WEIGHT * (
                -adv_re - damp * re_ref[mode, :, lanes]
            )
            new_im_ref[mode, :, lanes] = base_im_ref[mode, :, lanes] + STEP_WEIGHT * (
                -adv_im - damp * im_ref[mode, :, lanes]
            )
        stores.append(pltpu.make_async_copy(new_re_ref.at[mode], new_re.at[mode], sems.at[2 * mode]))
        stores.append(pltpu.make_async_copy(new_im_ref.at[mode], new_im.at[mode], sems.at[2 * mode + 1]))
        stores[-2].start()
        stores[-1].start()
    for copy in stores:
        copy.wait()


def call(kernel, outs, scratch, specs, flops, limit=SMALL, space=pltpu.VMEM):
    return pl.pallas_call(
        kernel,
        out_shape=outs,
        in_specs=specs,
        out_specs=jax.tree.map(lambda _: pl.BlockSpec(memory_space=space), outs),
        scratch_shapes=scratch,
        cost_estimate=pl.CostEstimate(flops=flops, bytes_accessed=4 * 1024 * 1024, transcendentals=0),
        compiler_params=pltpu.CompilerParams(vmem_limit_bytes=limit),
    )


def exchange(array, count):
    blocks = array.reshape(DEVS, count // 2, 2, 128)
    blocks = lax.all_to_all(blocks, ("mode", "grid"), split_axis=0, concat_axis=0, tiled=True)
    return blocks.reshape(DEVS * count, 128)


def shards(omega_re, omega_im, base_re, base_im, triple):
    vmem = pl.BlockSpec(memory_space=pltpu.VMEM)
    hbm = pl.BlockSpec(memory_space=pltpu.HBM)
    count = 3 * OWN
    ahead_x, back_x = x_tables()
    ahead_y, back_y = y_tables()
    columns = call(
        columns_kernel,
        jax.ShapeDtypeStruct((DEVS * OUT, 128), BF),
        [
            pltpu.VMEM((OWN, ROWS, NG), F32),
            pltpu.VMEM((OWN, ROWS, NG), F32),
            pltpu.VMEM((PARTS, 2 * QUART, 2 * QUART), BF),
            pltpu.VMEM((PARTS, count * ROWS, 2 * QUART), BF),
            pltpu.VMEM((PARTS, count * ROWS, 2 * QUART), F32),
            pltpu.VMEM((DEVS // 2 * OUT, 128), F32),
            pltpu.VMEM((2, DEVS // 2 * OUT, 128), BF),
            pltpu.SemaphoreType.DMA((2 * OWN + PARTS + 2,)),
        ],
        [hbm, hbm, hbm],
        1_000_000_000,
        LARGE,
        pltpu.HBM,
    )(omega_re, omega_im, ahead_x)
    slab = exchange(columns, OUT)
    halves = call(
        points_kernel,
        jax.ShapeDtypeStruct((DEVS * HOME, 128), BF),
        [
            pltpu.VMEM(ahead_y.shape, BF),
            pltpu.VMEM((MODES * MODES, MODES), BF),
            pltpu.VMEM(back_y.shape, BF),
            pltpu.VMEM((2, SLABS * OUT + 8, 128), F32),
            pltpu.VMEM((PARTS * 24 * GROUPS, NG), BF),
            pltpu.VMEM((PARTS * 24 * GROUPS, NG), F32),
            pltpu.VMEM((PARTS * 16 * GROUPS, NG), BF),
            pltpu.VMEM((PARTS * 16 * GROUPS, LIVE * 32), F32),
            pltpu.VMEM((DEVS * HOME, 128), F32),
            pltpu.SemaphoreType.DMA((3,)),
        ],
        [vmem, hbm, hbm, hbm],
        10_000_000_000,
    )(slab, ahead_y, triple.reshape(MODES * MODES, MODES), back_y)
    rows = exchange(halves, HOME)
    new = jax.ShapeDtypeStruct(base_re.shape, F32)
    return call(
        update_kernel,
        (new, new),
        [
            pltpu.VMEM((DEVS * HOME, 128), F32),
            pltpu.VMEM((PARTS, 2 * OWN * ROWS, 2 * QUART), BF),
            pltpu.VMEM((PARTS, 2 * OWN * ROWS, 2 * QUART), F32),
            pltpu.VMEM(base_re.shape, F32),
            pltpu.VMEM(base_re.shape, F32),
            pltpu.SemaphoreType.DMA((2 * OWN,)),
        ],
        [vmem] * 6,
        1_000_000_000,
        SMALL,
        pltpu.HBM,
    )(rows, back_x, omega_re, omega_im, base_re, base_im)


def solution(mesh):
    spec = P("mode", "grid", None)
    return jax.shard_map(
        shards, mesh=mesh, in_specs=(spec, spec, spec, spec, P()), out_specs=(spec, spec), check_vma=False
    )
```

```python
import functools
import math

import jax
import jax.numpy as jnp
import ml_dtypes
import numpy as np
from jax import lax
from jax.experimental import pallas as pl
from jax.experimental.pallas import tpu as pltpu
from jax.sharding import PartitionSpec as P

VISCOSITY = 4.0
STEP_WEIGHT = 0.5
NG = 1024
KEPT = 512
MODES = 56
GROUPS = 8
SLABS = 32
DEVS = GROUPS * SLABS
OWN = MODES // GROUPS
ROWS = KEPT // SLABS
PARTS = NG // DEVS
QUART = NG // 4
FACTOR = 1.0 / math.sqrt(NG)
OUT = 22
HOME = 2 * OWN
LIVE = 24
BF = jnp.bfloat16
F32 = jnp.float32
SMALL = 20 * 1024 * 1024
LARGE = 56 * 1024 * 1024


def circle(phases):
    angles = (phases % NG).astype(np.float32) * np.float32(2.0 * math.pi / NG)
    return np.cos(angles), np.sin(angles)


def x_tables():
    ahead, back = [], []
    short = np.arange(QUART)
    for part in range(PARTS):
        points = PARTS * short + part
        cos, sin = circle(short[:, None] * points[None, :])
        ahead.append(np.block([[cos, sin]]))
        cos, sin = circle(points[:, None] * short[None, :])
        back.append(np.block([[cos, -sin], [sin, cos]]))
    return (
        np.stack(ahead).astype(ml_dtypes.bfloat16),
        np.stack(back).astype(ml_dtypes.bfloat16),
    )


def y_tables():
    waves = np.arange(KEPT)
    points = np.arange(NG)
    cos, sin = circle(waves[:, None] * points[None, :])
    weights = np.where(waves == 0, 1.0, 2.0).astype(np.float32)[:, None]
    ahead = np.stack([(weights * cos).reshape(SLABS, ROWS, NG), (-weights * sin).reshape(SLABS, ROWS, NG)], axis=1)
    ahead = ahead.reshape(2 * KEPT, NG).astype(ml_dtypes.bfloat16)
    back = np.stack([cos.T.reshape(NG, SLABS, ROWS), -sin.T.reshape(NG, SLABS, ROWS)], axis=2)
    back = back[:, :LIVE].reshape(NG, LIVE * 2 * ROWS).astype(ml_dtypes.bfloat16)
    return ahead, back


def lane_masks():
    group = lax.broadcasted_iota(jnp.int32, (1, 128), 1) // 32
    return [group == 0, group == 1, group == 2]


def pick(masks, sources):
    return jnp.where(
        masks[0], sources[0], jnp.where(masks[1], sources[1], jnp.where(masks[2], sources[2], sources[3]))
    )


def turn(parts, sign):
    (r0, i0), (r1, i1), (r2, i2), (r3, i3) = parts
    er, ei, fr, fi = r0 + r2, i0 + i2, r0 - r2, i0 - i2
    gr, gi, hr, hi = r1 + r3, i1 + i3, r1 - r3, i1 - i3
    if sign < 0:
        hr, hi = -hr, -hi
    return (
        (er + gr, ei + gi),
        (fr - hi, fi + hr),
        (er - gr, ei - gi),
        (fr + hi, fi - hr),
    )


def waves_of(first_row):
    along_y = (first_row + lax.broadcasted_iota(jnp.int32, (ROWS, NG), 0)).astype(F32)
    index = lax.broadcasted_iota(jnp.int32, (ROWS, NG), 1)
    along_x = jnp.where(index < NG // 2, index, index - NG).astype(F32)
    return along_y, along_x


def slots_of(shift):
    return [lax.rem(slot + PARTS - lax.rem(shift, PARTS), PARTS) for slot in range(PARTS)]


def columns_kernel(
    re_hbm, im_hbm, table_hbm, out_hbm, re_ref, im_ref, table_ref, left_ref, prod_ref, turn_ref, send_ref, sems
):
    loads = []
    for mode in range(OWN):
        loads.append(
            (
                pltpu.make_async_copy(re_hbm.at[mode], re_ref.at[mode], sems.at[2 * mode]),
                pltpu.make_async_copy(im_hbm.at[mode], im_ref.at[mode], sems.at[2 * mode + 1]),
            )
        )
    tables = [
        pltpu.make_async_copy(table_hbm.at[part], table_ref.at[part, pl.ds(0, QUART)], sems.at[2 * OWN + part])
        for part in range(PARTS)
    ]
    for pair in loads:
        pair[0].start()
        pair[1].start()
    for copy in tables:
        copy.start()
    count = 3 * OWN
    half = DEVS // 2
    for at in range(count, OUT):
        turn_ref[pl.ds(at, half, stride=OUT), :] = jnp.zeros((half, 128), F32)
    slab = lax.axis_index("grid")
    along_y, along_x = waves_of(slab * ROWS)
    wave_sq = along_y * along_y + along_x * along_x
    inverse = jnp.where(wave_sq > 0.5, 1.0 / jnp.maximum(wave_sq, 1.0), 0.0)
    scale_y = along_y * inverse
    scale_x = along_x * inverse
    for mode in range(OWN):
        loads[mode][0].wait()
        loads[mode][1].wait()
        w_re, w_im = re_ref[mode], im_ref[mode]
        fields = (
            (w_re, w_im),
            (-scale_y * w_im, scale_y * w_re),
            (scale_x * w_im, -scale_x * w_re),
        )
        for member, (f_re, f_im) in enumerate(fields):
            pieces = [
                (f_re[:, QUART * p : QUART * (p + 1)], f_im[:, QUART * p : QUART * (p + 1)])
                for p in range(4)
            ]
            at = (member * OWN + mode) * ROWS
            for part, (b_re, b_im) in enumerate(turn(pieces, 1)):
                left_ref[part, at : at + ROWS, :QUART] = b_re.astype(BF)
                left_ref[part, at : at + ROWS, QUART:] = b_im.astype(BF)
    for part in range(PARTS):
        tables[part].wait()
        table_ref[part, QUART:, :QUART] = -table_ref[part, :QUART, QUART:]
        table_ref[part, QUART:, QUART:] = table_ref[part, :QUART, :QUART]
        prod_ref[part] = (
            jnp.dot(left_ref[part], table_ref[part], preferred_element_type=F32) * FACTOR
        )
    slots = slots_of(slab)
    sends = []
    for side in range(2):
        for at in range(count):
            rows = slice(at * ROWS, (at + 1) * ROWS)
            block = jnp.concatenate(
                [
                    prod_ref[slots[slot], rows, c * QUART + side * half : c * QUART + (side + 1) * half]
                    for slot in range(PARTS)
                    for c in range(2)
                ],
                axis=0,
            )
            turn_ref[pl.ds(at, half, stride=OUT), :] = block.T
        send_ref[side] = turn_ref[...].astype(BF)
        sends.append(
            pltpu.make_async_copy(
                send_ref.at[side], out_hbm.at[pl.ds(side * half * OUT, half * OUT)], sems.at[2 * OWN + PARTS + side]
            )
        )
        sends[side].start()
    for copy in sends:
        copy.wait()


def points_kernel(
    in_ref, ahead_ref, triple_ref, back_ref, out_ref, wide_ref, left_ref, phys_ref, flux_ref, half_ref, send_ref
):
    chunk = 512
    tall = 24 * GROUPS
    masks = lane_masks()
    span = SLABS * OUT
    for side in range(2):
        wide_ref[side, span:] = jnp.zeros((8, 128), F32)

    def gather(pair, carry):
        for side in range(2):
            wide_ref[side, :span] = in_ref[pl.ds(pl.multiple_of((pair * 2 + side) * span, span), span)].astype(F32)
        for quad in range(SLABS // 4):
            sides = []
            for side in range(2):
                blocks = [wide_ref[side, (quad * 4 + j) * OUT : (quad * 4 + j) * OUT + 24] for j in range(4)]
                parts = []
                for part in range(PARTS):
                    mixed = pick(masks, [blocks[(slot - part) % 4] for slot in range(4)])
                    parts.append(pltpu.roll(mixed, 128 - 32 * part, 1) if part else mixed)
                sides.append(parts)
            for part in range(PARTS):
                both = jnp.concatenate([sides[0][part], sides[1][part]], axis=0)
                rows = pl.ds(pl.multiple_of(part * tall + pair * 48, 48), 48)
                left_ref[rows, quad * 128 : (quad + 1) * 128] = both.astype(BF)
        return carry

    lax.fori_loop(0, GROUPS // 2, gather, 0, unroll=True)
    phys_ref[...] = jnp.dot(left_ref[...], ahead_ref[...], preferred_element_type=F32) * FACTOR

    def line(part, carry):
        base = pl.multiple_of(part * tall, tall)
        for step in range(NG // chunk):
            lanes = slice(step * chunk, (step + 1) * chunk)
            right = jnp.concatenate(
                [phys_ref[pl.ds(base + group * 24, 24), lanes][:OWN] for group in range(GROUPS)], axis=0
            ).astype(BF)
            sum_x = jnp.zeros((MODES, chunk), F32)
            sum_y = jnp.zeros((MODES, chunk), F32)
            for group in range(GROUPS):
                made = jnp.dot(
                    triple_ref[group * OWN * MODES : (group + 1) * OWN * MODES, :],
                    right,
                    preferred_element_type=F32,
                )
                vel = phys_ref[pl.ds(base + group * 24, 24), lanes]
                for mode in range(OWN):
                    block = made[mode * MODES : (mode + 1) * MODES]
                    sum_x = sum_x + block * vel[OWN + mode : OWN + mode + 1]
                    sum_y = sum_y + block * vel[2 * OWN + mode : 2 * OWN + mode + 1]
            for group in range(GROUPS):
                own = slice(group * OWN, (group + 1) * OWN)
                both = jnp.concatenate([sum_x[own], sum_y[own], jnp.zeros((2, chunk), F32)], axis=0)
                flux_ref[pl.ds(pl.multiple_of((part * GROUPS + group) * 16, 16), 16), lanes] = both.astype(BF)
        return carry

    lax.fori_loop(0, PARTS, line, 0)
    half_ref[...] = jnp.dot(flux_ref[...], back_ref[...], preferred_element_type=F32) * FACTOR
    for quad in range(LIVE // 4):
        rolled = []
        for part in range(PARTS):
            block = half_ref[part * 128 : (part + 1) * 128, quad * 128 : (quad + 1) * 128]
            rolled.append(pltpu.roll(block, 32 * part, 1) if part else block)
        for j in range(4):
            block = pick(masks, [rolled[(slot - j) % 4] for slot in range(4)])
            for group in range(GROUPS):
                at = (group * SLABS + quad * 4 + j) * HOME
                send_ref[at : at + HOME] = block[group * 16 : group * 16 + HOME]
    for group in range(GROUPS):
        at = (group * SLABS + LIVE) * HOME
        send_ref[at : at + (SLABS - LIVE) * HOME] = jnp.zeros(((SLABS - LIVE) * HOME, 128), F32)
    out_ref[...] = send_ref[...].astype(BF)


def update_kernel(
    in_ref, table_ref, re_ref, im_ref, base_re_ref, base_im_ref, new_re, new_im, wide_ref, left_ref, prod_ref, new_re_ref, new_im_ref, sems
):
    wide_ref[...] = in_ref[...].astype(F32)
    slab = lax.axis_index("grid")
    slots = slots_of(slab)
    for at in range(2 * OWN):
        block = wide_ref[pl.ds(at, DEVS, stride=HOME), :].T.astype(BF)
        for slot in range(PARTS):
            for c in range(2):
                row = (slot * 2 + c) * ROWS
                left_ref[slots[slot], at * ROWS : (at + 1) * ROWS, c * QUART : (c + 1) * QUART] = block[row : row + ROWS]
    for part in range(PARTS):
        prod_ref[part] = (
            jnp.dot(left_ref[part], table_ref[part], preferred_element_type=F32) * FACTOR
        )
    along_y, along_x = waves_of(slab * ROWS)
    wave_sq = along_y * along_y + along_x * along_x
    keep = (jnp.abs(along_x) * 3.0 < NG) & (along_y * 3.0 < NG)
    damping = VISCOSITY / (NG * NG) * wave_sq
    stores = []
    for mode in range(OWN):
        spectra = []
        for member in range(2):
            rows = slice((member * OWN + mode) * ROWS, (member * OWN + mode + 1) * ROWS)
            spectra.append(
                turn([(prod_ref[part, rows, :QUART], prod_ref[part, rows, QUART:]) for part in range(PARTS)], -1)
            )
        for p in range(4):
            lanes = slice(p * QUART, (p + 1) * QUART)
            (x_re, x_im), (y_re, y_im) = spectra[0][p], spectra[1][p]
            wx, wy = along_x[:, lanes], along_y[:, lanes]
            adv_re = jnp.where(keep[:, lanes], -(wx * x_im + wy * y_im), 0.0)
            adv_im = jnp.where(keep[:, lanes], wx * x_re + wy * y_re, 0.0)
            damp = damping[:, lanes]
            new_re_ref[mode, :, lanes] = base_re_ref[mode, :, lanes] + STEP_WEIGHT * (
                -adv_re - damp * re_ref[mode, :, lanes]
            )
            new_im_ref[mode, :, lanes] = base_im_ref[mode, :, lanes] + STEP_WEIGHT * (
                -adv_im - damp * im_ref[mode, :, lanes]
            )
        stores.append(pltpu.make_async_copy(new_re_ref.at[mode], new_re.at[mode], sems.at[2 * mode]))
        stores.append(pltpu.make_async_copy(new_im_ref.at[mode], new_im.at[mode], sems.at[2 * mode + 1]))
        stores[-2].start()
        stores[-1].start()
    for copy in stores:
        copy.wait()


def call(kernel, outs, scratch, specs, flops, limit=SMALL, space=pltpu.VMEM):
    return pl.pallas_call(
        kernel,
        out_shape=outs,
        in_specs=specs,
        out_specs=jax.tree.map(lambda _: pl.BlockSpec(memory_space=space), outs),
        scratch_shapes=scratch,
        cost_estimate=pl.CostEstimate(flops=flops, bytes_accessed=4 * 1024 * 1024, transcendentals=0),
        compiler_params=pltpu.CompilerParams(vmem_limit_bytes=limit),
    )


def exchange(array, count):
    blocks = array.reshape(DEVS, count // 2, 2, 128)
    blocks = lax.all_to_all(blocks, ("mode", "grid"), split_axis=0, concat_axis=0, tiled=True)
    return blocks.reshape(DEVS * count, 128)


def shards(omega_re, omega_im, base_re, base_im, triple):
    vmem = pl.BlockSpec(memory_space=pltpu.VMEM)
    hbm = pl.BlockSpec(memory_space=pltpu.HBM)
    count = 3 * OWN
    ahead_x, back_x = x_tables()
    ahead_y, back_y = y_tables()
    columns = call(
        columns_kernel,
        jax.ShapeDtypeStruct((DEVS * OUT, 128), BF),
        [
            pltpu.VMEM((OWN, ROWS, NG), F32),
            pltpu.VMEM((OWN, ROWS, NG), F32),
            pltpu.VMEM((PARTS, 2 * QUART, 2 * QUART), BF),
            pltpu.VMEM((PARTS, count * ROWS, 2 * QUART), BF),
            pltpu.VMEM((PARTS, count * ROWS, 2 * QUART), F32),
            pltpu.VMEM((DEVS // 2 * OUT, 128), F32),
            pltpu.VMEM((2, DEVS // 2 * OUT, 128), BF),
            pltpu.SemaphoreType.DMA((2 * OWN + PARTS + 2,)),
        ],
        [hbm, hbm, hbm],
        1_000_000_000,
        LARGE,
        pltpu.HBM,
    )(omega_re, omega_im, ahead_x)
    slab = exchange(columns, OUT)
    halves = call(
        points_kernel,
        jax.ShapeDtypeStruct((DEVS * HOME, 128), BF),
        [
            pltpu.VMEM((2, SLABS * OUT + 8, 128), F32),
            pltpu.VMEM((PARTS * 24 * GROUPS, NG), BF),
            pltpu.VMEM((PARTS * 24 * GROUPS, NG), F32),
            pltpu.VMEM((PARTS * 16 * GROUPS, NG), BF),
            pltpu.VMEM((PARTS * 16 * GROUPS, LIVE * 32), F32),
            pltpu.VMEM((DEVS * HOME, 128), F32),
        ],
        [vmem] * 4,
        10_000_000_000,
    )(slab, ahead_y, triple.reshape(MODES * MODES, MODES), back_y)
    rows = exchange(halves, HOME)
    new = jax.ShapeDtypeStruct(base_re.shape, F32)
    return call(
        update_kernel,
        (new, new),
        [
            pltpu.VMEM((DEVS * HOME, 128), F32),
            pltpu.VMEM((PARTS, 2 * OWN * ROWS, 2 * QUART), BF),
            pltpu.VMEM((PARTS, 2 * OWN * ROWS, 2 * QUART), F32),
            pltpu.VMEM(base_re.shape, F32),
            pltpu.VMEM(base_re.shape, F32),
            pltpu.SemaphoreType.DMA((2 * OWN,)),
        ],
        [vmem] * 6,
        1_000_000_000,
        SMALL,
        pltpu.HBM,
    )(rows, back_x, omega_re, omega_im, base_re, base_im)


def solution(mesh):
    spec = P("mode", "grid", None)
    return jax.shard_map(
        shards, mesh=mesh, in_specs=(spec, spec, spec, spec, P()), out_specs=(spec, spec), check_vma=False
    )
```

```python
import functools
import math

import jax
import jax.numpy as jnp
import ml_dtypes
import numpy as np
from jax import lax
from jax.experimental import pallas as pl
from jax.experimental.pallas import tpu as pltpu
from jax.sharding import PartitionSpec as P

VISCOSITY = 4.0
STEP_WEIGHT = 0.5
NG = 1024
KEPT = 512
MODES = 56
GROUPS = 8
SLABS = 32
DEVS = GROUPS * SLABS
OWN = MODES // GROUPS
ROWS = KEPT // SLABS
HALF = NG // 2
PARTS = NG // DEVS
QUART = NG // 4
FACTOR = 1.0 / math.sqrt(NG)
OUT = 22
HOME = 2 * OWN
LIVE = 24
BF = jnp.bfloat16
F32 = jnp.float32
SMALL = 20 * 1024 * 1024
LARGE = 56 * 1024 * 1024


def circle(phases):
    angles = (phases % NG).astype(np.float32) * np.float32(2.0 * math.pi / NG)
    return np.cos(angles), np.sin(angles)


def x_tables():
    ahead, back = [], []
    short = np.arange(QUART)
    for part in range(PARTS):
        points = PARTS * short + part
        cos, sin = circle(short[:, None] * points[None, :])
        ahead.append(np.block([[cos, sin]]))
        cos, sin = circle(points[:, None] * short[None, :])
        back.append(np.block([[cos, -sin], [sin, cos]]))
    return (
        np.stack(ahead).astype(ml_dtypes.bfloat16),
        np.stack(back).astype(ml_dtypes.bfloat16),
    )


def y_tables():
    waves = np.arange(KEPT)
    cos, sin = circle(waves[:, None] * np.arange(HALF)[None, :])
    weights = np.where(waves == 0, 1.0, 2.0).astype(np.float32)[:, None]
    split = (SLABS // 8, 2, 4, ROWS // 2, 2, HALF)
    ahead = np.stack([(weights * cos).reshape(split), (-weights * sin).reshape(split)], axis=6)
    ahead = ahead.transpose(4, 0, 2, 6, 3, 1, 5).reshape(2, KEPT, HALF)
    back = np.stack([cos.reshape(split), -sin.reshape(split)], axis=6)[: LIVE // 8]
    back = back.transpose(4, 5, 0, 2, 6, 3, 1).reshape(2, HALF, LIVE * ROWS)
    return ahead.astype(ml_dtypes.bfloat16), back.astype(ml_dtypes.bfloat16)


def even_odd(first, second):
    lane = lax.broadcasted_iota(jnp.int32, first.shape, 1)
    return (
        jnp.where(lane % 2 == 0, first, pltpu.roll(second, 1, 1)),
        jnp.where(lane % 2 == 0, pltpu.roll(first, 127, 1), second),
    )


def lane_masks():
    group = lax.broadcasted_iota(jnp.int32, (1, 128), 1) // 32
    return [group == 0, group == 1, group == 2]


def pick(masks, sources):
    return jnp.where(
        masks[0], sources[0], jnp.where(masks[1], sources[1], jnp.where(masks[2], sources[2], sources[3]))
    )


def turn(parts, sign):
    (r0, i0), (r1, i1), (r2, i2), (r3, i3) = parts
    er, ei, fr, fi = r0 + r2, i0 + i2, r0 - r2, i0 - i2
    gr, gi, hr, hi = r1 + r3, i1 + i3, r1 - r3, i1 - i3
    if sign < 0:
        hr, hi = -hr, -hi
    return (
        (er + gr, ei + gi),
        (fr - hi, fi + hr),
        (er - gr, ei - gi),
        (fr + hi, fi - hr),
    )


def waves_of(first_row):
    along_y = (first_row + lax.broadcasted_iota(jnp.int32, (ROWS, NG), 0)).astype(F32)
    index = lax.broadcasted_iota(jnp.int32, (ROWS, NG), 1)
    along_x = jnp.where(index < NG // 2, index, index - NG).astype(F32)
    return along_y, along_x


def slots_of(shift):
    return [lax.rem(slot + PARTS - lax.rem(shift, PARTS), PARTS) for slot in range(PARTS)]


def columns_kernel(
    re_hbm, im_hbm, table_hbm, out_hbm, re_ref, im_ref, table_ref, left_ref, prod_ref, turn_ref, send_ref, sems
):
    loads = []
    for mode in range(OWN):
        loads.append(
            (
                pltpu.make_async_copy(re_hbm.at[mode], re_ref.at[mode], sems.at[2 * mode]),
                pltpu.make_async_copy(im_hbm.at[mode], im_ref.at[mode], sems.at[2 * mode + 1]),
            )
        )
    tables = [
        pltpu.make_async_copy(table_hbm.at[part], table_ref.at[part, pl.ds(0, QUART)], sems.at[2 * OWN + part])
        for part in range(PARTS)
    ]
    for pair in loads:
        pair[0].start()
        pair[1].start()
    for copy in tables:
        copy.start()
    count = 3 * OWN
    half = DEVS // 2
    for at in range(count, OUT):
        turn_ref[pl.ds(at, half, stride=OUT), :] = jnp.zeros((half, 128), F32)
    slab = lax.axis_index("grid")
    along_y, along_x = waves_of(slab * ROWS)
    wave_sq = along_y * along_y + along_x * along_x
    inverse = jnp.where(wave_sq > 0.5, 1.0 / jnp.maximum(wave_sq, 1.0), 0.0)
    scale_y = along_y * inverse
    scale_x = along_x * inverse
    for mode in range(OWN):
        loads[mode][0].wait()
        loads[mode][1].wait()
        w_re, w_im = re_ref[mode], im_ref[mode]
        fields = (
            (w_re, w_im),
            (-scale_y * w_im, scale_y * w_re),
            (scale_x * w_im, -scale_x * w_re),
        )
        for member, (f_re, f_im) in enumerate(fields):
            pieces = [
                (f_re[:, QUART * p : QUART * (p + 1)], f_im[:, QUART * p : QUART * (p + 1)])
                for p in range(4)
            ]
            at = (member * OWN + mode) * ROWS
            for part, (b_re, b_im) in enumerate(turn(pieces, 1)):
                left_ref[part, at : at + ROWS, :QUART] = b_re.astype(BF)
                left_ref[part, at : at + ROWS, QUART:] = b_im.astype(BF)
    for part in range(PARTS):
        tables[part].wait()
        table_ref[part, QUART:, :QUART] = -table_ref[part, :QUART, QUART:]
        table_ref[part, QUART:, QUART:] = table_ref[part, :QUART, :QUART]
        prod_ref[part] = (
            jnp.dot(left_ref[part], table_ref[part], preferred_element_type=F32) * FACTOR
        )
    slots = slots_of(slab)
    sends = []
    for side in range(2):
        for at in range(count):
            rows = slice(at * ROWS, (at + 1) * ROWS)
            block = jnp.concatenate(
                [
                    prod_ref[slots[slot], rows, c * QUART + side * half : c * QUART + (side + 1) * half]
                    for slot in range(PARTS)
                    for c in range(2)
                ],
                axis=0,
            )
            turn_ref[pl.ds(at, half, stride=OUT), :] = block.T
        send_ref[side] = turn_ref[...].astype(BF)
        sends.append(
            pltpu.make_async_copy(
                send_ref.at[side], out_hbm.at[pl.ds(side * half * OUT, half * OUT)], sems.at[2 * OWN + PARTS + side]
            )
        )
        sends[side].start()
    for copy in sends:
        copy.wait()


def points_kernel(
    in_ref, ahead_ref, triple_ref, back_ref, out_ref, wide_ref, left_ref, phys_ref, keep_ref, flux_ref, half_ref, send_ref
):
    chunk = HALF
    tall = 24 * GROUPS
    masks = lane_masks()
    span = SLABS * OUT
    for side in range(2):
        wide_ref[side, span:] = jnp.zeros((8, 128), F32)

    def gather(pair, carry):
        for side in range(2):
            wide_ref[side, :span] = in_ref[pl.ds(pl.multiple_of((pair * 2 + side) * span, span), span)].astype(F32)
        for eight in range(SLABS // 8):
            quads = []
            for quad in (2 * eight, 2 * eight + 1):
                blocks = []
                for j in range(4):
                    at = (quad * 4 + j) * OUT
                    blocks.append(jnp.concatenate([wide_ref[side, at : at + 24] for side in range(2)], axis=0).astype(BF))
                quads.append(blocks)
            for part in range(PARTS):
                mixed = []
                for blocks in quads:
                    one = pick(masks, [blocks[(slot - part) % 4] for slot in range(4)])
                    mixed.append(pltpu.roll(one, 128 - 32 * part, 1) if part else one)
                rows = pl.ds(pl.multiple_of(part * tall + pair * 48, 48), 48)
                for parity, both in enumerate(even_odd(*mixed)):
                    left_ref[parity, rows, eight * 128 : (eight + 1) * 128] = both.astype(BF)
        return carry

    lax.fori_loop(0, GROUPS // 2, gather, 0, unroll=True)
    even = jnp.dot(left_ref[0], ahead_ref[0], preferred_element_type=F32) * FACTOR
    odd = jnp.dot(left_ref[1], ahead_ref[1], preferred_element_type=F32) * FACTOR
    phys_ref[:, :HALF] = even + odd
    phys_ref[:, HALF:] = even - odd

    def line(part, carry):
        base = pl.multiple_of(part * tall, tall)
        for step in range(NG // chunk):
            lanes = slice(step * chunk, (step + 1) * chunk)
            right = jnp.concatenate(
                [phys_ref[pl.ds(base + group * 24, 24), lanes][:OWN] for group in range(GROUPS)], axis=0
            ).astype(BF)
            sum_x = jnp.zeros((MODES, chunk), F32)
            sum_y = jnp.zeros((MODES, chunk), F32)
            for group in range(GROUPS):
                made = jnp.dot(
                    triple_ref[group * OWN * MODES : (group + 1) * OWN * MODES, :],
                    right,
                    preferred_element_type=F32,
                )
                vel = phys_ref[pl.ds(base + group * 24, 24), lanes]
                for mode in range(OWN):
                    block = made[mode * MODES : (mode + 1) * MODES]
                    sum_x = sum_x + block * vel[OWN + mode : OWN + mode + 1]
                    sum_y = sum_y + block * vel[2 * OWN + mode : 2 * OWN + mode + 1]
            for group in range(GROUPS):
                own = slice(group * OWN, (group + 1) * OWN)
                both = jnp.concatenate([sum_x[own], sum_y[own], jnp.zeros((2, chunk), F32)], axis=0)
                if step == 0:
                    keep_ref[group * 16 : (group + 1) * 16] = both
                else:
                    first = keep_ref[group * 16 : (group + 1) * 16]
                    rows = pl.ds(pl.multiple_of((part * GROUPS + group) * 16, 16), 16)
                    flux_ref[0, rows] = (first + both).astype(BF)
                    flux_ref[1, rows] = (first - both).astype(BF)
        return carry

    lax.fori_loop(0, PARTS, line, 0)
    for parity in range(2):
        half_ref[parity] = jnp.dot(flux_ref[parity], back_ref[parity], preferred_element_type=F32) * FACTOR
    for eight in range(LIVE // 8):
        quads = ([], [])
        for part in range(PARTS):
            rows, lanes = slice(part * 128, (part + 1) * 128), slice(eight * 128, (eight + 1) * 128)
            for rolled, block in zip(quads, even_odd(half_ref[0, rows, lanes].astype(BF), half_ref[1, rows, lanes].astype(BF))):
                rolled.append(pltpu.roll(block, 32 * part, 1) if part else block)
        for quad, rolled in enumerate(quads):
            for j in range(4):
                block = pick(masks, [rolled[(slot - j) % 4] for slot in range(4)]).astype(F32)
                for group in range(GROUPS):
                    at = (group * SLABS + eight * 8 + quad * 4 + j) * HOME
                    send_ref[at : at + HOME] = block[group * 16 : group * 16 + HOME]
    for group in range(GROUPS):
        at = (group * SLABS + LIVE) * HOME
        send_ref[at : at + (SLABS - LIVE) * HOME] = jnp.zeros(((SLABS - LIVE) * HOME, 128), F32)
    out_ref[...] = send_ref[...].astype(BF)


def update_kernel(
    in_ref, table_ref, re_ref, im_ref, base_re_ref, base_im_ref, new_re, new_im, wide_ref, left_ref, prod_ref, new_re_ref, new_im_ref, sems
):
    wide_ref[...] = in_ref[...].astype(F32)
    slab = lax.axis_index("grid")
    slots = slots_of(slab)
    for at in range(2 * OWN):
        block = wide_ref[pl.ds(at, DEVS, stride=HOME), :].T.astype(BF)
        for slot in range(PARTS):
            for c in range(2):
                row = (slot * 2 + c) * ROWS
                left_ref[slots[slot], at * ROWS : (at + 1) * ROWS, c * QUART : (c + 1) * QUART] = block[row : row + ROWS]
    for part in range(PARTS):
        prod_ref[part] = (
            jnp.dot(left_ref[part], table_ref[part], preferred_element_type=F32) * FACTOR
        )
    along_y, along_x = waves_of(slab * ROWS)
    wave_sq = along_y * along_y + along_x * along_x
    keep = (jnp.abs(along_x) * 3.0 < NG) & (along_y * 3.0 < NG)
    damping = VISCOSITY / (NG * NG) * wave_sq
    stores = []
    for mode in range(OWN):
        spectra = []
        for member in range(2):
            rows = slice((member * OWN + mode) * ROWS, (member * OWN + mode + 1) * ROWS)
            spectra.append(
                turn([(prod_ref[part, rows, :QUART], prod_ref[part, rows, QUART:]) for part in range(PARTS)], -1)
            )
        for p in range(4):
            lanes = slice(p * QUART, (p + 1) * QUART)
            (x_re, x_im), (y_re, y_im) = spectra[0][p], spectra[1][p]
            wx, wy = along_x[:, lanes], along_y[:, lanes]
            adv_re = jnp.where(keep[:, lanes], -(wx * x_im + wy * y_im), 0.0)
            adv_im = jnp.where(keep[:, lanes], wx * x_re + wy * y_re, 0.0)
            damp = damping[:, lanes]
            new_re_ref[mode, :, lanes] = base_re_ref[mode, :, lanes] + STEP_WEIGHT * (
                -adv_re - damp * re_ref[mode, :, lanes]
            )
            new_im_ref[mode, :, lanes] = base_im_ref[mode, :, lanes] + STEP_WEIGHT * (
                -adv_im - damp * im_ref[mode, :, lanes]
            )
        stores.append(pltpu.make_async_copy(new_re_ref.at[mode], new_re.at[mode], sems.at[2 * mode]))
        stores.append(pltpu.make_async_copy(new_im_ref.at[mode], new_im.at[mode], sems.at[2 * mode + 1]))
        stores[-2].start()
        stores[-1].start()
    for copy in stores:
        copy.wait()


def call(kernel, outs, scratch, specs, flops, limit=SMALL, space=pltpu.VMEM):
    return pl.pallas_call(
        kernel,
        out_shape=outs,
        in_specs=specs,
        out_specs=jax.tree.map(lambda _: pl.BlockSpec(memory_space=space), outs),
        scratch_shapes=scratch,
        cost_estimate=pl.CostEstimate(flops=flops, bytes_accessed=4 * 1024 * 1024, transcendentals=0),
        compiler_params=pltpu.CompilerParams(vmem_limit_bytes=limit),
    )


def exchange(array, count):
    blocks = array.reshape(DEVS, count // 2, 2, 128)
    blocks = lax.all_to_all(blocks, ("mode", "grid"), split_axis=0, concat_axis=0, tiled=True)
    return blocks.reshape(DEVS * count, 128)


def shards(omega_re, omega_im, base_re, base_im, triple):
    vmem = pl.BlockSpec(memory_space=pltpu.VMEM)
    hbm = pl.BlockSpec(memory_space=pltpu.HBM)
    count = 3 * OWN
    ahead_x, back_x = x_tables()
    ahead_y, back_y = y_tables()
    columns = call(
        columns_kernel,
        jax.ShapeDtypeStruct((DEVS * OUT, 128), BF),
        [
            pltpu.VMEM((OWN, ROWS, NG), F32),
            pltpu.VMEM((OWN, ROWS, NG), F32),
            pltpu.VMEM((PARTS, 2 * QUART, 2 * QUART), BF),
            pltpu.VMEM((PARTS, count * ROWS, 2 * QUART), BF),
            pltpu.VMEM((PARTS, count * ROWS, 2 * QUART), F32),
            pltpu.VMEM((DEVS // 2 * OUT, 128), F32),
            pltpu.VMEM((2, DEVS // 2 * OUT, 128), BF),
            pltpu.SemaphoreType.DMA((2 * OWN + PARTS + 2,)),
        ],
        [hbm, hbm, hbm],
        1_000_000_000,
        LARGE,
        pltpu.HBM,
    )(omega_re, omega_im, ahead_x)
    slab = exchange(columns, OUT)
    halves = call(
        points_kernel,
        jax.ShapeDtypeStruct((DEVS * HOME, 128), BF),
        [
            pltpu.VMEM((2, SLABS * OUT + 8, 128), F32),
            pltpu.VMEM((2, PARTS * 24 * GROUPS, KEPT), BF),
            pltpu.VMEM((PARTS * 24 * GROUPS, NG), F32),
            pltpu.VMEM((16 * GROUPS, HALF), F32),
            pltpu.VMEM((2, PARTS * 16 * GROUPS, HALF), BF),
            pltpu.VMEM((2, PARTS * 16 * GROUPS, LIVE * ROWS), F32),
            pltpu.VMEM((DEVS * HOME, 128), F32),
        ],
        [vmem] * 4,
        10_000_000_000,
    )(slab, ahead_y, triple.reshape(MODES * MODES, MODES), back_y)
    rows = exchange(halves, HOME)
    new = jax.ShapeDtypeStruct(base_re.shape, F32)
    return call(
        update_kernel,
        (new, new),
        [
            pltpu.VMEM((DEVS * HOME, 128), F32),
            pltpu.VMEM((PARTS, 2 * OWN * ROWS, 2 * QUART), BF),
            pltpu.VMEM((PARTS, 2 * OWN * ROWS, 2 * QUART), F32),
            pltpu.VMEM(base_re.shape, F32),
            pltpu.VMEM(base_re.shape, F32),
            pltpu.SemaphoreType.DMA((2 * OWN,)),
        ],
        [vmem] * 6,
        1_000_000_000,
        SMALL,
        pltpu.HBM,
    )(rows, back_x, omega_re, omega_im, base_re, base_im)


def solution(mesh):
    spec = P("mode", "grid", None)
    return jax.shard_map(
        shards, mesh=mesh, in_specs=(spec, spec, spec, spec, P()), out_specs=(spec, spec), check_vma=False
    )
```

```python
import functools
import math

import jax
import jax.numpy as jnp
import ml_dtypes
import numpy as np
from jax import lax
from jax.experimental import pallas as pl
from jax.experimental.pallas import tpu as pltpu
from jax.sharding import PartitionSpec as P

VISCOSITY = 4.0
STEP_WEIGHT = 0.5
NG = 1024
KEPT = 512
MODES = 56
GROUPS = 8
SLABS = 32
DEVS = GROUPS * SLABS
OWN = MODES // GROUPS
ROWS = KEPT // SLABS
HALF = NG // 2
PARTS = NG // DEVS
QUART = NG // 4
FACTOR = 1.0 / math.sqrt(NG)
OUT = 22
HOME = 2 * OWN
LIVE = 24
BF = jnp.bfloat16
F32 = jnp.float32
SMALL = 20 * 1024 * 1024
LARGE = 56 * 1024 * 1024


def circle(phases):
    angles = (phases % NG).astype(np.float32) * np.float32(2.0 * math.pi / NG)
    return np.cos(angles), np.sin(angles)


def scaled(table):
    return (table.astype(ml_dtypes.bfloat16).astype(np.float32) * np.float32(FACTOR)).astype(ml_dtypes.bfloat16)


def x_tables():
    ahead, back = [], []
    short = np.arange(QUART)
    for part in range(PARTS):
        points = PARTS * short + part
        cos, sin = circle(short[:, None] * points[None, :])
        ahead.append(np.block([[cos, sin]]))
        cos, sin = circle(points[:, None] * short[None, :])
        back.append(np.block([[cos, -sin], [sin, cos]]))
    return scaled(np.stack(ahead)), scaled(np.stack(back))


def y_tables():
    waves = np.arange(KEPT)
    cos, sin = circle(waves[:, None] * np.arange(HALF)[None, :])
    weights = np.where(waves == 0, 1.0, 2.0).astype(np.float32)[:, None]
    split = (SLABS // 8, 2, 4, ROWS // 2, 2, HALF)
    ahead = np.stack([(weights * cos).reshape(split), (-weights * sin).reshape(split)], axis=6)
    ahead = ahead.transpose(4, 0, 2, 6, 3, 1, 5).reshape(2, KEPT, HALF)
    back = np.stack([cos.reshape(split), -sin.reshape(split)], axis=6)[: LIVE // 8]
    back = back.transpose(4, 5, 0, 2, 6, 3, 1).reshape(2, HALF, LIVE * ROWS)
    return scaled(ahead), scaled(back)


def even_odd(first, second):
    lane = lax.broadcasted_iota(jnp.int32, first.shape, 1)
    return (
        jnp.where(lane % 2 == 0, first, pltpu.roll(second, 1, 1)),
        jnp.where(lane % 2 == 0, pltpu.roll(first, 127, 1), second),
    )


def lane_masks():
    group = lax.broadcasted_iota(jnp.int32, (1, 128), 1) // 32
    return [group == 0, group == 1, group == 2]


def pick(masks, sources):
    return jnp.where(
        masks[0], sources[0], jnp.where(masks[1], sources[1], jnp.where(masks[2], sources[2], sources[3]))
    )


def turn(parts, sign):
    (r0, i0), (r1, i1), (r2, i2), (r3, i3) = parts
    er, ei, fr, fi = r0 + r2, i0 + i2, r0 - r2, i0 - i2
    gr, gi, hr, hi = r1 + r3, i1 + i3, r1 - r3, i1 - i3
    if sign < 0:
        hr, hi = -hr, -hi
    return (
        (er + gr, ei + gi),
        (fr - hi, fi + hr),
        (er - gr, ei - gi),
        (fr + hi, fi - hr),
    )


def waves_of(first_row):
    along_y = (first_row + lax.broadcasted_iota(jnp.int32, (ROWS, NG), 0)).astype(F32)
    index = lax.broadcasted_iota(jnp.int32, (ROWS, NG), 1)
    along_x = jnp.where(index < NG // 2, index, index - NG).astype(F32)
    return along_y, along_x


def slots_of(shift):
    return [lax.rem(slot + PARTS - lax.rem(shift, PARTS), PARTS) for slot in range(PARTS)]


def columns_kernel(
    re_hbm, im_hbm, table_hbm, out_hbm, re_ref, im_ref, table_ref, left_ref, prod_ref, turn_ref, send_ref, sems
):
    loads = []
    for mode in range(OWN):
        loads.append(
            (
                pltpu.make_async_copy(re_hbm.at[mode], re_ref.at[mode], sems.at[2 * mode]),
                pltpu.make_async_copy(im_hbm.at[mode], im_ref.at[mode], sems.at[2 * mode + 1]),
            )
        )
    tables = [
        pltpu.make_async_copy(table_hbm.at[part], table_ref.at[part, pl.ds(0, QUART)], sems.at[2 * OWN + part])
        for part in range(PARTS)
    ]
    for pair in loads:
        pair[0].start()
        pair[1].start()
    for copy in tables:
        copy.start()
    count = 3 * OWN
    half = DEVS // 2
    for at in range(count, OUT):
        turn_ref[pl.ds(at, half, stride=OUT), :] = jnp.zeros((half, 128), F32)
    slab = lax.axis_index("grid")
    along_y, along_x = waves_of(slab * ROWS)
    wave_sq = along_y * along_y + along_x * along_x
    inverse = jnp.where(wave_sq > 0.5, 1.0 / jnp.maximum(wave_sq, 1.0), 0.0)
    scale_y = along_y * inverse
    scale_x = along_x * inverse
    for mode in range(OWN):
        loads[mode][0].wait()
        loads[mode][1].wait()
        w_re, w_im = re_ref[mode], im_ref[mode]
        fields = (
            (w_re, w_im),
            (-scale_y * w_im, scale_y * w_re),
            (scale_x * w_im, -scale_x * w_re),
        )
        for member, (f_re, f_im) in enumerate(fields):
            pieces = [
                (f_re[:, QUART * p : QUART * (p + 1)], f_im[:, QUART * p : QUART * (p + 1)])
                for p in range(4)
            ]
            at = (member * OWN + mode) * ROWS
            for part, (b_re, b_im) in enumerate(turn(pieces, 1)):
                left_ref[part, at : at + ROWS, :QUART] = b_re.astype(BF)
                left_ref[part, at : at + ROWS, QUART:] = b_im.astype(BF)
    for part in range(PARTS):
        tables[part].wait()
        table_ref[part, QUART:, :QUART] = -table_ref[part, :QUART, QUART:]
        table_ref[part, QUART:, QUART:] = table_ref[part, :QUART, :QUART]
        prod_ref[part] = jnp.dot(left_ref[part], table_ref[part], preferred_element_type=F32)
    slots = slots_of(slab)
    sends = []
    for side in range(2):
        for at in range(count):
            rows = slice(at * ROWS, (at + 1) * ROWS)
            block = jnp.concatenate(
                [
                    prod_ref[slots[slot], rows, c * QUART + side * half : c * QUART + (side + 1) * half]
                    for slot in range(PARTS)
                    for c in range(2)
                ],
                axis=0,
            )
            turn_ref[pl.ds(at, half, stride=OUT), :] = block.T
        send_ref[side] = turn_ref[: half * OUT].astype(BF)
        sends.append(
            pltpu.make_async_copy(
                send_ref.at[side], out_hbm.at[pl.ds(side * half * OUT, half * OUT)], sems.at[2 * OWN + PARTS + side]
            )
        )
        sends[side].start()
    for copy in sends:
        copy.wait()


def points_kernel(
    in_ref, ahead_ref, triple_ref, back_ref, out_ref, wide_ref, left_ref, phys_ref, keep_ref, flux_ref, half_ref, send_ref
):
    chunk = HALF
    tall = 24 * GROUPS
    masks = lane_masks()
    span = SLABS * OUT
    for side in range(2):
        wide_ref[side, span:] = jnp.zeros((16, 128), F32)

    def gather(pair, carry):
        for side in range(2):
            wide_ref[side, :span] = in_ref[pl.ds(pl.multiple_of((pair * 2 + side) * span, span), span)].astype(F32)
        for eight in range(SLABS // 8):
            quads = []
            for quad in (2 * eight, 2 * eight + 1):
                blocks = []
                for j in range(4):
                    at = (quad * 4 + j) * OUT
                    blocks.append(jnp.concatenate([wide_ref[side, at : at + 24] for side in range(2)], axis=0).astype(BF))
                quads.append(blocks)
            for part in range(PARTS):
                mixed = []
                for blocks in quads:
                    one = pick(masks, [blocks[(slot - part) % 4] for slot in range(4)])
                    mixed.append(pltpu.roll(one, 128 - 32 * part, 1) if part else one)
                rows = pl.ds(pl.multiple_of(part * tall + pair * 48, 48), 48)
                for parity, both in enumerate(even_odd(*mixed)):
                    left_ref[parity, rows, eight * 128 : (eight + 1) * 128] = both.astype(BF)
        return carry

    lax.fori_loop(0, GROUPS // 2, gather, 0, unroll=True)
    even = jnp.dot(left_ref[0], ahead_ref[0], preferred_element_type=F32)
    odd = jnp.dot(left_ref[1], ahead_ref[1], preferred_element_type=F32)
    phys_ref[:, :HALF] = even + odd
    phys_ref[:, HALF:] = even - odd

    def line(part, carry):
        base = pl.multiple_of(part * tall, tall)
        for step in range(NG // chunk):
            lanes = slice(step * chunk, (step + 1) * chunk)
            right = jnp.concatenate(
                [phys_ref[pl.ds(base + group * 24, 24), lanes][:OWN] for group in range(GROUPS)], axis=0
            ).astype(BF)
            sum_x = jnp.zeros((MODES, chunk), F32)
            sum_y = jnp.zeros((MODES, chunk), F32)
            for group in range(GROUPS):
                made = jnp.dot(
                    triple_ref[group * OWN * MODES : (group + 1) * OWN * MODES, :],
                    right,
                    preferred_element_type=F32,
                )
                vel = phys_ref[pl.ds(base + group * 24, 24), lanes]
                for mode in range(OWN):
                    block = made[mode * MODES : (mode + 1) * MODES]
                    sum_x = sum_x + block * vel[OWN + mode : OWN + mode + 1]
                    sum_y = sum_y + block * vel[2 * OWN + mode : 2 * OWN + mode + 1]
            for group in range(GROUPS):
                own = slice(group * OWN, (group + 1) * OWN)
                both = jnp.concatenate([sum_x[own], sum_y[own], jnp.zeros((2, chunk), F32)], axis=0)
                if step == 0:
                    keep_ref[group * 16 : (group + 1) * 16] = both
                else:
                    first = keep_ref[group * 16 : (group + 1) * 16]
                    rows = pl.ds(pl.multiple_of((part * GROUPS + group) * 16, 16), 16)
                    flux_ref[0, rows] = (first + both).astype(BF)
                    flux_ref[1, rows] = (first - both).astype(BF)
        return carry

    lax.fori_loop(0, PARTS, line, 0)
    for parity in range(2):
        half_ref[parity] = jnp.dot(flux_ref[parity], back_ref[parity], preferred_element_type=F32)
    for eight in range(LIVE // 8):
        quads = ([], [])
        for part in range(PARTS):
            rows, lanes = slice(part * 128, (part + 1) * 128), slice(eight * 128, (eight + 1) * 128)
            for rolled, block in zip(quads, even_odd(half_ref[0, rows, lanes].astype(BF), half_ref[1, rows, lanes].astype(BF))):
                rolled.append(pltpu.roll(block, 32 * part, 1) if part else block)
        for quad, rolled in enumerate(quads):
            for j in range(4):
                block = pick(masks, [rolled[(slot - j) % 4] for slot in range(4)]).astype(F32)
                for group in range(GROUPS):
                    at = (group * SLABS + eight * 8 + quad * 4 + j) * HOME
                    send_ref[at : at + HOME] = block[group * 16 : group * 16 + HOME]
    for group in range(GROUPS):
        at = (group * SLABS + LIVE) * HOME
        send_ref[at : at + (SLABS - LIVE) * HOME] = jnp.zeros(((SLABS - LIVE) * HOME, 128), F32)
    out_ref[...] = send_ref[: DEVS * HOME].astype(BF)


def update_kernel(
    in_ref, table_ref, re_ref, im_ref, base_re_ref, base_im_ref, new_re, new_im, wide_ref, left_ref, prod_ref, new_re_ref, new_im_ref, sems
):
    wide_ref[: DEVS * HOME] = in_ref[...].astype(F32)
    slab = lax.axis_index("grid")
    slots = slots_of(slab)
    for at in range(2 * OWN):
        block = wide_ref[pl.ds(at, DEVS, stride=HOME), :].astype(BF).T
        for slot in range(PARTS):
            for c in range(2):
                row = (slot * 2 + c) * ROWS
                left_ref[slots[slot], at * ROWS : (at + 1) * ROWS, c * QUART : (c + 1) * QUART] = block[row : row + ROWS]
    for part in range(PARTS):
        prod_ref[part] = jnp.dot(left_ref[part], table_ref[part], preferred_element_type=F32)
    along_y, along_x = waves_of(slab * ROWS)
    wave_sq = along_y * along_y + along_x * along_x
    keep = (jnp.abs(along_x) * 3.0 < NG) & (along_y * 3.0 < NG)
    damping = VISCOSITY / (NG * NG) * wave_sq
    stores = []
    for mode in range(OWN):
        spectra = []
        for member in range(2):
            rows = slice((member * OWN + mode) * ROWS, (member * OWN + mode + 1) * ROWS)
            spectra.append(
                turn([(prod_ref[part, rows, :QUART], prod_ref[part, rows, QUART:]) for part in range(PARTS)], -1)
            )
        for p in range(4):
            lanes = slice(p * QUART, (p + 1) * QUART)
            (x_re, x_im), (y_re, y_im) = spectra[0][p], spectra[1][p]
            wx, wy = along_x[:, lanes], along_y[:, lanes]
            adv_re = jnp.where(keep[:, lanes], -(wx * x_im + wy * y_im), 0.0)
            adv_im = jnp.where(keep[:, lanes], wx * x_re + wy * y_re, 0.0)
            damp = damping[:, lanes]
            new_re_ref[mode, :, lanes] = base_re_ref[mode, :, lanes] + STEP_WEIGHT * (
                -adv_re - damp * re_ref[mode, :, lanes]
            )
            new_im_ref[mode, :, lanes] = base_im_ref[mode, :, lanes] + STEP_WEIGHT * (
                -adv_im - damp * im_ref[mode, :, lanes]
            )
        stores.append(pltpu.make_async_copy(new_re_ref.at[mode], new_re.at[mode], sems.at[2 * mode]))
        stores.append(pltpu.make_async_copy(new_im_ref.at[mode], new_im.at[mode], sems.at[2 * mode + 1]))
        stores[-2].start()
        stores[-1].start()
    for copy in stores:
        copy.wait()


def call(kernel, outs, scratch, specs, flops, limit=SMALL, space=pltpu.VMEM):
    return pl.pallas_call(
        kernel,
        out_shape=outs,
        in_specs=specs,
        out_specs=jax.tree.map(lambda _: pl.BlockSpec(memory_space=space), outs),
        scratch_shapes=scratch,
        cost_estimate=pl.CostEstimate(flops=flops, bytes_accessed=4 * 1024 * 1024, transcendentals=0),
        compiler_params=pltpu.CompilerParams(vmem_limit_bytes=limit),
    )


def exchange(array, count):
    blocks = array.reshape(DEVS, count // 2, 2, 128)
    blocks = lax.all_to_all(blocks, ("mode", "grid"), split_axis=0, concat_axis=0, tiled=True)
    return blocks.reshape(DEVS * count, 128)


def shards(omega_re, omega_im, base_re, base_im, triple):
    vmem = pl.BlockSpec(memory_space=pltpu.VMEM)
    hbm = pl.BlockSpec(memory_space=pltpu.HBM)
    count = 3 * OWN
    ahead_x, back_x = x_tables()
    ahead_y, back_y = y_tables()
    columns = call(
        columns_kernel,
        jax.ShapeDtypeStruct((DEVS * OUT, 128), BF),
        [
            pltpu.VMEM((OWN, ROWS, NG), F32),
            pltpu.VMEM((OWN, ROWS, NG), F32),
            pltpu.VMEM((PARTS, 2 * QUART, 2 * QUART), BF),
            pltpu.VMEM((PARTS, count * ROWS, 2 * QUART), BF),
            pltpu.VMEM((PARTS, count * ROWS, 2 * QUART), F32),
            pltpu.VMEM((DEVS // 2 * OUT + 32, 128), F32),
            pltpu.VMEM((2, DEVS // 2 * OUT, 128), BF),
            pltpu.SemaphoreType.DMA((2 * OWN + PARTS + 2,)),
        ],
        [hbm, hbm, hbm],
        1_000_000_000,
        LARGE,
        pltpu.HBM,
    )(omega_re, omega_im, ahead_x)
    slab = exchange(columns, OUT)
    halves = call(
        points_kernel,
        jax.ShapeDtypeStruct((DEVS * HOME, 128), BF),
        [
            pltpu.VMEM((2, SLABS * OUT + 16, 128), F32),
            pltpu.VMEM((2, PARTS * 24 * GROUPS, KEPT), BF),
            pltpu.VMEM((PARTS * 24 * GROUPS, NG), F32),
            pltpu.VMEM((16 * GROUPS, HALF), F32),
            pltpu.VMEM((2, PARTS * 16 * GROUPS, HALF), BF),
            pltpu.VMEM((2, PARTS * 16 * GROUPS, LIVE * ROWS), F32),
            pltpu.VMEM((DEVS * HOME + 16, 128), F32),
        ],
        [vmem] * 4,
        10_000_000_000,
    )(slab, ahead_y, triple.reshape(MODES * MODES, MODES), back_y)
    rows = exchange(halves, HOME)
    new = jax.ShapeDtypeStruct(base_re.shape, F32)
    return call(
        update_kernel,
        (new, new),
        [
            pltpu.VMEM((DEVS * HOME + 16, 128), F32),
            pltpu.VMEM((PARTS, 2 * OWN * ROWS, 2 * QUART), BF),
            pltpu.VMEM((PARTS, 2 * OWN * ROWS, 2 * QUART), F32),
            pltpu.VMEM(base_re.shape, F32),
            pltpu.VMEM(base_re.shape, F32),
            pltpu.SemaphoreType.DMA((2 * OWN,)),
        ],
        [vmem] * 6,
        1_000_000_000,
        SMALL,
        pltpu.HBM,
    )(rows, back_x, omega_re, omega_im, base_re, base_im)


def solution(mesh):
    spec = P("mode", "grid", None)
    return jax.shard_map(
        shards, mesh=mesh, in_specs=(spec, spec, spec, spec, P()), out_specs=(spec, spec), check_vma=False
    )
```

```python
import functools
import math

import jax
import jax.numpy as jnp
import ml_dtypes
import numpy as np
from jax import lax
from jax.experimental import pallas as pl
from jax.experimental.pallas import tpu as pltpu
from jax.sharding import PartitionSpec as P

VISCOSITY = 4.0
STEP_WEIGHT = 0.5
NG = 1024
KEPT = 512
MODES = 56
GROUPS = 8
SLABS = 32
DEVS = GROUPS * SLABS
OWN = MODES // GROUPS
ROWS = KEPT // SLABS
HALF = NG // 2
PARTS = NG // DEVS
QUART = NG // 4
FACTOR = 1.0 / math.sqrt(NG)
OUT = 22
HOME = 2 * OWN
LIVE = 24
BF = jnp.bfloat16
F32 = jnp.float32
SMALL = 20 * 1024 * 1024
LARGE = 56 * 1024 * 1024


def circle(phases):
    angles = (phases % NG).astype(np.float32) * np.float32(2.0 * math.pi / NG)
    return np.cos(angles), np.sin(angles)


def scaled(table):
    return (table.astype(ml_dtypes.bfloat16).astype(np.float32) * np.float32(FACTOR)).astype(ml_dtypes.bfloat16)


def x_tables():
    ahead, back = [], []
    short = np.arange(QUART)
    for part in range(PARTS):
        points = PARTS * short + part
        cos, sin = circle(short[:, None] * points[None, :])
        ahead.append(np.block([[cos, sin]]))
        cos, sin = circle(points[:, None] * short[None, :])
        back.append(np.block([[cos, -sin], [sin, cos]]))
    return scaled(np.stack(ahead)), scaled(np.stack(back))


def y_tables():
    waves = np.arange(KEPT)
    cos, sin = circle(waves[:, None] * np.arange(HALF)[None, :])
    weights = np.where(waves == 0, 1.0, 2.0).astype(np.float32)[:, None]
    split = (SLABS // 8, 2, 4, ROWS // 2, 2, HALF)
    ahead = np.stack([(weights * cos).reshape(split), (-weights * sin).reshape(split)], axis=6)
    ahead = ahead.transpose(4, 0, 2, 6, 3, 1, 5).reshape(2, KEPT, HALF)
    back = np.stack([cos.reshape(split), -sin.reshape(split)], axis=6)[: LIVE // 8]
    back = back.transpose(4, 5, 0, 2, 6, 3, 1).reshape(2, HALF, LIVE * ROWS)
    return scaled(ahead), scaled(back)


def even_odd(first, second):
    lane = lax.broadcasted_iota(jnp.int32, first.shape, 1)
    return (
        jnp.where(lane % 2 == 0, first, pltpu.roll(second, 1, 1)),
        jnp.where(lane % 2 == 0, pltpu.roll(first, 127, 1), second),
    )


def lane_masks():
    group = lax.broadcasted_iota(jnp.int32, (1, 128), 1) // 32
    return [group == 0, group == 1, group == 2]


def pick(masks, sources):
    return jnp.where(
        masks[0], sources[0], jnp.where(masks[1], sources[1], jnp.where(masks[2], sources[2], sources[3]))
    )


def turn(parts, sign):
    (r0, i0), (r1, i1), (r2, i2), (r3, i3) = parts
    er, ei, fr, fi = r0 + r2, i0 + i2, r0 - r2, i0 - i2
    gr, gi, hr, hi = r1 + r3, i1 + i3, r1 - r3, i1 - i3
    if sign < 0:
        hr, hi = -hr, -hi
    return (
        (er + gr, ei + gi),
        (fr - hi, fi + hr),
        (er - gr, ei - gi),
        (fr + hi, fi - hr),
    )


def waves_of(first_row):
    along_y = (first_row + lax.broadcasted_iota(jnp.int32, (ROWS, NG), 0)).astype(F32)
    index = lax.broadcasted_iota(jnp.int32, (ROWS, NG), 1)
    along_x = jnp.where(index < NG // 2, index, index - NG).astype(F32)
    return along_y, along_x


def slots_of(shift):
    return [lax.rem(slot + PARTS - lax.rem(shift, PARTS), PARTS) for slot in range(PARTS)]


def columns_kernel(
    re_hbm, im_hbm, table_hbm, out_hbm, re_ref, im_ref, table_ref, left_ref, prod_ref, turn_ref, send_ref, sems
):
    loads = []
    for mode in range(OWN):
        loads.append(
            (
                pltpu.make_async_copy(re_hbm.at[mode], re_ref.at[mode], sems.at[2 * mode]),
                pltpu.make_async_copy(im_hbm.at[mode], im_ref.at[mode], sems.at[2 * mode + 1]),
            )
        )
    tables = [
        pltpu.make_async_copy(table_hbm.at[part], table_ref.at[part, pl.ds(0, QUART)], sems.at[2 * OWN + part])
        for part in range(PARTS)
    ]
    for pair in loads:
        pair[0].start()
        pair[1].start()
    for copy in tables:
        copy.start()
    count = 3 * OWN
    half = DEVS // 2
    for at in range(count, OUT):
        turn_ref[pl.ds(at, half, stride=OUT), :] = jnp.zeros((half, 128), F32)
    slab = lax.axis_index("grid")
    along_y, along_x = waves_of(slab * ROWS)
    wave_sq = along_y * along_y + along_x * along_x
    inverse = jnp.where(wave_sq > 0.5, 1.0 / jnp.maximum(wave_sq, 1.0), 0.0)
    scale_y = along_y * inverse
    scale_x = along_x * inverse
    for mode in range(OWN):
        loads[mode][0].wait()
        loads[mode][1].wait()
        w_re, w_im = re_ref[mode], im_ref[mode]
        fields = (
            (w_re, w_im),
            (-scale_y * w_im, scale_y * w_re),
            (scale_x * w_im, -scale_x * w_re),
        )
        for member, (f_re, f_im) in enumerate(fields):
            pieces = [
                (f_re[:, QUART * p : QUART * (p + 1)], f_im[:, QUART * p : QUART * (p + 1)])
                for p in range(4)
            ]
            at = (member * OWN + mode) * ROWS
            for part, (b_re, b_im) in enumerate(turn(pieces, 1)):
                left_ref[part, at : at + ROWS, :QUART] = b_re.astype(BF)
                left_ref[part, at : at + ROWS, QUART:] = b_im.astype(BF)
    for part in range(PARTS):
        tables[part].wait()
        table_ref[part, QUART:, :QUART] = -table_ref[part, :QUART, QUART:]
        table_ref[part, QUART:, QUART:] = table_ref[part, :QUART, :QUART]
    slots = slots_of(slab)
    sends = []
    for side in range(2):
        for part in range(PARTS):
            own = jnp.concatenate(
                [table_ref[part, :, c * QUART + side * half : c * QUART + (side + 1) * half] for c in range(2)], axis=1
            )
            prod_ref[side, part] = jnp.dot(left_ref[part], own, preferred_element_type=F32)
        for at in range(count):
            rows = slice(at * ROWS, (at + 1) * ROWS)
            block = jnp.concatenate(
                [
                    prod_ref[side, slots[slot], rows, c * half : (c + 1) * half]
                    for slot in range(PARTS)
                    for c in range(2)
                ],
                axis=0,
            )
            turn_ref[pl.ds(at, half, stride=OUT), :] = block.astype(BF).T.astype(F32)
        send_ref[side] = turn_ref[: half * OUT].astype(BF)
        sends.append(
            pltpu.make_async_copy(
                send_ref.at[side], out_hbm.at[pl.ds(side * half * OUT, half * OUT)], sems.at[2 * OWN + PARTS + side]
            )
        )
        sends[side].start()
    for copy in sends:
        copy.wait()


def points_kernel(
    in_ref, ahead_ref, triple_ref, back_ref, out_ref, wide_ref, left_ref, phys_ref, keep_ref, flux_ref, half_ref, send_ref
):
    chunk = HALF
    tall = 24 * GROUPS
    masks = lane_masks()
    span = SLABS * OUT
    for side in range(2):
        wide_ref[side, span:] = jnp.zeros((16, 128), F32)

    def gather(pair, carry):
        for side in range(2):
            wide_ref[side, :span] = in_ref[pl.ds(pl.multiple_of((pair * 2 + side) * span, span), span)].astype(F32)
        for eight in range(SLABS // 8):
            quads = []
            for quad in (2 * eight, 2 * eight + 1):
                blocks = []
                for j in range(4):
                    at = (quad * 4 + j) * OUT
                    blocks.append(jnp.concatenate([wide_ref[side, at : at + 24] for side in range(2)], axis=0).astype(BF))
                quads.append(blocks)
            for part in range(PARTS):
                mixed = []
                for blocks in quads:
                    one = pick(masks, [blocks[(slot - part) % 4] for slot in range(4)])
                    mixed.append(pltpu.roll(one, 128 - 32 * part, 1) if part else one)
                rows = pl.ds(pl.multiple_of(part * tall + pair * 48, 48), 48)
                for parity, both in enumerate(even_odd(*mixed)):
                    left_ref[parity, rows, eight * 128 : (eight + 1) * 128] = both.astype(BF)
        return carry

    lax.fori_loop(0, GROUPS // 2, gather, 0, unroll=True)
    even = jnp.dot(left_ref[0], ahead_ref[0], preferred_element_type=F32)
    odd = jnp.dot(left_ref[1], ahead_ref[1], preferred_element_type=F32)
    phys_ref[:, :HALF] = even + odd
    phys_ref[:, HALF:] = even - odd

    def line(part, carry):
        base = pl.multiple_of(part * tall, tall)
        for step in range(NG // chunk):
            lanes = slice(step * chunk, (step + 1) * chunk)
            right = jnp.concatenate(
                [phys_ref[pl.ds(base + group * 24, 24), lanes][:OWN] for group in range(GROUPS)], axis=0
            ).astype(BF)
            sum_x = jnp.zeros((MODES, chunk), F32)
            sum_y = jnp.zeros((MODES, chunk), F32)
            for group in range(GROUPS):
                made = jnp.dot(
                    triple_ref[group * OWN * MODES : (group + 1) * OWN * MODES, :],
                    right,
                    preferred_element_type=F32,
                )
                vel = phys_ref[pl.ds(base + group * 24, 24), lanes]
                for mode in range(OWN):
                    block = made[mode * MODES : (mode + 1) * MODES]
                    sum_x = sum_x + block * vel[OWN + mode : OWN + mode + 1]
                    sum_y = sum_y + block * vel[2 * OWN + mode : 2 * OWN + mode + 1]
            for group in range(GROUPS):
                own = slice(group * OWN, (group + 1) * OWN)
                both = jnp.concatenate([sum_x[own], sum_y[own], jnp.zeros((2, chunk), F32)], axis=0)
                if step == 0:
                    keep_ref[group * 16 : (group + 1) * 16] = both
                else:
                    first = keep_ref[group * 16 : (group + 1) * 16]
                    rows = pl.ds(pl.multiple_of((part * GROUPS + group) * 16, 16), 16)
                    flux_ref[0, rows] = (first + both).astype(BF)
                    flux_ref[1, rows] = (first - both).astype(BF)
        return carry

    lax.fori_loop(0, PARTS, line, 0)
    for parity in range(2):
        half_ref[parity] = jnp.dot(flux_ref[parity], back_ref[parity], preferred_element_type=F32)
    for eight in range(LIVE // 8):
        quads = ([], [])
        for part in range(PARTS):
            rows, lanes = slice(part * 128, (part + 1) * 128), slice(eight * 128, (eight + 1) * 128)
            for rolled, block in zip(quads, even_odd(half_ref[0, rows, lanes].astype(BF), half_ref[1, rows, lanes].astype(BF))):
                rolled.append(pltpu.roll(block, 32 * part, 1) if part else block)
        for quad, rolled in enumerate(quads):
            for j in range(4):
                block = pick(masks, [rolled[(slot - j) % 4] for slot in range(4)]).astype(F32)
                for group in range(GROUPS):
                    at = (group * SLABS + eight * 8 + quad * 4 + j) * HOME
                    send_ref[at : at + HOME] = block[group * 16 : group * 16 + HOME]
    for group in range(GROUPS):
        at = (group * SLABS + LIVE) * HOME
        send_ref[at : at + (SLABS - LIVE) * HOME] = jnp.zeros(((SLABS - LIVE) * HOME, 128), F32)
    out_ref[...] = send_ref[: DEVS * HOME].astype(BF)


def update_kernel(
    in_ref, table_ref, re_ref, im_ref, base_re_ref, base_im_ref, new_re, new_im, wide_ref, left_ref, prod_ref, new_re_ref, new_im_ref, sems
):
    wide_ref[: DEVS * HOME] = in_ref[...].astype(F32)
    slab = lax.axis_index("grid")
    slots = slots_of(slab)
    for at in range(2 * OWN):
        block = wide_ref[pl.ds(at, DEVS, stride=HOME), :].astype(BF).T
        for slot in range(PARTS):
            for c in range(2):
                row = (slot * 2 + c) * ROWS
                left_ref[slots[slot], at * ROWS : (at + 1) * ROWS, c * QUART : (c + 1) * QUART] = block[row : row + ROWS]
    for part in range(PARTS):
        prod_ref[part] = jnp.dot(left_ref[part], table_ref[part], preferred_element_type=F32)
    along_y, along_x = waves_of(slab * ROWS)
    wave_sq = along_y * along_y + along_x * along_x
    keep = (jnp.abs(along_x) * 3.0 < NG) & (along_y * 3.0 < NG)
    damping = VISCOSITY / (NG * NG) * wave_sq
    stores = []
    for mode in range(OWN):
        spectra = []
        for member in range(2):
            rows = slice((member * OWN + mode) * ROWS, (member * OWN + mode + 1) * ROWS)
            spectra.append(
                turn([(prod_ref[part, rows, :QUART], prod_ref[part, rows, QUART:]) for part in range(PARTS)], -1)
            )
        for p in range(4):
            lanes = slice(p * QUART, (p + 1) * QUART)
            (x_re, x_im), (y_re, y_im) = spectra[0][p], spectra[1][p]
            wx, wy = along_x[:, lanes], along_y[:, lanes]
            adv_re = jnp.where(keep[:, lanes], -(wx * x_im + wy * y_im), 0.0)
            adv_im = jnp.where(keep[:, lanes], wx * x_re + wy * y_re, 0.0)
            damp = damping[:, lanes]
            new_re_ref[mode, :, lanes] = base_re_ref[mode, :, lanes] + STEP_WEIGHT * (
                -adv_re - damp * re_ref[mode, :, lanes]
            )
            new_im_ref[mode, :, lanes] = base_im_ref[mode, :, lanes] + STEP_WEIGHT * (
                -adv_im - damp * im_ref[mode, :, lanes]
            )
        stores.append(pltpu.make_async_copy(new_re_ref.at[mode], new_re.at[mode], sems.at[2 * mode]))
        stores.append(pltpu.make_async_copy(new_im_ref.at[mode], new_im.at[mode], sems.at[2 * mode + 1]))
        stores[-2].start()
        stores[-1].start()
    for copy in stores:
        copy.wait()


def call(kernel, outs, scratch, specs, flops, limit=SMALL, space=pltpu.VMEM):
    return pl.pallas_call(
        kernel,
        out_shape=outs,
        in_specs=specs,
        out_specs=jax.tree.map(lambda _: pl.BlockSpec(memory_space=space), outs),
        scratch_shapes=scratch,
        cost_estimate=pl.CostEstimate(flops=flops, bytes_accessed=4 * 1024 * 1024, transcendentals=0),
        compiler_params=pltpu.CompilerParams(vmem_limit_bytes=limit),
    )


def exchange(array, count):
    blocks = array.reshape(DEVS, count // 2, 2, 128)
    blocks = lax.all_to_all(blocks, ("mode", "grid"), split_axis=0, concat_axis=0, tiled=True)
    return blocks.reshape(DEVS * count, 128)


def shards(omega_re, omega_im, base_re, base_im, triple):
    vmem = pl.BlockSpec(memory_space=pltpu.VMEM)
    hbm = pl.BlockSpec(memory_space=pltpu.HBM)
    count = 3 * OWN
    ahead_x, back_x = x_tables()
    ahead_y, back_y = y_tables()
    columns = call(
        columns_kernel,
        jax.ShapeDtypeStruct((DEVS * OUT, 128), BF),
        [
            pltpu.VMEM((OWN, ROWS, NG), F32),
            pltpu.VMEM((OWN, ROWS, NG), F32),
            pltpu.VMEM((PARTS, 2 * QUART, 2 * QUART), BF),
            pltpu.VMEM((PARTS, count * ROWS, 2 * QUART), BF),
            pltpu.VMEM((2, PARTS, count * ROWS, QUART), F32),
            pltpu.VMEM((DEVS // 2 * OUT + 32, 128), F32),
            pltpu.VMEM((2, DEVS // 2 * OUT, 128), BF),
            pltpu.SemaphoreType.DMA((2 * OWN + PARTS + 2,)),
        ],
        [hbm, hbm, hbm],
        1_000_000_000,
        LARGE,
        pltpu.HBM,
    )(omega_re, omega_im, ahead_x)
    slab = exchange(columns, OUT)
    halves = call(
        points_kernel,
        jax.ShapeDtypeStruct((DEVS * HOME, 128), BF),
        [
            pltpu.VMEM((2, SLABS * OUT + 16, 128), F32),
            pltpu.VMEM((2, PARTS * 24 * GROUPS, KEPT), BF),
            pltpu.VMEM((PARTS * 24 * GROUPS, NG), F32),
            pltpu.VMEM((16 * GROUPS, HALF), F32),
            pltpu.VMEM((2, PARTS * 16 * GROUPS, HALF), BF),
            pltpu.VMEM((2, PARTS * 16 * GROUPS, LIVE * ROWS), F32),
            pltpu.VMEM((DEVS * HOME + 16, 128), F32),
        ],
        [vmem] * 4,
        10_000_000_000,
    )(slab, ahead_y, triple.reshape(MODES * MODES, MODES), back_y)
    rows = exchange(halves, HOME)
    new = jax.ShapeDtypeStruct(base_re.shape, F32)
    return call(
        update_kernel,
        (new, new),
        [
            pltpu.VMEM((DEVS * HOME + 16, 128), F32),
            pltpu.VMEM((PARTS, 2 * OWN * ROWS, 2 * QUART), BF),
            pltpu.VMEM((PARTS, 2 * OWN * ROWS, 2 * QUART), F32),
            pltpu.VMEM(base_re.shape, F32),
            pltpu.VMEM(base_re.shape, F32),
            pltpu.SemaphoreType.DMA((2 * OWN,)),
        ],
        [vmem] * 6,
        1_000_000_000,
        SMALL,
        pltpu.HBM,
    )(rows, back_x, omega_re, omega_im, base_re, base_im)


def solution(mesh):
    spec = P("mode", "grid", None)
    return jax.shard_map(
        shards, mesh=mesh, in_specs=(spec, spec, spec, spec, P()), out_specs=(spec, spec), check_vma=False
    )
```

```python
import functools
import math

import jax
import jax.numpy as jnp
import ml_dtypes
import numpy as np
from jax import lax
from jax.experimental import pallas as pl
from jax.experimental.pallas import tpu as pltpu
from jax.sharding import PartitionSpec as P

VISCOSITY = 4.0
STEP_WEIGHT = 0.5
NG = 1024
KEPT = 512
MODES = 56
GROUPS = 8
SLABS = 32
DEVS = GROUPS * SLABS
OWN = MODES // GROUPS
ROWS = KEPT // SLABS
HALF = NG // 2
PARTS = NG // DEVS
QUART = NG // 4
FACTOR = 1.0 / math.sqrt(NG)
OUT = 22
HOME = 2 * OWN
LIVE = 24
BF = jnp.bfloat16
F32 = jnp.float32
SMALL = 20 * 1024 * 1024
LARGE = 56 * 1024 * 1024


def circle(phases):
    angles = (phases % NG).astype(np.float32) * np.float32(2.0 * math.pi / NG)
    return np.cos(angles), np.sin(angles)


def scaled(table):
    return (table.astype(ml_dtypes.bfloat16).astype(np.float32) * np.float32(FACTOR)).astype(ml_dtypes.bfloat16)


def x_tables():
    ahead, back = [], []
    short = np.arange(QUART)
    for part in range(PARTS):
        points = PARTS * short + part
        cos, sin = circle(short[:, None] * points[None, :])
        ahead.append(np.block([[cos, sin]]))
        cos, sin = circle(points[:, None] * short[None, :])
        back.append(np.block([[cos, -sin], [sin, cos]]))
    return scaled(np.stack(ahead)), scaled(np.stack(back))


def y_tables():
    waves = np.arange(KEPT)
    cos, sin = circle(waves[:, None] * np.arange(HALF)[None, :])
    weights = np.where(waves == 0, 1.0, 2.0).astype(np.float32)[:, None]
    split = (SLABS // 8, 2, 4, ROWS // 2, 2, HALF)
    ahead = np.stack([(weights * cos).reshape(split), (-weights * sin).reshape(split)], axis=6)
    ahead = ahead.transpose(4, 0, 2, 6, 3, 1, 5).reshape(2, KEPT, HALF)
    back = np.stack([cos.reshape(split), -sin.reshape(split)], axis=6)[: LIVE // 8]
    back = back.transpose(4, 5, 0, 2, 6, 3, 1).reshape(2, HALF, LIVE * ROWS)
    return scaled(ahead), scaled(back)


def even_odd(first, second):
    lane = lax.broadcasted_iota(jnp.int32, first.shape, 1)
    return (
        jnp.where(lane % 2 == 0, first, pltpu.roll(second, 1, 1)),
        jnp.where(lane % 2 == 0, pltpu.roll(first, 127, 1), second),
    )


def lane_masks():
    group = lax.broadcasted_iota(jnp.int32, (1, 128), 1) // 32
    return [group == 0, group == 1, group == 2]


def pick(masks, sources):
    return jnp.where(
        masks[0], sources[0], jnp.where(masks[1], sources[1], jnp.where(masks[2], sources[2], sources[3]))
    )


def turn(parts, sign):
    (r0, i0), (r1, i1), (r2, i2), (r3, i3) = parts
    er, ei, fr, fi = r0 + r2, i0 + i2, r0 - r2, i0 - i2
    gr, gi, hr, hi = r1 + r3, i1 + i3, r1 - r3, i1 - i3
    if sign < 0:
        hr, hi = -hr, -hi
    return (
        (er + gr, ei + gi),
        (fr - hi, fi + hr),
        (er - gr, ei - gi),
        (fr + hi, fi - hr),
    )


def waves_of(first_row):
    along_y = (first_row + lax.broadcasted_iota(jnp.int32, (ROWS, NG), 0)).astype(F32)
    index = lax.broadcasted_iota(jnp.int32, (ROWS, NG), 1)
    along_x = jnp.where(index < NG // 2, index, index - NG).astype(F32)
    return along_y, along_x


def slots_of(shift):
    return [lax.rem(slot + PARTS - lax.rem(shift, PARTS), PARTS) for slot in range(PARTS)]


def columns_kernel(
    re_hbm, im_hbm, table_hbm, out_hbm, re_ref, im_ref, table_ref, left_ref, prod_ref, turn_ref, send_ref, sems
):
    loads = []
    for mode in range(OWN):
        loads.append(
            (
                pltpu.make_async_copy(re_hbm.at[mode], re_ref.at[mode], sems.at[2 * mode]),
                pltpu.make_async_copy(im_hbm.at[mode], im_ref.at[mode], sems.at[2 * mode + 1]),
            )
        )
    tables = [
        pltpu.make_async_copy(table_hbm.at[part], table_ref.at[part, pl.ds(0, QUART)], sems.at[2 * OWN + part])
        for part in range(PARTS)
    ]
    for pair in loads:
        pair[0].start()
        pair[1].start()
    for copy in tables:
        copy.start()
    count = 3 * OWN
    half = DEVS // 2
    for at in range(count, OUT):
        turn_ref[pl.ds(at, half, stride=OUT), :] = jnp.zeros((half, 128), F32)
    slab = lax.axis_index("grid")
    along_y, along_x = waves_of(slab * ROWS)
    wave_sq = along_y * along_y + along_x * along_x
    inverse = jnp.where(wave_sq > 0.5, 1.0 / jnp.maximum(wave_sq, 1.0), 0.0)
    scale_y = along_y * inverse
    scale_x = along_x * inverse
    for mode in range(OWN):
        loads[mode][0].wait()
        loads[mode][1].wait()
        w_re, w_im = re_ref[mode], im_ref[mode]
        fields = (
            (w_re, w_im),
            (-scale_y * w_im, scale_y * w_re),
            (scale_x * w_im, -scale_x * w_re),
        )
        for member, (f_re, f_im) in enumerate(fields):
            pieces = [
                (f_re[:, QUART * p : QUART * (p + 1)], f_im[:, QUART * p : QUART * (p + 1)])
                for p in range(4)
            ]
            at = (member * OWN + mode) * ROWS
            for part, (b_re, b_im) in enumerate(turn(pieces, 1)):
                left_ref[part, at : at + ROWS, :QUART] = b_re.astype(BF)
                left_ref[part, at : at + ROWS, QUART:] = b_im.astype(BF)
    for part in range(PARTS):
        tables[part].wait()
        table_ref[part, QUART:, :QUART] = -table_ref[part, :QUART, QUART:]
        table_ref[part, QUART:, QUART:] = table_ref[part, :QUART, :QUART]
    slots = slots_of(slab)
    sends = []
    for side in range(2):
        for part in range(PARTS):
            own = jnp.concatenate(
                [table_ref[part, :, c * QUART + side * half : c * QUART + (side + 1) * half] for c in range(2)], axis=1
            )
            prod_ref[side, part] = jnp.dot(left_ref[part], own, preferred_element_type=F32)
        for at in range(count):
            rows = slice(at * ROWS, (at + 1) * ROWS)
            block = jnp.concatenate(
                [
                    prod_ref[side, slots[slot], rows, c * half : (c + 1) * half]
                    for slot in range(PARTS)
                    for c in range(2)
                ],
                axis=0,
            )
            turn_ref[pl.ds(at, half, stride=OUT), :] = block.astype(BF).T.astype(F32)
        send_ref[side] = turn_ref[: half * OUT].astype(BF)
        sends.append(
            pltpu.make_async_copy(
                send_ref.at[side], out_hbm.at[pl.ds(side * half * OUT, half * OUT)], sems.at[2 * OWN + PARTS + side]
            )
        )
        sends[side].start()
    for copy in sends:
        copy.wait()


def points_kernel(
    in_ref, ahead_ref, triple_ref, back_ref, out_ref, left_ref, phys_ref, keep_ref, flux_ref, half_ref
):
    chunk = HALF
    tall = 24 * GROUPS
    masks = lane_masks()
    span = SLABS * OUT

    def gather(pair, carry):
        held = [in_ref[pl.ds(pl.multiple_of((pair * 2 + side) * span, span), span)] for side in range(2)]
        nothing = jnp.zeros((24 - OUT, 128), BF)
        for eight in range(SLABS // 8):
            quads = []
            for quad in (2 * eight, 2 * eight + 1):
                blocks = []
                for j in range(4):
                    at = (quad * 4 + j) * OUT
                    blocks.append(jnp.concatenate([held[0][at : at + OUT], nothing, held[1][at : at + OUT], nothing], axis=0))
                quads.append(blocks)
            for part in range(PARTS):
                mixed = []
                for blocks in quads:
                    one = pick(masks, [blocks[(slot - part) % 4] for slot in range(4)])
                    mixed.append(pltpu.roll(one, 128 - 32 * part, 1) if part else one)
                rows = pl.ds(pl.multiple_of(part * tall + pair * 48, 48), 48)
                for parity, both in enumerate(even_odd(*mixed)):
                    left_ref[parity, rows, eight * 128 : (eight + 1) * 128] = both.astype(BF)
        return carry

    lax.fori_loop(0, GROUPS // 2, gather, 0, unroll=True)
    even = jnp.dot(left_ref[0], ahead_ref[0], preferred_element_type=F32)
    odd = jnp.dot(left_ref[1], ahead_ref[1], preferred_element_type=F32)
    phys_ref[:, :HALF] = even + odd
    phys_ref[:, HALF:] = even - odd

    def line(part, carry):
        base = pl.multiple_of(part * tall, tall)
        for step in range(NG // chunk):
            lanes = slice(step * chunk, (step + 1) * chunk)
            right = jnp.concatenate(
                [phys_ref[pl.ds(base + group * 24, 24), lanes][:OWN] for group in range(GROUPS)], axis=0
            ).astype(BF)
            sum_x = jnp.zeros((MODES, chunk), F32)
            sum_y = jnp.zeros((MODES, chunk), F32)
            for group in range(GROUPS):
                made = jnp.dot(
                    triple_ref[group * OWN * MODES : (group + 1) * OWN * MODES, :],
                    right,
                    preferred_element_type=F32,
                )
                vel = phys_ref[pl.ds(base + group * 24, 24), lanes]
                for mode in range(OWN):
                    block = made[mode * MODES : (mode + 1) * MODES]
                    sum_x = sum_x + block * vel[OWN + mode : OWN + mode + 1]
                    sum_y = sum_y + block * vel[2 * OWN + mode : 2 * OWN + mode + 1]
            for group in range(GROUPS):
                own = slice(group * OWN, (group + 1) * OWN)
                both = jnp.concatenate([sum_x[own], sum_y[own], jnp.zeros((2, chunk), F32)], axis=0)
                if step == 0:
                    keep_ref[group * 16 : (group + 1) * 16] = both
                else:
                    first = keep_ref[group * 16 : (group + 1) * 16]
                    rows = pl.ds(pl.multiple_of((part * GROUPS + group) * 16, 16), 16)
                    flux_ref[0, rows] = (first + both).astype(BF)
                    flux_ref[1, rows] = (first - both).astype(BF)
        return carry

    lax.fori_loop(0, PARTS, line, 0)
    for parity in range(2):
        half_ref[parity] = jnp.dot(flux_ref[parity], back_ref[parity], preferred_element_type=F32)
    picked = []
    for eight in range(LIVE // 8):
        quads = ([], [])
        for part in range(PARTS):
            rows, lanes = slice(part * 128, (part + 1) * 128), slice(eight * 128, (eight + 1) * 128)
            for rolled, block in zip(
                quads, even_odd(half_ref[0, rows, lanes].astype(BF), half_ref[1, rows, lanes].astype(BF))
            ):
                rolled.append(pltpu.roll(block, 32 * part, 1) if part else block)
        for rolled in quads:
            for j in range(4):
                picked.append(pick(masks, [rolled[(slot - j) % 4] for slot in range(4)]))
    dead = jnp.zeros(((SLABS - LIVE) * HOME, 128), BF)
    for group in range(GROUPS):
        own = slice(group * 16, group * 16 + HOME)
        out_ref[group * SLABS * HOME : (group + 1) * SLABS * HOME] = jnp.concatenate(
            [block[own] for block in picked] + [dead], axis=0
        )


def update_kernel(
    in_ref, table_ref, re_ref, im_ref, base_re_ref, base_im_ref, new_re, new_im, wide_ref, left_ref, prod_ref, new_re_ref, new_im_ref, sems
):
    wide_ref[: DEVS * HOME] = in_ref[...].astype(F32)
    slab = lax.axis_index("grid")
    slots = slots_of(slab)
    for at in range(2 * OWN):
        block = wide_ref[pl.ds(at, DEVS, stride=HOME), :].astype(BF).T
        for slot in range(PARTS):
            for c in range(2):
                row = (slot * 2 + c) * ROWS
                left_ref[slots[slot], at * ROWS : (at + 1) * ROWS, c * QUART : (c + 1) * QUART] = block[row : row + ROWS]
    for part in range(PARTS):
        prod_ref[part] = jnp.dot(left_ref[part], table_ref[part], preferred_element_type=F32)
    along_y, along_x = waves_of(slab * ROWS)
    wave_sq = along_y * along_y + along_x * along_x
    keep = (jnp.abs(along_x) * 3.0 < NG) & (along_y * 3.0 < NG)
    damping = VISCOSITY / (NG * NG) * wave_sq
    stores = []
    for mode in range(OWN):
        spectra = []
        for member in range(2):
            rows = slice((member * OWN + mode) * ROWS, (member * OWN + mode + 1) * ROWS)
            spectra.append(
                turn([(prod_ref[part, rows, :QUART], prod_ref[part, rows, QUART:]) for part in range(PARTS)], -1)
            )
        for p in range(4):
            lanes = slice(p * QUART, (p + 1) * QUART)
            (x_re, x_im), (y_re, y_im) = spectra[0][p], spectra[1][p]
            wx, wy = along_x[:, lanes], along_y[:, lanes]
            adv_re = jnp.where(keep[:, lanes], -(wx * x_im + wy * y_im), 0.0)
            adv_im = jnp.where(keep[:, lanes], wx * x_re + wy * y_re, 0.0)
            damp = damping[:, lanes]
            new_re_ref[mode, :, lanes] = base_re_ref[mode, :, lanes] + STEP_WEIGHT * (
                -adv_re - damp * re_ref[mode, :, lanes]
            )
            new_im_ref[mode, :, lanes] = base_im_ref[mode, :, lanes] + STEP_WEIGHT * (
                -adv_im - damp * im_ref[mode, :, lanes]
            )
        stores.append(pltpu.make_async_copy(new_re_ref.at[mode], new_re.at[mode], sems.at[2 * mode]))
        stores.append(pltpu.make_async_copy(new_im_ref.at[mode], new_im.at[mode], sems.at[2 * mode + 1]))
        stores[-2].start()
        stores[-1].start()
    for copy in stores:
        copy.wait()


def call(kernel, outs, scratch, specs, flops, limit=SMALL, space=pltpu.VMEM):
    return pl.pallas_call(
        kernel,
        out_shape=outs,
        in_specs=specs,
        out_specs=jax.tree.map(lambda _: pl.BlockSpec(memory_space=space), outs),
        scratch_shapes=scratch,
        cost_estimate=pl.CostEstimate(flops=flops, bytes_accessed=4 * 1024 * 1024, transcendentals=0),
        compiler_params=pltpu.CompilerParams(vmem_limit_bytes=limit),
    )


def exchange(array, count):
    blocks = array.reshape(DEVS, count // 2, 2, 128)
    blocks = lax.all_to_all(blocks, ("mode", "grid"), split_axis=0, concat_axis=0, tiled=True)
    return blocks.reshape(DEVS * count, 128)


def shards(omega_re, omega_im, base_re, base_im, triple):
    vmem = pl.BlockSpec(memory_space=pltpu.VMEM)
    hbm = pl.BlockSpec(memory_space=pltpu.HBM)
    count = 3 * OWN
    ahead_x, back_x = x_tables()
    ahead_y, back_y = y_tables()
    columns = call(
        columns_kernel,
        jax.ShapeDtypeStruct((DEVS * OUT, 128), BF),
        [
            pltpu.VMEM((OWN, ROWS, NG), F32),
            pltpu.VMEM((OWN, ROWS, NG), F32),
            pltpu.VMEM((PARTS, 2 * QUART, 2 * QUART), BF),
            pltpu.VMEM((PARTS, count * ROWS, 2 * QUART), BF),
            pltpu.VMEM((2, PARTS, count * ROWS, QUART), F32),
            pltpu.VMEM((DEVS // 2 * OUT + 32, 128), F32),
            pltpu.VMEM((2, DEVS // 2 * OUT, 128), BF),
            pltpu.SemaphoreType.DMA((2 * OWN + PARTS + 2,)),
        ],
        [hbm, hbm, hbm],
        1_000_000_000,
        LARGE,
        pltpu.HBM,
    )(omega_re, omega_im, ahead_x)
    slab = exchange(columns, OUT)
    halves = call(
        points_kernel,
        jax.ShapeDtypeStruct((DEVS * HOME, 128), BF),
        [
            pltpu.VMEM((2, PARTS * 24 * GROUPS, KEPT), BF),
            pltpu.VMEM((PARTS * 24 * GROUPS, NG), F32),
            pltpu.VMEM((16 * GROUPS, HALF), F32),
            pltpu.VMEM((2, PARTS * 16 * GROUPS, HALF), BF),
            pltpu.VMEM((2, PARTS * 16 * GROUPS, LIVE * ROWS), F32),
        ],
        [vmem] * 4,
        10_000_000_000,
    )(slab, ahead_y, triple.reshape(MODES * MODES, MODES), back_y)
    rows = exchange(halves, HOME)
    new = jax.ShapeDtypeStruct(base_re.shape, F32)
    return call(
        update_kernel,
        (new, new),
        [
            pltpu.VMEM((DEVS * HOME + 16, 128), F32),
            pltpu.VMEM((PARTS, 2 * OWN * ROWS, 2 * QUART), BF),
            pltpu.VMEM((PARTS, 2 * OWN * ROWS, 2 * QUART), F32),
            pltpu.VMEM(base_re.shape, F32),
            pltpu.VMEM(base_re.shape, F32),
            pltpu.SemaphoreType.DMA((2 * OWN,)),
        ],
        [vmem] * 6,
        1_000_000_000,
        SMALL,
        pltpu.HBM,
    )(rows, back_x, omega_re, omega_im, base_re, base_im)


def solution(mesh):
    spec = P("mode", "grid", None)
    return jax.shard_map(
        shards, mesh=mesh, in_specs=(spec, spec, spec, spec, P()), out_specs=(spec, spec), check_vma=False
    )
```

```python
import functools
import math

import jax
import jax.numpy as jnp
import ml_dtypes
import numpy as np
from jax import lax
from jax.experimental import pallas as pl
from jax.experimental.pallas import tpu as pltpu
from jax.sharding import PartitionSpec as P

VISCOSITY = 4.0
STEP_WEIGHT = 0.5
NG = 1024
KEPT = 512
MODES = 56
GROUPS = 8
SLABS = 32
DEVS = GROUPS * SLABS
OWN = MODES // GROUPS
ROWS = KEPT // SLABS
HALF = NG // 2
PARTS = NG // DEVS
QUART = NG // 4
FACTOR = 1.0 / math.sqrt(NG)
OUT = 22
HOME = 2 * OWN
LIVE = 24
BF = jnp.bfloat16
F32 = jnp.float32
SMALL = 20 * 1024 * 1024
LARGE = 56 * 1024 * 1024


def circle(phases):
    angles = (phases % NG).astype(np.float32) * np.float32(2.0 * math.pi / NG)
    return np.cos(angles), np.sin(angles)


def scaled(table):
    return (table.astype(ml_dtypes.bfloat16).astype(np.float32) * np.float32(FACTOR)).astype(ml_dtypes.bfloat16)


def x_tables():
    ahead, back = [], []
    short = np.arange(QUART)
    for part in range(PARTS):
        points = PARTS * short + part
        cos, sin = circle(short[:, None] * points[None, :])
        ahead.append(np.block([[cos, sin]]))
        cos, sin = circle(points[:, None] * short[None, :])
        back.append(np.block([[cos, -sin], [sin, cos]]))
    return scaled(np.stack(ahead)), scaled(np.stack(back))


def y_tables():
    waves = np.arange(KEPT)
    cos, sin = circle(waves[:, None] * np.arange(HALF)[None, :])
    weights = np.where(waves == 0, 1.0, 2.0).astype(np.float32)[:, None]
    split = (SLABS // 8, 2, 4, ROWS // 2, 2, HALF)
    ahead = np.stack([(weights * cos).reshape(split), (-weights * sin).reshape(split)], axis=6)
    ahead = ahead.transpose(4, 0, 2, 6, 3, 1, 5).reshape(2, KEPT, HALF)
    back = np.stack([cos.reshape(split), -sin.reshape(split)], axis=6)[: LIVE // 8]
    back = back.transpose(4, 5, 0, 2, 6, 3, 1).reshape(2, HALF, LIVE * ROWS)
    return scaled(ahead), scaled(back)


def even_odd(first, second):
    lane = lax.broadcasted_iota(jnp.int32, first.shape, 1)
    return (
        jnp.where(lane % 2 == 0, first, pltpu.roll(second, 1, 1)),
        jnp.where(lane % 2 == 0, pltpu.roll(first, 127, 1), second),
    )


def lane_masks():
    group = lax.broadcasted_iota(jnp.int32, (1, 128), 1) // 32
    return [group == 0, group == 1, group == 2]


def pick(masks, sources):
    return jnp.where(
        masks[0], sources[0], jnp.where(masks[1], sources[1], jnp.where(masks[2], sources[2], sources[3]))
    )


def turn(parts, sign):
    (r0, i0), (r1, i1), (r2, i2), (r3, i3) = parts
    er, ei, fr, fi = r0 + r2, i0 + i2, r0 - r2, i0 - i2
    gr, gi, hr, hi = r1 + r3, i1 + i3, r1 - r3, i1 - i3
    if sign < 0:
        hr, hi = -hr, -hi
    return (
        (er + gr, ei + gi),
        (fr - hi, fi + hr),
        (er - gr, ei - gi),
        (fr + hi, fi - hr),
    )


def waves_of(first_row):
    along_y = (first_row + lax.broadcasted_iota(jnp.int32, (ROWS, NG), 0)).astype(F32)
    index = lax.broadcasted_iota(jnp.int32, (ROWS, NG), 1)
    along_x = jnp.where(index < NG // 2, index, index - NG).astype(F32)
    return along_y, along_x


def slots_of(shift):
    return [lax.rem(slot + PARTS - lax.rem(shift, PARTS), PARTS) for slot in range(PARTS)]


def columns_kernel(
    re_hbm, im_hbm, table_hbm, out_hbm, re_ref, im_ref, table_ref, left_ref, prod_ref, turn_ref, send_ref, sems
):
    loads = []
    for mode in range(OWN):
        loads.append(
            (
                pltpu.make_async_copy(re_hbm.at[mode], re_ref.at[mode], sems.at[2 * mode]),
                pltpu.make_async_copy(im_hbm.at[mode], im_ref.at[mode], sems.at[2 * mode + 1]),
            )
        )
    tables = [
        pltpu.make_async_copy(table_hbm.at[part], table_ref.at[part, pl.ds(0, QUART)], sems.at[2 * OWN + part])
        for part in range(PARTS)
    ]
    for pair in loads:
        pair[0].start()
        pair[1].start()
    for copy in tables:
        copy.start()
    count = 3 * OWN
    half = DEVS // 2
    for at in range(count, OUT):
        turn_ref[pl.ds(at, half, stride=OUT), :] = jnp.zeros((half, 128), F32)
    slab = lax.axis_index("grid")
    along_y, along_x = waves_of(slab * ROWS)
    wave_sq = along_y * along_y + along_x * along_x
    inverse = jnp.where(wave_sq > 0.5, 1.0 / jnp.maximum(wave_sq, 1.0), 0.0)
    scale_y = along_y * inverse
    scale_x = along_x * inverse
    for mode in range(OWN):
        loads[mode][0].wait()
        loads[mode][1].wait()
        w_re, w_im = re_ref[mode], im_ref[mode]
        fields = (
            (w_re, w_im),
            (-scale_y * w_im, scale_y * w_re),
            (scale_x * w_im, -scale_x * w_re),
        )
        for member, (f_re, f_im) in enumerate(fields):
            pieces = [
                (f_re[:, QUART * p : QUART * (p + 1)], f_im[:, QUART * p : QUART * (p + 1)])
                for p in range(4)
            ]
            at = (member * OWN + mode) * ROWS
            for part, (b_re, b_im) in enumerate(turn(pieces, 1)):
                left_ref[part, at : at + ROWS, :QUART] = b_re.astype(BF)
                left_ref[part, at : at + ROWS, QUART:] = b_im.astype(BF)
    for part in range(PARTS):
        tables[part].wait()
        table_ref[part, QUART:, :QUART] = -table_ref[part, :QUART, QUART:]
        table_ref[part, QUART:, QUART:] = table_ref[part, :QUART, :QUART]
    slots = slots_of(slab)
    sends = []
    for side in range(2):
        for part in range(PARTS):
            own = jnp.concatenate(
                [table_ref[part, :, c * QUART + side * half : c * QUART + (side + 1) * half] for c in range(2)], axis=1
            )
            prod_ref[side, part] = jnp.dot(left_ref[part], own, preferred_element_type=F32)
        for at in range(count):
            rows = slice(at * ROWS, (at + 1) * ROWS)
            block = jnp.concatenate(
                [
                    prod_ref[side, slots[slot], rows, c * half : (c + 1) * half]
                    for slot in range(PARTS)
                    for c in range(2)
                ],
                axis=0,
            )
            turn_ref[pl.ds(at, half, stride=OUT), :] = block.astype(BF).T.astype(F32)
        send_ref[side] = turn_ref[: half * OUT].astype(BF)
        sends.append(
            pltpu.make_async_copy(
                send_ref.at[side], out_hbm.at[pl.ds(side * half * OUT, half * OUT)], sems.at[2 * OWN + PARTS + side]
            )
        )
        sends[side].start()
    for copy in sends:
        copy.wait()


def points_kernel(
    in_ref, ahead_ref, triple_ref, back_ref, out_ref, left_ref, phys_ref, keep_ref, flux_ref, half_ref
):
    chunk = HALF
    tall = 24 * GROUPS
    masks = lane_masks()
    span = SLABS * OUT

    def gather(pair, carry):
        held = [in_ref[pl.ds(pl.multiple_of((pair * 2 + side) * span, span), span)] for side in range(2)]
        nothing = jnp.zeros((24 - OUT, 128), BF)
        for eight in range(SLABS // 8):
            quads = []
            for quad in (2 * eight, 2 * eight + 1):
                blocks = []
                for j in range(4):
                    at = (quad * 4 + j) * OUT
                    blocks.append(jnp.concatenate([held[0][at : at + OUT], nothing, held[1][at : at + OUT], nothing], axis=0))
                quads.append(blocks)
            for part in range(PARTS):
                mixed = []
                for blocks in quads:
                    one = pick(masks, [blocks[(slot - part) % 4] for slot in range(4)])
                    mixed.append(pltpu.roll(one, 128 - 32 * part, 1) if part else one)
                rows = pl.ds(pl.multiple_of(part * tall + pair * 48, 48), 48)
                for parity, both in enumerate(even_odd(*mixed)):
                    left_ref[parity, rows, eight * 128 : (eight + 1) * 128] = both.astype(BF)
        return carry

    lax.fori_loop(0, GROUPS // 2, gather, 0, unroll=True)
    even = jnp.dot(left_ref[0], ahead_ref[0], preferred_element_type=F32)
    odd = jnp.dot(left_ref[1], ahead_ref[1], preferred_element_type=F32)
    phys_ref[:, :HALF] = even + odd
    phys_ref[:, HALF:] = even - odd

    def line(part, carry):
        base = pl.multiple_of(part * tall, tall)
        for step in range(NG // chunk):
            lanes = slice(step * chunk, (step + 1) * chunk)
            right = jnp.concatenate(
                [phys_ref[pl.ds(base + group * 24, 24), lanes][:OWN] for group in range(GROUPS)], axis=0
            ).astype(BF)
            sum_x = jnp.zeros((MODES, chunk), F32)
            sum_y = jnp.zeros((MODES, chunk), F32)
            for group in range(GROUPS):
                made = jnp.dot(
                    triple_ref[group * OWN * MODES : (group + 1) * OWN * MODES, :],
                    right,
                    preferred_element_type=F32,
                )
                vel = phys_ref[pl.ds(base + group * 24, 24), lanes]
                for mode in range(OWN):
                    block = made[mode * MODES : (mode + 1) * MODES]
                    sum_x = sum_x + block * vel[OWN + mode : OWN + mode + 1]
                    sum_y = sum_y + block * vel[2 * OWN + mode : 2 * OWN + mode + 1]
            for group in range(GROUPS):
                own = slice(group * OWN, (group + 1) * OWN)
                both = jnp.concatenate([sum_x[own], sum_y[own], jnp.zeros((2, chunk), F32)], axis=0)
                if step == 0:
                    keep_ref[group * 16 : (group + 1) * 16] = both
                else:
                    first = keep_ref[group * 16 : (group + 1) * 16]
                    rows = pl.ds(pl.multiple_of((part * GROUPS + group) * 16, 16), 16)
                    flux_ref[0, rows] = (first + both).astype(BF)
                    flux_ref[1, rows] = (first - both).astype(BF)
        return carry

    lax.fori_loop(0, PARTS, line, 0)
    for parity in range(2):
        half_ref[parity] = jnp.dot(flux_ref[parity], back_ref[parity], preferred_element_type=F32)
    picked = []
    for eight in range(LIVE // 8):
        quads = ([], [])
        for part in range(PARTS):
            rows, lanes = slice(part * 128, (part + 1) * 128), slice(eight * 128, (eight + 1) * 128)
            for rolled, block in zip(
                quads, even_odd(half_ref[0, rows, lanes].astype(BF), half_ref[1, rows, lanes].astype(BF))
            ):
                rolled.append(pltpu.roll(block, 32 * part, 1) if part else block)
        for rolled in quads:
            for j in range(4):
                picked.append(pick(masks, [rolled[(slot - j) % 4] for slot in range(4)]))
    dead = jnp.zeros(((SLABS - LIVE) * HOME, 128), BF)
    for group in range(GROUPS):
        own = slice(group * 16, group * 16 + HOME)
        out_ref[group * SLABS * HOME : (group + 1) * SLABS * HOME] = jnp.concatenate(
            [block[own] for block in picked] + [dead], axis=0
        )


def update_kernel(
    in_ref, table_ref, re_ref, im_ref, base_re_ref, base_im_ref, new_re, new_im, wide_ref, left_ref, prod_ref, new_re_ref, new_im_ref, sems
):
    wide_ref[: DEVS * HOME] = in_ref[...].astype(F32)
    slab = lax.axis_index("grid")
    slots = slots_of(slab)
    for at in range(2 * OWN):
        block = wide_ref[pl.ds(at, DEVS, stride=HOME), :].astype(BF).T
        for slot in range(PARTS):
            for c in range(2):
                row = (slot * 2 + c) * ROWS
                left_ref[slots[slot], at * ROWS : (at + 1) * ROWS, c * QUART : (c + 1) * QUART] = block[row : row + ROWS]
    for part in range(PARTS):
        prod_ref[part] = jnp.dot(left_ref[part], table_ref[part], preferred_element_type=F32)
    along_y, along_x = waves_of(slab * ROWS)
    wave_sq = along_y * along_y + along_x * along_x
    keep = (jnp.abs(along_x) * 3.0 < NG) & (along_y * 3.0 < NG)
    damping = VISCOSITY / (NG * NG) * wave_sq
    stores = []
    for mode in range(OWN):
        spectra = []
        for member in range(2):
            rows = slice((member * OWN + mode) * ROWS, (member * OWN + mode + 1) * ROWS)
            spectra.append(
                turn([(prod_ref[part, rows, :QUART], prod_ref[part, rows, QUART:]) for part in range(PARTS)], -1)
            )
        for p in range(4):
            for side in range(2):
                own = slice(side * HALF // 4, (side + 1) * HALF // 4)
                at = p * QUART + side * HALF // 4
                lanes = slice(at, at + HALF // 4)
                damp = damping[:, lanes]
                rhs_re = -damp * re_ref[mode, :, lanes]
                rhs_im = -damp * im_ref[mode, :, lanes]
                nearest = at if at < HALF else NG - at - HALF // 4 + 1
                if 3 * nearest < NG:
                    (x_re, x_im), (y_re, y_im) = [[half[:, own] for half in spectra[g][p]] for g in range(2)]
                    wx, wy = along_x[:, lanes], along_y[:, lanes]
                    rhs_re = rhs_re - jnp.where(keep[:, lanes], -(wx * x_im + wy * y_im), 0.0)
                    rhs_im = rhs_im - jnp.where(keep[:, lanes], wx * x_re + wy * y_re, 0.0)
                new_re_ref[mode, :, lanes] = base_re_ref[mode, :, lanes] + STEP_WEIGHT * rhs_re
                new_im_ref[mode, :, lanes] = base_im_ref[mode, :, lanes] + STEP_WEIGHT * rhs_im
        stores.append(pltpu.make_async_copy(new_re_ref.at[mode], new_re.at[mode], sems.at[2 * mode]))
        stores.append(pltpu.make_async_copy(new_im_ref.at[mode], new_im.at[mode], sems.at[2 * mode + 1]))
        stores[-2].start()
        stores[-1].start()
    for copy in stores:
        copy.wait()


def call(kernel, outs, scratch, specs, flops, limit=SMALL, space=pltpu.VMEM):
    return pl.pallas_call(
        kernel,
        out_shape=outs,
        in_specs=specs,
        out_specs=jax.tree.map(lambda _: pl.BlockSpec(memory_space=space), outs),
        scratch_shapes=scratch,
        cost_estimate=pl.CostEstimate(flops=flops, bytes_accessed=4 * 1024 * 1024, transcendentals=0),
        compiler_params=pltpu.CompilerParams(vmem_limit_bytes=limit),
    )


def exchange(array, count):
    blocks = array.reshape(DEVS, count // 2, 2, 128)
    blocks = lax.all_to_all(blocks, ("mode", "grid"), split_axis=0, concat_axis=0, tiled=True)
    return blocks.reshape(DEVS * count, 128)


def shards(omega_re, omega_im, base_re, base_im, triple):
    vmem = pl.BlockSpec(memory_space=pltpu.VMEM)
    hbm = pl.BlockSpec(memory_space=pltpu.HBM)
    count = 3 * OWN
    ahead_x, back_x = x_tables()
    ahead_y, back_y = y_tables()
    columns = call(
        columns_kernel,
        jax.ShapeDtypeStruct((DEVS * OUT, 128), BF),
        [
            pltpu.VMEM((OWN, ROWS, NG), F32),
            pltpu.VMEM((OWN, ROWS, NG), F32),
            pltpu.VMEM((PARTS, 2 * QUART, 2 * QUART), BF),
            pltpu.VMEM((PARTS, count * ROWS, 2 * QUART), BF),
            pltpu.VMEM((2, PARTS, count * ROWS, QUART), F32),
            pltpu.VMEM((DEVS // 2 * OUT + 32, 128), F32),
            pltpu.VMEM((2, DEVS // 2 * OUT, 128), BF),
            pltpu.SemaphoreType.DMA((2 * OWN + PARTS + 2,)),
        ],
        [hbm, hbm, hbm],
        1_000_000_000,
        LARGE,
        pltpu.HBM,
    )(omega_re, omega_im, ahead_x)
    slab = exchange(columns, OUT)
    halves = call(
        points_kernel,
        jax.ShapeDtypeStruct((DEVS * HOME, 128), BF),
        [
            pltpu.VMEM((2, PARTS * 24 * GROUPS, KEPT), BF),
            pltpu.VMEM((PARTS * 24 * GROUPS, NG), F32),
            pltpu.VMEM((16 * GROUPS, HALF), F32),
            pltpu.VMEM((2, PARTS * 16 * GROUPS, HALF), BF),
            pltpu.VMEM((2, PARTS * 16 * GROUPS, LIVE * ROWS), F32),
        ],
        [vmem] * 4,
        10_000_000_000,
    )(slab, ahead_y, triple.reshape(MODES * MODES, MODES), back_y)
    rows = exchange(halves, HOME)
    new = jax.ShapeDtypeStruct(base_re.shape, F32)
    return call(
        update_kernel,
        (new, new),
        [
            pltpu.VMEM((DEVS * HOME + 16, 128), F32),
            pltpu.VMEM((PARTS, 2 * OWN * ROWS, 2 * QUART), BF),
            pltpu.VMEM((PARTS, 2 * OWN * ROWS, 2 * QUART), F32),
            pltpu.VMEM(base_re.shape, F32),
            pltpu.VMEM(base_re.shape, F32),
            pltpu.SemaphoreType.DMA((2 * OWN,)),
        ],
        [vmem] * 6,
        1_000_000_000,
        SMALL,
        pltpu.HBM,
    )(rows, back_x, omega_re, omega_im, base_re, base_im)


def solution(mesh):
    spec = P("mode", "grid", None)
    return jax.shard_map(
        shards, mesh=mesh, in_specs=(spec, spec, spec, spec, P()), out_specs=(spec, spec), check_vma=False
    )
```

```python
import functools
import math

import jax
import jax.numpy as jnp
import ml_dtypes
import numpy as np
from jax import lax
from jax.experimental import pallas as pl
from jax.experimental.pallas import tpu as pltpu
from jax.sharding import PartitionSpec as P

VISCOSITY = 4.0
STEP_WEIGHT = 0.5
NG = 1024
KEPT = 512
MODES = 56
GROUPS = 8
SLABS = 32
DEVS = GROUPS * SLABS
OWN = MODES // GROUPS
ROWS = KEPT // SLABS
HALF = NG // 2
PARTS = NG // DEVS
QUART = NG // 4
FACTOR = 1.0 / math.sqrt(NG)
OUT = 22
HOME = 2 * OWN
LIVE = 24
BF = jnp.bfloat16
F32 = jnp.float32
SMALL = 20 * 1024 * 1024
LARGE = 56 * 1024 * 1024


def circle(phases):
    angles = (phases % NG).astype(np.float32) * np.float32(2.0 * math.pi / NG)
    return np.cos(angles), np.sin(angles)


def scaled(table):
    return (table.astype(ml_dtypes.bfloat16).astype(np.float32) * np.float32(FACTOR)).astype(ml_dtypes.bfloat16)


def x_tables():
    ahead, back = [], []
    short = np.arange(QUART)
    for part in range(PARTS):
        points = PARTS * short + part
        cos, sin = circle(short[:, None] * points[None, :])
        ahead.append(np.block([[cos, sin]]))
        cos, sin = circle(points[:, None] * short[None, :])
        back.append(np.block([[cos, -sin], [sin, cos]]))
    return scaled(np.stack(ahead)), scaled(np.stack(back))


def y_tables():
    waves = np.arange(KEPT)
    cos, sin = circle(waves[:, None] * np.arange(HALF)[None, :])
    weights = np.where(waves == 0, 1.0, 2.0).astype(np.float32)[:, None]
    split = (SLABS // 8, 2, 4, ROWS // 2, 2, HALF)
    ahead = np.stack([(weights * cos).reshape(split), (-weights * sin).reshape(split)], axis=6)
    ahead = ahead.transpose(4, 0, 2, 6, 3, 1, 5).reshape(2, KEPT, HALF)
    back = np.stack([cos.reshape(split), -sin.reshape(split)], axis=6)[: LIVE // 8]
    back = back.transpose(4, 5, 0, 2, 6, 3, 1).reshape(2, HALF, LIVE * ROWS)
    return scaled(ahead), scaled(back)


def even_odd(first, second):
    lane = lax.broadcasted_iota(jnp.int32, first.shape, 1)
    return (
        jnp.where(lane % 2 == 0, first, pltpu.roll(second, 1, 1)),
        jnp.where(lane % 2 == 0, pltpu.roll(first, 127, 1), second),
    )


def lane_masks():
    group = lax.broadcasted_iota(jnp.int32, (1, 128), 1) // 32
    return [group == 0, group == 1, group == 2]


def pick(masks, sources):
    return jnp.where(
        masks[0], sources[0], jnp.where(masks[1], sources[1], jnp.where(masks[2], sources[2], sources[3]))
    )


def turn(parts, sign):
    (r0, i0), (r1, i1), (r2, i2), (r3, i3) = parts
    er, ei, fr, fi = r0 + r2, i0 + i2, r0 - r2, i0 - i2
    gr, gi, hr, hi = r1 + r3, i1 + i3, r1 - r3, i1 - i3
    if sign < 0:
        hr, hi = -hr, -hi
    return (
        (er + gr, ei + gi),
        (fr - hi, fi + hr),
        (er - gr, ei - gi),
        (fr + hi, fi - hr),
    )


def waves_of(first_row):
    along_y = (first_row + lax.broadcasted_iota(jnp.int32, (ROWS, NG), 0)).astype(F32)
    index = lax.broadcasted_iota(jnp.int32, (ROWS, NG), 1)
    along_x = jnp.where(index < NG // 2, index, index - NG).astype(F32)
    return along_y, along_x


def slots_of(shift):
    return [lax.rem(slot + PARTS - lax.rem(shift, PARTS), PARTS) for slot in range(PARTS)]


def columns_kernel(
    re_hbm, im_hbm, table_hbm, out_hbm, re_ref, im_ref, table_ref, left_ref, prod_ref, turn_ref, send_ref, sems
):
    loads = []
    for mode in range(OWN):
        loads.append(
            (
                pltpu.make_async_copy(re_hbm.at[mode], re_ref.at[mode], sems.at[2 * mode]),
                pltpu.make_async_copy(im_hbm.at[mode], im_ref.at[mode], sems.at[2 * mode + 1]),
            )
        )
    tables = [
        pltpu.make_async_copy(table_hbm.at[part], table_ref.at[part, pl.ds(0, QUART)], sems.at[2 * OWN + part])
        for part in range(PARTS)
    ]
    for pair in loads:
        pair[0].start()
        pair[1].start()
    for copy in tables:
        copy.start()
    count = 3 * OWN
    half = DEVS // 2
    for at in range(count, OUT):
        turn_ref[pl.ds(at, half, stride=OUT), :] = jnp.zeros((half, 128), F32)
    slab = lax.axis_index("grid")
    along_y, along_x = waves_of(slab * ROWS)
    wave_sq = along_y * along_y + along_x * along_x
    inverse = jnp.where(wave_sq > 0.5, 1.0 / jnp.maximum(wave_sq, 1.0), 0.0)
    scale_y = along_y * inverse
    scale_x = along_x * inverse
    for mode in range(OWN):
        loads[mode][0].wait()
        loads[mode][1].wait()
        w_re, w_im = re_ref[mode], im_ref[mode]
        fields = (
            (w_re, w_im),
            (-scale_y * w_im, scale_y * w_re),
            (scale_x * w_im, -scale_x * w_re),
        )
        for member, (f_re, f_im) in enumerate(fields):
            pieces = [
                (f_re[:, QUART * p : QUART * (p + 1)], f_im[:, QUART * p : QUART * (p + 1)])
                for p in range(4)
            ]
            at = (member * OWN + mode) * ROWS
            for part, (b_re, b_im) in enumerate(turn(pieces, 1)):
                left_ref[part, at : at + ROWS, :QUART] = b_re.astype(BF)
                left_ref[part, at : at + ROWS, QUART:] = b_im.astype(BF)
    for part in range(PARTS):
        tables[part].wait()
        table_ref[part, QUART:, :QUART] = -table_ref[part, :QUART, QUART:]
        table_ref[part, QUART:, QUART:] = table_ref[part, :QUART, :QUART]
    slots = slots_of(slab)
    sends = []
    for side in range(2):
        for part in range(PARTS):
            own = jnp.concatenate(
                [table_ref[part, :, c * QUART + side * half : c * QUART + (side + 1) * half] for c in range(2)], axis=1
            )
            prod_ref[side, part] = jnp.dot(left_ref[part], own, preferred_element_type=F32).astype(BF)
        for at in range(count):
            rows = slice(at * ROWS, (at + 1) * ROWS)
            block = jnp.concatenate(
                [
                    prod_ref[side, slots[slot], rows, c * half : (c + 1) * half]
                    for slot in range(PARTS)
                    for c in range(2)
                ],
                axis=0,
            )
            turn_ref[pl.ds(at, half, stride=OUT), :] = block.T.astype(F32)
        send_ref[side] = turn_ref[: half * OUT].astype(BF)
        sends.append(
            pltpu.make_async_copy(
                send_ref.at[side], out_hbm.at[pl.ds(side * half * OUT, half * OUT)], sems.at[2 * OWN + PARTS + side]
            )
        )
        sends[side].start()
    for copy in sends:
        copy.wait()


def points_kernel(
    in_ref, ahead_ref, triple_ref, back_ref, out_ref, left_ref, phys_ref, keep_ref, flux_ref, half_ref
):
    chunk = HALF
    tall = 24 * GROUPS
    masks = lane_masks()
    span = SLABS * OUT

    def gather(pair, carry):
        held = [in_ref[pl.ds(pl.multiple_of((pair * 2 + side) * span, span), span)] for side in range(2)]
        nothing = jnp.zeros((24 - OUT, 128), BF)
        for eight in range(SLABS // 8):
            quads = []
            for quad in (2 * eight, 2 * eight + 1):
                blocks = []
                for j in range(4):
                    at = (quad * 4 + j) * OUT
                    blocks.append(jnp.concatenate([held[0][at : at + OUT], nothing, held[1][at : at + OUT], nothing], axis=0))
                quads.append(blocks)
            for part in range(PARTS):
                mixed = []
                for blocks in quads:
                    one = pick(masks, [blocks[(slot - part) % 4] for slot in range(4)])
                    mixed.append(pltpu.roll(one, 128 - 32 * part, 1) if part else one)
                rows = pl.ds(pl.multiple_of(part * tall + pair * 48, 48), 48)
                for parity, both in enumerate(even_odd(*mixed)):
                    left_ref[parity, rows, eight * 128 : (eight + 1) * 128] = both.astype(BF)
        return carry

    lax.fori_loop(0, GROUPS // 2, gather, 0, unroll=True)
    even = jnp.dot(left_ref[0], ahead_ref[0], preferred_element_type=F32)
    odd = jnp.dot(left_ref[1], ahead_ref[1], preferred_element_type=F32)
    phys_ref[:, :HALF] = even + odd
    phys_ref[:, HALF:] = even - odd

    def line(part, carry):
        base = pl.multiple_of(part * tall, tall)
        for step in range(NG // chunk):
            lanes = slice(step * chunk, (step + 1) * chunk)
            right = jnp.concatenate(
                [phys_ref[pl.ds(base + group * 24, 24), lanes][:OWN] for group in range(GROUPS)], axis=0
            ).astype(BF)
            sum_x = jnp.zeros((MODES, chunk), F32)
            sum_y = jnp.zeros((MODES, chunk), F32)
            for group in range(GROUPS):
                made = jnp.dot(
                    triple_ref[group * OWN * MODES : (group + 1) * OWN * MODES, :],
                    right,
                    preferred_element_type=F32,
                )
                vel = phys_ref[pl.ds(base + group * 24, 24), lanes]
                for mode in range(OWN):
                    block = made[mode * MODES : (mode + 1) * MODES]
                    sum_x = sum_x + block * vel[OWN + mode : OWN + mode + 1]
                    sum_y = sum_y + block * vel[2 * OWN + mode : 2 * OWN + mode + 1]
            for group in range(GROUPS):
                own = slice(group * OWN, (group + 1) * OWN)
                both = jnp.concatenate([sum_x[own], sum_y[own], jnp.zeros((2, chunk), F32)], axis=0)
                if step == 0:
                    keep_ref[group * 16 : (group + 1) * 16] = both
                else:
                    first = keep_ref[group * 16 : (group + 1) * 16]
                    rows = pl.ds(pl.multiple_of((part * GROUPS + group) * 16, 16), 16)
                    flux_ref[0, rows] = (first + both).astype(BF)
                    flux_ref[1, rows] = (first - both).astype(BF)
        return carry

    lax.fori_loop(0, PARTS, line, 0)
    for parity in range(2):
        half_ref[parity] = jnp.dot(flux_ref[parity], back_ref[parity], preferred_element_type=F32)
    picked = []
    for eight in range(LIVE // 8):
        quads = ([], [])
        for part in range(PARTS):
            rows, lanes = slice(part * 128, (part + 1) * 128), slice(eight * 128, (eight + 1) * 128)
            for rolled, block in zip(
                quads, even_odd(half_ref[0, rows, lanes].astype(BF), half_ref[1, rows, lanes].astype(BF))
            ):
                rolled.append(pltpu.roll(block, 32 * part, 1) if part else block)
        for rolled in quads:
            for j in range(4):
                picked.append(pick(masks, [rolled[(slot - j) % 4] for slot in range(4)]))
    dead = jnp.zeros(((SLABS - LIVE) * HOME, 128), BF)
    for group in range(GROUPS):
        own = slice(group * 16, group * 16 + HOME)
        out_ref[group * SLABS * HOME : (group + 1) * SLABS * HOME] = jnp.concatenate(
            [block[own] for block in picked] + [dead], axis=0
        )


def update_kernel(
    in_ref, table_ref, re_ref, im_ref, base_re_ref, base_im_ref, new_re, new_im, wide_ref, left_ref, prod_ref, new_re_ref, new_im_ref, sems
):
    wide_ref[: DEVS * HOME] = in_ref[...].astype(F32)
    slab = lax.axis_index("grid")
    slots = slots_of(slab)
    for at in range(2 * OWN):
        block = wide_ref[pl.ds(at, DEVS, stride=HOME), :].astype(BF).T
        for slot in range(PARTS):
            for c in range(2):
                row = (slot * 2 + c) * ROWS
                left_ref[slots[slot], at * ROWS : (at + 1) * ROWS, c * QUART : (c + 1) * QUART] = block[row : row + ROWS]
    for part in range(PARTS):
        prod_ref[part] = jnp.dot(left_ref[part], table_ref[part], preferred_element_type=F32)
    along_y, along_x = waves_of(slab * ROWS)
    wave_sq = along_y * along_y + along_x * along_x
    keep = (jnp.abs(along_x) * 3.0 < NG) & (along_y * 3.0 < NG)
    damping = VISCOSITY / (NG * NG) * wave_sq
    stores = []
    for mode in range(OWN):
        spectra = []
        for member in range(2):
            rows = slice((member * OWN + mode) * ROWS, (member * OWN + mode + 1) * ROWS)
            spectra.append(
                turn([(prod_ref[part, rows, :QUART], prod_ref[part, rows, QUART:]) for part in range(PARTS)], -1)
            )
        for p in range(4):
            lanes = slice(p * QUART, (p + 1) * QUART)
            (x_re, x_im), (y_re, y_im) = spectra[0][p], spectra[1][p]
            wx, wy = along_x[:, lanes], along_y[:, lanes]
            adv_re = jnp.where(keep[:, lanes], -(wx * x_im + wy * y_im), 0.0)
            adv_im = jnp.where(keep[:, lanes], wx * x_re + wy * y_re, 0.0)
            damp = damping[:, lanes]
            new_re_ref[mode, :, lanes] = base_re_ref[mode, :, lanes] + STEP_WEIGHT * (
                -adv_re - damp * re_ref[mode, :, lanes]
            )
            new_im_ref[mode, :, lanes] = base_im_ref[mode, :, lanes] + STEP_WEIGHT * (
                -adv_im - damp * im_ref[mode, :, lanes]
            )
        stores.append(pltpu.make_async_copy(new_re_ref.at[mode], new_re.at[mode], sems.at[2 * mode]))
        stores.append(pltpu.make_async_copy(new_im_ref.at[mode], new_im.at[mode], sems.at[2 * mode + 1]))
        stores[-2].start()
        stores[-1].start()
    for copy in stores:
        copy.wait()


def call(kernel, outs, scratch, specs, flops, limit=SMALL, space=pltpu.VMEM):
    return pl.pallas_call(
        kernel,
        out_shape=outs,
        in_specs=specs,
        out_specs=jax.tree.map(lambda _: pl.BlockSpec(memory_space=space), outs),
        scratch_shapes=scratch,
        cost_estimate=pl.CostEstimate(flops=flops, bytes_accessed=4 * 1024 * 1024, transcendentals=0),
        compiler_params=pltpu.CompilerParams(vmem_limit_bytes=limit),
    )


def exchange(array, count):
    blocks = array.reshape(DEVS, count // 2, 2, 128)
    blocks = lax.all_to_all(blocks, ("mode", "grid"), split_axis=0, concat_axis=0, tiled=True)
    return blocks.reshape(DEVS * count, 128)


def shards(omega_re, omega_im, base_re, base_im, triple):
    vmem = pl.BlockSpec(memory_space=pltpu.VMEM)
    hbm = pl.BlockSpec(memory_space=pltpu.HBM)
    count = 3 * OWN
    ahead_x, back_x = x_tables()
    ahead_y, back_y = y_tables()
    columns = call(
        columns_kernel,
        jax.ShapeDtypeStruct((DEVS * OUT, 128), BF),
        [
            pltpu.VMEM((OWN, ROWS, NG), F32),
            pltpu.VMEM((OWN, ROWS, NG), F32),
            pltpu.VMEM((PARTS, 2 * QUART, 2 * QUART), BF),
            pltpu.VMEM((PARTS, count * ROWS, 2 * QUART), BF),
            pltpu.VMEM((2, PARTS, count * ROWS, QUART), BF),
            pltpu.VMEM((DEVS // 2 * OUT + 32, 128), F32),
            pltpu.VMEM((2, DEVS // 2 * OUT, 128), BF),
            pltpu.SemaphoreType.DMA((2 * OWN + PARTS + 2,)),
        ],
        [hbm, hbm, hbm],
        1_000_000_000,
        LARGE,
        pltpu.HBM,
    )(omega_re, omega_im, ahead_x)
    slab = exchange(columns, OUT)
    halves = call(
        points_kernel,
        jax.ShapeDtypeStruct((DEVS * HOME, 128), BF),
        [
            pltpu.VMEM((2, PARTS * 24 * GROUPS, KEPT), BF),
            pltpu.VMEM((PARTS * 24 * GROUPS, NG), F32),
            pltpu.VMEM((16 * GROUPS, HALF), F32),
            pltpu.VMEM((2, PARTS * 16 * GROUPS, HALF), BF),
            pltpu.VMEM((2, PARTS * 16 * GROUPS, LIVE * ROWS), F32),
        ],
        [vmem] * 4,
        10_000_000_000,
    )(slab, ahead_y, triple.reshape(MODES * MODES, MODES), back_y)
    rows = exchange(halves, HOME)
    new = jax.ShapeDtypeStruct(base_re.shape, F32)
    return call(
        update_kernel,
        (new, new),
        [
            pltpu.VMEM((DEVS * HOME + 16, 128), F32),
            pltpu.VMEM((PARTS, 2 * OWN * ROWS, 2 * QUART), BF),
            pltpu.VMEM((PARTS, 2 * OWN * ROWS, 2 * QUART), F32),
            pltpu.VMEM(base_re.shape, F32),
            pltpu.VMEM(base_re.shape, F32),
            pltpu.SemaphoreType.DMA((2 * OWN,)),
        ],
        [vmem] * 6,
        1_000_000_000,
        SMALL,
        pltpu.HBM,
    )(rows, back_x, omega_re, omega_im, base_re, base_im)


def solution(mesh):
    spec = P("mode", "grid", None)
    return jax.shard_map(
        shards, mesh=mesh, in_specs=(spec, spec, spec, spec, P()), out_specs=(spec, spec), check_vma=False
    )
```
